32 devices in a mesh: dp: 8 (over z, core), tensor: 4 (over y, x).
Axes of the slice: x: 2, y: 2, z: 4, core: 2. Of those that a mesh axis runs over, the one named last changes fastest.
Arguments:
- tokens: bfloat16 [4096, 2048], P('dp'), may hold values from -6 to 6
- cotangent: bfloat16 [4096, 2048], P('dp'), may hold values from -6 to 6
- block_ids: int32 [4096], replicated, may hold values from 0 to 31, as said below
- routes: int32 [4096, 6], P('dp'), may hold values from 0 to 11, all different within a row; in each aligned block of 512 rows (0 to 511, 512 to 1023, ...) at most 384 rows name the same one
- first_gain: float32 [2048], replicated, may hold values from 0.5 to 1.5
- query_weight: bfloat16 [2048, 3072], P(None, 'tensor'), may hold values from -0.125 to 0.125
- latent_down: bfloat16 [2048, 576], replicated, may hold values from -0.125 to 0.125
- latent_gain: float32 [512], replicated, may hold values from 0.5 to 1.5
- latent_up: bfloat16 [512, 4096], P(None, 'tensor'), may hold values from -0.25 to 0.25
- output_weight: bfloat16 [2048, 2048], P('tensor'), may hold values from -2 to 2
- second_gain: float32 [2048], replicated, may hold values from 0.5 to 1.5
- router_weight: bfloat16 [2048, 12], replicated, may hold values from -0.0625 to 0.0625
- gate_weight: bfloat16 [12, 2048, 1408], P(None, None, 'tensor'), may hold values from -0.125 to 0.125
- up_weight: bfloat16 [12, 2048, 1408], P(None, None, 'tensor'), may hold values from -0.125 to 0.125
- down_weight: bfloat16 [12, 1408, 2048], P(None, 'tensor'), may hold values from -0.3125 to 0.3125
- shared_gate: bfloat16 [2048, 2816], P(None, 'tensor'), may hold values from -0.125 to 0.125
- shared_up: bfloat16 [2048, 2816], P(None, 'tensor'), may hold values from -0.125 to 0.125
- shared_down: bfloat16 [2816, 2048], P('tensor'), may hold values from -0.15625 to 0.15625
Outputs:
- result: bfloat16 [4096, 2048], P('dp')
- token_grad: bfloat16 [4096, 2048], P('dp')
- grad_first_gain: float32 [2048], P('dp')
- grad_query: float32 [2048, 3072], P('dp', 'tensor')
- grad_latent_down: float32 [2048, 576], P(('dp', 'tensor'))
- grad_latent_gain: float32 [512], P(('dp', 'tensor'))
- grad_latent_up: float32 [512, 4096], P('dp', 'tensor')
- grad_output: float32 [2048, 2048], P('tensor', 'dp')
- grad_second_gain: float32 [2048], P('dp')
- grad_router: float32 [2048, 12], P(('dp', 'tensor'))
- grad_gate: float32 [12, 2048, 1408], P(None, 'dp', 'tensor')
- grad_up: float32 [12, 2048, 1408], P(None, 'dp', 'tensor')
- grad_down: float32 [12, 1408, 2048], P(None, 'tensor', 'dp')
- grad_shared_gate: float32 [2048, 2816], P('dp', 'tensor')
- grad_shared_up: float32 [2048, 2816], P('dp', 'tensor')
- grad_shared_down: float32 [2816, 2048], P('tensor', 'dp')
The draws below stay inside these ranges and needn't reach their ends.
Inputs may be any that keep to these rules, and one draw needn't show every extreme that they name: `routes`: each row names 6 different experts. In the rows of one index of dp no expert is named by more than 384 rows, and in some draws' devices one expert by exactly 384. `block_ids`: Non-decreasing along the positions; the j-th aligned run of 256 positions holds the blocks 2 j and 2 j + 1, each of 64 to 192 positions.
All inputs are finite; a program needn't handle non-finite values.
Results may differ from the reference program's by a relative error of at most 0.025.
Values may be sent and summed in bfloat16 or wider, within the bound.
A program may use at most 448 MiB of HBM per device.

```python
import math
import jax
import jax.numpy as jnp
import numpy as np
from jax import lax

D = 2048
H = 16
ND = 128
RD = 64
VD = 128
KVL = 512
MFF = 1408
SFF = 2816
EXPERTS = 12
TOP = 6
BLOCK = 256
TOK_DEV = 512
TOKENS = 4096
SEQ = 4096
CAP = 384
N_DP = 8


def draw_block_ids(key, part):
    key = jax.random.fold_in(key, 11)
    run_count = TOKENS // BLOCK
    cut_points = jax.random.randint(key, (run_count,), BLOCK // 4, 3 * BLOCK // 4 + 1, dtype=jnp.int32)
    places = jnp.arange(TOKENS, dtype=jnp.int32)
    run_number = places // BLOCK
    return (2 * run_number + (places % BLOCK >= cut_points[run_number]).astype(jnp.int32)).astype(jnp.int32)


def steps_of(rng, extent, cuts, low, largest):
    def one(axis_at, blocks):
        draws = jax.random.uniform(jax.random.fold_in(jax.random.fold_in(rng, 6), axis_at), (blocks,), jnp.float32, low / len(cuts), largest / len(cuts))
        return jnp.repeat(jnp.exp(draws), extent[axis_at] // blocks).reshape((-1,) + (1,) * (len(extent) - axis_at - 1))

    level = one(*cuts[0])
    for cut in cuts[1:]:
        level = level * one(*cut)
    return level


def assign_block(rng, own, number, rows, number_of, top, reach, slope):
    sequence = jax.random.permutation(rng, number_of)
    packed, common = load_shares(number_of, rows * top, reach, slope, True), load_shares(number_of, rows * top, reach, slope, False)
    places = jnp.arange(number_of)

    def named(tallies, turn):
        used = int((tallies > 0).sum())
        fixed = max(1, used // 4)
        shifted = fixed + (places - fixed + turn * (used - fixed)) % max(1, number_of - fixed)
        return jnp.zeros((number_of,), jnp.int32).at[sequence[jnp.where(places < fixed, places, shifted)]].set(jnp.asarray(tallies, jnp.int32))

    tallies = jnp.where(number % 4 == 0, named(packed, number // 4), named(common, number - number // 4 - 1))
    mixed = jax.random.permutation(jax.random.fold_in(own, 3), number_of)
    giver, taker = mixed[0:number_of // 2 * 2:2], mixed[1:number_of // 2 * 2:2]
    room = jnp.minimum(tallies[giver] - 1, reach - tallies[taker]) // 2
    room = jnp.where((giver == sequence[0]) | (taker == sequence[0]) | (tallies[taker] == 0), 0, jnp.maximum(room, 0))
    shifted = jax.random.randint(jax.random.fold_in(own, 4), (number_of // 2,), 0, 1 << 20) % (room + 1)
    tallies = tallies.at[giver].add(-shifted).at[taker].add(shifted)
    labels = jnp.searchsorted(jnp.cumsum(tallies), jnp.arange(rows * top), side="right").astype(jnp.int32)
    listing = labels.reshape(top, rows).T
    listing = listing[jax.random.permutation(jax.random.fold_in(own, 1), rows)]
    turn = jax.random.randint(jax.random.fold_in(own, 2), (rows, 1), 0, top)
    return jnp.take_along_axis(listing, (jnp.arange(top)[None, :] + turn) % top, axis=1)


def load_shares(number_of, total, limit, lean, full):
    loads = [(1 << 20) // math.isqrt(rank ** lean) + 1 for rank in range(1, number_of + 1)]
    largest = limit if full else min(limit, max(-(-total // number_of), total * loads[0] // sum(loads)))
    least = 1 if total - largest >= number_of - 1 else 0
    holding, rest = [largest] + [least] * (number_of - 1), total - largest - least * (number_of - 1)
    while rest > 0:
        free = [i for i in range(1, number_of) if holding[i] < largest] or [i for i in range(1, number_of) if holding[i] < limit]
        whole, remaining = sum([loads[i] for i in free]), rest
        for i in free:
            addition = min(limit - holding[i], max(1, remaining * loads[i] // whole), rest)
            holding[i] = holding[i] + addition
            rest = rest - addition
    return np.array(holding)


def centred(own_key, shape, deviation, most, shards=(), kind=jnp.bfloat16):
    array = deviation * jax.random.normal(own_key, shape, jnp.float32)
    if shards:
        array = array * steps_of(own_key, shape, shards, -0.22, 0.18)
    return jnp.clip(array, -most, most).astype(kind)


def setup_inputs(seed: int = 0) -> dict:
    key_of = jax.random.split(jax.random.key(seed), 19)
    tokens = centred(key_of[0], (TOKENS, D), 1.0, 6.0, ((0, 8),))
    cotangent = centred(key_of[1], (TOKENS, D), 1.0, 6.0, ((0, 8),))
    block_ids = draw_block_ids(jax.random.fold_in(key_of[18], 71), 0)
    routes_keys = jax.random.split(jax.random.fold_in(key_of[3], 1), TOKENS // TOK_DEV)
    routes_turns = jax.random.permutation(jax.random.fold_in(key_of[3], 3), TOKENS // TOK_DEV)
    routes = jax.vmap(lambda own, number: assign_block(jax.random.fold_in(key_of[3], 2), own, number, TOK_DEV, EXPERTS, TOP, CAP, 1))(routes_keys, routes_turns).reshape((TOKENS, TOP))
    first_gain = jnp.clip(1.0 + 0.1 * jax.random.normal(key_of[4], (D,), jnp.float32), 0.5, 1.5)
    query_weight = centred(key_of[5], (D, H * (ND + RD)), D ** -0.5, 0.125, ((1, 4),))
    latent_down = centred(key_of[6], (D, KVL + RD), D ** -0.5, 0.125)
    latent_gain = jnp.clip(1.0 + 0.1 * jax.random.normal(key_of[7], (KVL,), jnp.float32), 0.5, 1.5)
    latent_up = centred(key_of[8], (KVL, H * (ND + VD)), KVL ** -0.5, 0.25, ((1, 4),))
    output_weight = centred(key_of[9], (H * VD, D), (max(1, H * VD * 16 // SEQ)) ** -0.5, 2.0, ((0, 4),))
    second_gain = jnp.clip(1.0 + 0.1 * jax.random.normal(key_of[10], (D,), jnp.float32), 0.5, 1.5)
    router_weight = centred(key_of[11], (D, EXPERTS), (4 * D) ** -0.5, 0.0625)
    gate_weight = centred(key_of[12], (EXPERTS, D, MFF), D ** -0.5, 0.125, ((2, 4),))
    up_weight = centred(key_of[13], (EXPERTS, D, MFF), D ** -0.5, 0.125, ((2, 4),))
    down_weight = centred(key_of[14], (EXPERTS, MFF, D), (MFF // 4) ** -0.5, 0.3125, ((1, 4),))
    shared_gate = centred(key_of[15], (D, SFF), D ** -0.5, 0.125, ((1, 4),))
    shared_up = centred(key_of[16], (D, SFF), D ** -0.5, 0.125, ((1, 4),))
    shared_down = centred(key_of[17], (SFF, D), (SFF // 2) ** -0.5, 0.15625, ((0, 4),))
    return dict(tokens=tokens, cotangent=cotangent, block_ids=block_ids, routes=routes, first_gain=first_gain, query_weight=query_weight, latent_down=latent_down, latent_gain=latent_gain, latent_up=latent_up, output_weight=output_weight, second_gain=second_gain, router_weight=router_weight, gate_weight=gate_weight, up_weight=up_weight, down_weight=down_weight, shared_gate=shared_gate, shared_up=shared_up, shared_down=shared_down)


EPSILON = 1e-06
HIGHEST = lax.Precision.HIGHEST

@jax.custom_vjp
def low(v):
    return lax.optimization_barrier(v.astype(jnp.bfloat16)).astype(jnp.float32)

@jax.custom_vjp
def low_back(v):
    return v

def low_keep(v):
    return (low(v), None)

def low_pass(kept, grad):
    return (grad,)

def back_keep(v):
    return (v, None)

def back_low(kept, grad):
    return (low(grad),)
low.defvjp(low_keep, low_pass)
low_back.defvjp(back_keep, back_low)

def rotary_tables(places, rotary_width):
    halfway = rotary_width // 2
    frequency = 10000.0 ** (-jnp.arange(halfway, dtype=jnp.float32) * 2.0 / rotary_width)
    angles = places.astype(jnp.float32)[:, None] * frequency[None, :]
    return (jnp.cos(angles), jnp.sin(angles))

def rotate(values, cosine, sine_table):
    halfway = values.shape[-1] // 2
    leading = values[..., :halfway]
    trailing = values[..., halfway:]
    return jnp.concatenate([leading * cosine - trailing * sine_table, trailing * cosine + leading * sine_table], axis=-1)

def norm_rows(values, gain_row):
    return values * lax.rsqrt(lax.optimization_barrier(jnp.mean(values * values, axis=-1, keepdims=True)) + EPSILON) * gain_row

def slot_table(route_rows):
    flat_routes = route_rows.reshape(-1)
    pair_count = flat_routes.shape[0]
    matches = (flat_routes[:, None] == jnp.arange(EXPERTS, dtype=jnp.int32)[None, :]).astype(jnp.int32)
    slot_rank = lax.optimization_barrier(jnp.sum(matches * (jnp.cumsum(matches, axis=0) - 1), axis=1))
    slot_index = jnp.full((EXPERTS, CAP), pair_count, dtype=jnp.int32)
    return slot_index.at[flat_routes, slot_rank].set(jnp.arange(pair_count, dtype=jnp.int32))

def forward(tokens, first_gain, query_weight, latent_down, latent_gain, latent_up, output_weight, second_gain, router_weight, gate_weight, up_weight, down_weight, shared_gate, shared_up, shared_down, block_ids, routes):
    cosine, sine_table = rotary_tables(jnp.arange(TOKENS, dtype=jnp.int32) % SEQ, RD)
    attention_input = low(norm_rows(tokens, first_gain))
    queries = low_back(jnp.dot(attention_input, query_weight, precision=HIGHEST)).reshape(TOKENS, H, ND + RD)
    queries = low(jnp.concatenate([queries[..., :ND], rotate(queries[..., ND:], cosine[:, None], sine_table[:, None])], axis=-1))
    compressed = jnp.dot(attention_input, latent_down, precision=HIGHEST)
    latent = low(norm_rows(compressed[:, :KVL], latent_gain))
    key_rope = low(rotate(compressed[:, KVL:], cosine, sine_table))
    expanded = low(jnp.dot(latent, latent_up, precision=HIGHEST)).reshape(TOKENS, H, ND + VD)
    key_nope = expanded[..., :ND]
    values = expanded[..., ND:]
    factor = (ND + RD) ** (-0.5)
    block_rows = math.gcd(512, SEQ)

    def attend(offset):
        seq_start = (offset // SEQ * SEQ).astype(jnp.int32)
        query_rows = lax.dynamic_slice_in_dim(queries, offset, block_rows, 0)
        query_blocks = lax.dynamic_slice_in_dim(block_ids, offset, block_rows, 0)
        seq_nope = lax.dynamic_slice_in_dim(key_nope, seq_start, SEQ, 0)
        seq_rope = lax.dynamic_slice_in_dim(key_rope, seq_start, SEQ, 0)
        seq_values = lax.dynamic_slice_in_dim(values, seq_start, SEQ, 0)
        seq_blocks = lax.dynamic_slice_in_dim(block_ids, seq_start, SEQ, 0)
        scores = jnp.einsum('qhd,khd->hqk', query_rows[..., :ND], seq_nope, precision=HIGHEST)
        scores = scores + jnp.einsum('qhd,kd->hqk', query_rows[..., ND:], seq_rope, precision=HIGHEST)
        scores = low_back(scores * factor)
        scores = jnp.where(seq_blocks[None, None, :] <= query_blocks[None, :, None], scores, -1e+30)
        highest = lax.optimization_barrier(jnp.max(scores, axis=2, keepdims=True))
        weights = jnp.exp(scores - highest)
        chances = low(weights / lax.optimization_barrier(jnp.sum(weights, axis=2, keepdims=True)))
        return jnp.einsum('hqk,khd->qhd', chances, seq_values, precision=HIGHEST)
    attention_mix = lax.map(jax.checkpoint(attend), jnp.arange(TOKENS // block_rows, dtype=jnp.int32) * block_rows)
    attended = low(low_back(attention_mix.reshape(TOKENS, H * VD)))
    residual = tokens + low_back(jnp.dot(attended, output_weight, precision=HIGHEST))
    expert_input = low(norm_rows(residual, second_gain))
    router = jax.nn.softmax(jnp.dot(expert_input, router_weight, precision=HIGHEST), axis=-1)
    route_gates = jnp.take_along_axis(router, routes, axis=1)

    def device_experts(pieces):
        input_rows, gate_rows, route_rows = pieces
        slot_index = slot_table(route_rows)
        slot_token = slot_index // TOP
        buffer = jnp.concatenate([input_rows, jnp.zeros((1, D), jnp.float32)], axis=0)[slot_token]
        slot_gate = jnp.concatenate([gate_rows.reshape(-1), jnp.zeros((1,), jnp.float32)], axis=0)[slot_index]
        gate_pre = low_back(jnp.einsum('ecd,edf->ecf', buffer, gate_weight, precision=HIGHEST))
        up_pre = low_back(jnp.einsum('ecd,edf->ecf', buffer, up_weight, precision=HIGHEST))
        hidden = low(jax.nn.silu(gate_pre) * up_pre)
        expert_out = low_back(jnp.einsum('ecf,efd->ecd', hidden, down_weight, precision=HIGHEST))
        placed = jnp.zeros((TOK_DEV + 1, D), jnp.float32).at[slot_token.reshape(-1)].add((slot_gate[..., None] * expert_out).reshape(-1, D))
        return placed[:TOK_DEV]
    routed = lax.map(jax.checkpoint(device_experts), (expert_input.reshape(N_DP, TOK_DEV, D), route_gates.reshape(N_DP, TOK_DEV, TOP), routes.reshape(N_DP, TOK_DEV, TOP))).reshape(TOKENS, D)
    shared_pre = low_back(jnp.dot(expert_input, shared_gate, precision=HIGHEST))
    shared_lift = low_back(jnp.dot(expert_input, shared_up, precision=HIGHEST))
    shared_hidden = low(jax.nn.silu(shared_pre) * shared_lift)
    shared_out = low_back(jnp.dot(shared_hidden, shared_down, precision=HIGHEST))
    return residual + routed + shared_out

def reference(tokens, cotangent, block_ids, routes, first_gain, query_weight, latent_down, latent_gain, latent_up, output_weight, second_gain, router_weight, gate_weight, up_weight, down_weight, shared_gate, shared_up, shared_down):
    primals = (tokens.astype(jnp.float32), first_gain.astype(jnp.float32), query_weight.astype(jnp.float32), latent_down.astype(jnp.float32), latent_gain.astype(jnp.float32), latent_up.astype(jnp.float32), output_weight.astype(jnp.float32), second_gain.astype(jnp.float32), router_weight.astype(jnp.float32), gate_weight.astype(jnp.float32), up_weight.astype(jnp.float32), down_weight.astype(jnp.float32), shared_gate.astype(jnp.float32), shared_up.astype(jnp.float32), shared_down.astype(jnp.float32))
    output, pullback = jax.vjp(lambda *floats: forward(*floats, block_ids, routes), *primals)
    gradients = pullback(cotangent.astype(jnp.float32))
    return (output.astype(jnp.bfloat16), gradients[0].astype(jnp.bfloat16), gradients[1], gradients[2], gradients[3], gradients[4], gradients[5], gradients[6], gradients[7], gradients[8], gradients[9], gradients[10], gradients[11], gradients[12], gradients[13], gradients[14])
```

```python
import jax
import jax.numpy as jnp
from jax import lax
from jax.experimental import pallas as pl
from jax.experimental.pallas import tpu as pltpu
from jax.sharding import Mesh
from jax.sharding import PartitionSpec as P

ND = 128
RD = 64
VD = 128
KVL = 512
EXPERTS = 12
LAT = 640
EPSILON = 1e-06
LOG2E = 1.4426950408889634
BF = jnp.bfloat16
F32 = jnp.float32
VMEM_LIMIT = 60 * 1024 * 1024
DP = ("dpo", "core")
SPREAD = ("dpo", "tensor")
ALL = ("dpo", "core", "tensor")


def nn(former, latter):
    return jnp.dot(former, latter, preferred_element_type=F32)


def nt(former, latter):
    return lax.dot_general(former, latter, (((1,), (1,)), ((), ())), preferred_element_type=F32)


def tn(former, latter):
    return lax.dot_general(former, latter, (((0,), (0,)), ((), ())), preferred_element_type=F32)


def rotary_tables(places):
    halfway = RD // 2
    frequency = 10000.0 ** (-jnp.arange(halfway, dtype=F32) * 2.0 / RD)
    angles = places.astype(F32)[:, None] * frequency[None, :]
    return jnp.cos(angles), jnp.sin(angles)


def rotate(values, cosine, sine_table):
    halfway = values.shape[-1] // 2
    leading = values[..., :halfway]
    trailing = values[..., halfway:]
    return jnp.concatenate(
        [leading * cosine - trailing * sine_table, trailing * cosine + leading * sine_table],
        axis=-1,
    )


def norm_rows(values, gain_row):
    factor = lax.rsqrt(jnp.mean(values * values, axis=-1, keepdims=True) + EPSILON)
    return values * factor * gain_row, factor


def norm_back(values, factor, gain_row, upstream):
    weighted = upstream * gain_row
    common = jnp.mean(weighted * values, axis=-1, keepdims=True)
    return (
        factor * weighted - values * factor * factor * factor * common,
        jnp.sum(upstream * values * factor, axis=0),
    )


def expert_unit(gate_pre, up_pre, hidden_grad, gate):
    sigmoid = 0.5 * jnp.tanh(0.5 * gate_pre) + 0.5
    silu = gate_pre * sigmoid
    hidden = silu * up_pre
    scaled = gate * hidden_grad
    d_up = scaled * silu
    d_gate = scaled * up_pre * (sigmoid + silu - silu * sigmoid)
    return (
        (gate * hidden).astype(BF),
        d_gate.astype(BF),
        d_up.astype(BF),
        hidden * hidden_grad,
    )


def weight_copies(routed, shared, held, sems, step, slot, steps, width, begin):
    def each(refs):
        for i, ref in enumerate(refs):
            copy = pltpu.make_async_copy(
                ref, held.at[slot, pl.ds(i * width, width)], sems.at[slot, i]
            )
            if begin:
                copy.start()
            else:
                copy.wait()

    @pl.when(step < steps - 1)
    def _():
        rows = pl.ds(pl.multiple_of(step * width, width), width)
        each([ref.at[rows] for ref in routed])

    @pl.when(step == steps - 1)
    def _():
        each(shared)


def gate_rows(gates, width):
    parts, columns = gates.shape
    return jnp.concatenate(
        [jnp.broadcast_to(gates[i : i + 1], (width // parts, columns)) for i in range(parts)],
        axis=0,
    )


def own_experts(rows, upstream, gates, weights):
    count, model = rows.shape
    steps, parts, _ = gates.shape
    width = weights[3].shape[0]
    unit = width // parts
    wide = 512

    def kernel(x_ref, c_ref, g_ref, gw, uw, dw, sg, su, sd, out, back, kept_h, kept_g, kept_u, dots, held, sems):
        step = pl.program_id(0)
        slot = lax.rem(step, 2)
        routed, shared = (gw, uw, dw), (sg, su, sd)

        @pl.when(step == 0)
        def _():
            weight_copies(routed, shared, held, sems, step, slot, steps, width, True)
            out[...] = jnp.zeros_like(out)
            back[...] = jnp.zeros_like(back)

        weight_copies(routed, shared, held, sems, step, slot, steps, width, False)

        @pl.when(step < steps - 1)
        def _():
            weight_copies(routed, shared, held, sems, step + 1, 1 - slot, steps, width, True)

        both = nt(held[slot, : 2 * width], x_ref[...])
        hidden_grad = nt(held[slot, 2 * width :], c_ref[...])
        hidden, d_gate, d_up, products = expert_unit(
            both[:width], both[width:], hidden_grad, gate_rows(g_ref[0], width)
        )
        kept_h[0] = hidden
        kept_g[0] = d_gate
        kept_u[0] = d_up
        dots[0] = jnp.concatenate(
            [
                jnp.sum(products[i * unit : (i + 1) * unit], axis=0, keepdims=True)
                for i in range(parts)
            ],
            axis=0,
        )
        turned = hidden.T
        turned_back = jnp.concatenate([d_gate, d_up], axis=0).T
        for at in range(0, model, wide):
            columns = slice(at, at + wide)
            out[:, columns] += nn(turned, held[slot, 2 * width :, columns])
            back[:, columns] += nn(turned_back, held[slot, : 2 * width, columns])

    def whole(shape):
        return pl.BlockSpec(shape, lambda p: (0,) * len(shape), pipeline_mode=pl.Buffered(1))

    def one(shape):
        return pl.BlockSpec((1,) + shape, lambda p: (p, 0, 0))

    kept = jax.ShapeDtypeStruct((steps, width, count), BF)
    total = jax.ShapeDtypeStruct((count, model), F32)
    return pl.pallas_call(
        kernel,
        name="own_experts",
        grid=(steps,),
        in_specs=[whole(rows.shape), whole(upstream.shape), one((parts, count))]
        + [pl.BlockSpec(memory_space=pl.ANY)] * 6,
        out_specs=[whole((count, model))] * 2 + [one((width, count))] * 3 + [one((parts, count))],
        out_shape=[total, total, kept, kept, kept, jax.ShapeDtypeStruct((steps, parts, count), F32)],
        scratch_shapes=[
            pltpu.VMEM((2, 3 * width, model), BF),
            pltpu.SemaphoreType.DMA((2, 3)),
        ],
        cost_estimate=pl.CostEstimate(
            flops=steps * 12 * count * model * width,
            bytes_accessed=steps * 6 * width * model + 24 * count * model,
            transcendentals=0,
        ),
        compiler_params=pltpu.CompilerParams(
            vmem_limit_bytes=VMEM_LIMIT, dimension_semantics=("arbitrary",)
        ),
    )(rows, upstream, gates, *weights)


def group_gradients(place, rows, upstream, row_cols, up_cols, gates, kept, weights):
    chips, count, model = rows.shape
    steps, _, parts, _ = gates.shape
    width = weights[3].shape[0]
    half = row_cols.shape[2] // 2

    def kernel(place_ref, x_ref, c_ref, xc, cc, g_ref, kept_h, kept_g, kept_u, gw, uw, dw, sg, su, sd,
               own_g, own_u, own_d, far_g, far_u, far_d, held, sems, sum_g, sum_u, sum_d):
        step = pl.program_id(0)
        turn = pl.program_id(1)
        slot = lax.rem(step, 2)
        routed, shared = (gw, uw, dw), (sg, su, sd)

        @pl.when(turn == 0)
        def _():
            @pl.when(step == 0)
            def _():
                weight_copies(routed, shared, held, sems, step, slot, steps, width, True)

            sum_g[...] = nn(kept_g[0], xc[0])
            sum_u[...] = nn(kept_u[0], xc[0])
            sum_d[...] = nn(kept_h[0], cc[0])
            weight_copies(routed, shared, held, sems, step, slot, steps, width, False)

            @pl.when(step < steps - 1)
            def _():
                weight_copies(routed, shared, held, sems, step + 1, 1 - slot, steps, width, True)

        @pl.when(turn > 0)
        def _():
            unit = width // 2
            x = x_ref[0]
            c = c_ref[0]
            gate = gate_rows(g_ref[0, 0], width)
            for at in range(0, width, unit):
                gate_pre = nt(held[slot, at : at + unit], x)
                up_pre = nt(held[slot, width + at : width + at + unit], x)
                hidden_grad = nt(held[slot, 2 * width + at : 2 * width + at + unit], c)
                hidden, d_gate, d_up, _ = expert_unit(
                    gate_pre, up_pre, hidden_grad, gate[at : at + unit]
                )
                sum_g[at : at + unit] += nn(d_gate, xc[0])
                sum_u[at : at + unit] += nn(d_up, xc[0])
                sum_d[at : at + unit] += nn(hidden, cc[0])

        @pl.when(turn == chips - 1)
        def _():
            for total, near, far in ((sum_g, own_g, far_g), (sum_u, own_u, far_u), (sum_d, own_d, far_d)):
                near[...] = total[:, :half]
                far[...] = total[:, half:].astype(BF)

    def at_chip(shape):
        return pl.BlockSpec((1,) + shape, lambda p, k, z: (lax.rem(z[0] + k, chips), 0, 0))

    def one(shape):
        return pl.BlockSpec((1,) + shape, lambda p, k, z: (p, 0, 0))

    block = pl.BlockSpec((width, half), lambda p, k, z: (p, 0))
    flops = steps * 2 * width * count * (3 * (chips - 1) * model + 6 * chips * half)
    return pl.pallas_call(
        kernel,
        name="group_gradients",
        grid_spec=pltpu.PrefetchScalarGridSpec(
            num_scalar_prefetch=1,
            grid=(steps, chips),
            in_specs=[at_chip((count, model))] * 2
            + [at_chip((count, 2 * half))] * 2
            + [pl.BlockSpec((1, 1, parts, count), lambda p, k, z: (p, lax.rem(z[0] + k, chips), 0, 0))]
            + [one((width, count))] * 3
            + [pl.BlockSpec(memory_space=pl.ANY)] * 6,
            out_specs=[block] * 6,
            scratch_shapes=[
                pltpu.VMEM((2, 3 * width, model), BF),
                pltpu.SemaphoreType.DMA((2, 3)),
            ]
            + [pltpu.VMEM((width, 2 * half), F32)] * 3,
        ),
        out_shape=[jax.ShapeDtypeStruct((steps * width, half), F32)] * 3
        + [jax.ShapeDtypeStruct((steps * width, half), BF)] * 3,
        cost_estimate=pl.CostEstimate(
            flops=flops, bytes_accessed=steps * (6 * width * model + 4 * chips * count * model), transcendentals=0
        ),
        compiler_params=pltpu.CompilerParams(
            vmem_limit_bytes=VMEM_LIMIT, dimension_semantics=("arbitrary", "arbitrary")
        ),
    )(place, rows, upstream, row_cols, up_cols, gates, *kept, *weights)


def attention_forward(place, queries, latents, latent_up, key_ids, query_ids):
    count = queries.shape[0]
    heads = queries.shape[1] // 256
    scale = (ND + RD) ** (-0.5) * LOG2E

    def kernel(place_ref, q_ref, lat_ref, up_ref, kid_ref, qid_ref, att_ref, lse_ref, keys, top, low, mix):
        top[...] = jnp.full_like(top, -1e30)
        low[...] = jnp.zeros_like(low)
        mix[...] = jnp.zeros_like(mix)

        def chunk(at, masked):
            rows = pl.ds(pl.multiple_of(at * count, count), count)
            lat = lat_ref[rows, :KVL]
            rope = lat_ref[rows, KVL:]
            for h in range(heads):
                keys[h, :, ND:] = rope
                both = nn(lat, up_ref[:, h * 256 : (h + 1) * 256]).astype(BF)
                keys[h, :, :ND] = both[:, :ND]
                values = both[:, ND:].T
                scores = nt(keys[h], q_ref[:, h * 256 : (h + 1) * 256]) * scale
                if masked:
                    scores = jnp.where(kid_ref[...] <= qid_ref[...], scores, -1e30)
                before = top[h]
                highest = jnp.maximum(before, jnp.max(scores, axis=0, keepdims=True))
                weights = jnp.exp2(scores - highest)
                decay = jnp.exp2(before - highest)
                top[h] = highest
                low[h] = low[h] * decay + jnp.sum(weights, axis=0, keepdims=True)
                mix[h] = mix[h] * decay + nn(values, weights.astype(BF))

        place_at = place_ref[0]
        lax.fori_loop(0, place_at, lambda at, carry: (chunk(at, False), carry)[1], 0)
        chunk(place_at, True)
        for h in range(heads):
            att_ref[:, h * VD : (h + 1) * VD] = (mix[h] / low[h]).T.astype(BF)
            lse_ref[h] = top[h] + jnp.log2(low[h])

    def whole(shape):
        return pl.BlockSpec(shape, lambda i, z: (0,) * len(shape), pipeline_mode=pl.Buffered(1))

    return pl.pallas_call(
        kernel,
        name="attention_forward",
        grid_spec=pltpu.PrefetchScalarGridSpec(
            num_scalar_prefetch=1,
            grid=(1,),
            in_specs=[whole(a.shape) for a in (queries, latents, latent_up, key_ids, query_ids)],
            out_specs=[whole((count, heads * VD)), whole((heads, 1, count))],
            scratch_shapes=[
                pltpu.VMEM((heads, count, 256), BF),
                pltpu.VMEM((heads, 1, count), F32),
                pltpu.VMEM((heads, 1, count), F32),
                pltpu.VMEM((heads, VD, count), F32),
            ],
        ),
        out_shape=[
            jax.ShapeDtypeStruct((count, heads * VD), BF),
            jax.ShapeDtypeStruct((heads, 1, count), F32),
        ],
        cost_estimate=pl.CostEstimate(
            flops=heads * count * latents.shape[0] * 2 * 640, bytes_accessed=12_000_000, transcendentals=0
        ),
        compiler_params=pltpu.CompilerParams(
            vmem_limit_bytes=VMEM_LIMIT, dimension_semantics=("arbitrary",)
        ),
    )(place, queries, latents, latent_up, key_ids, query_ids)


def attention_backward(place, queries, latents, latent_up, key_ids, query_ids, mix_grad, lse, delta):
    count = queries.shape[0]
    heads = queries.shape[1] // 256
    total = latents.shape[0]
    factor = (ND + RD) ** (-0.5)
    scale = factor * LOG2E

    def kernel(place_ref, q_ref, lat_ref, up_ref, kid_ref, qid_ref, do_ref, lse_ref, delta_ref,
               dq_ref, dup_ref, dlat_ref, keys, dq, dlat):
        dq[...] = jnp.zeros_like(dq)
        dup_ref[...] = jnp.zeros_like(dup_ref)

        def chunk(at, masked):
            rows = pl.ds(pl.multiple_of(at * count, count), count)
            lat = lat_ref[rows, :KVL]
            turned = lat.T
            rope = lat_ref[rows, KVL:]
            dlat[...] = jnp.zeros_like(dlat)
            for h in range(heads):
                up = up_ref[:, h * 256 : (h + 1) * 256]
                query = q_ref[:, h * 256 : (h + 1) * 256]
                upstream = do_ref[:, h * VD : (h + 1) * VD]
                keys[h, :, ND:] = rope
                both = nn(lat, up).astype(BF)
                keys[h, :, :ND] = both[:, :ND]
                scores = nt(keys[h], query) * scale
                chances = jnp.exp2(scores - lse_ref[h])
                if masked:
                    chances = jnp.where(kid_ref[...] <= qid_ref[...], chances, 0.0)
                chance_grad = nt(both[:, ND:], upstream)
                score_grad = (chances * (chance_grad - delta_ref[h])).astype(BF)
                value_grad = nn(chances.astype(BF), upstream)
                key_grad = nn(score_grad, query) * factor
                dq[h] += nn(keys[h].T, score_grad)
                both_grad = jnp.concatenate([key_grad[:, :ND], value_grad], axis=1).astype(BF)
                dlat[:, :KVL] += nt(both_grad, up)
                dlat[:, KVL:] += key_grad[:, ND:]
                dup_ref[:, h * 256 : (h + 1) * 256] += nn(turned, both_grad)
            dlat_ref[rows, :] = dlat[...].astype(BF)

        place_at = place_ref[0]
        lax.fori_loop(0, place_at, lambda at, carry: (chunk(at, False), carry)[1], 0)
        chunk(place_at, True)

        def clear(at, carry):
            rows = pl.ds(pl.multiple_of(at * count, count), count)
            dlat_ref[rows, :] = jnp.zeros((count, LAT), BF)
            return carry

        lax.fori_loop(place_at + 1, total // count, clear, 0)
        for h in range(heads):
            dq_ref[:, h * 256 : (h + 1) * 256] = dq[h].T * factor

    def whole(shape):
        return pl.BlockSpec(shape, lambda i, z: (0,) * len(shape), pipeline_mode=pl.Buffered(1))

    ins = (queries, latents, latent_up, key_ids, query_ids, mix_grad, lse, delta)
    outs = [
        jax.ShapeDtypeStruct((count, heads * 256), F32),
        jax.ShapeDtypeStruct((KVL, heads * 256), F32),
        jax.ShapeDtypeStruct((total, LAT), BF),
    ]
    return pl.pallas_call(
        kernel,
        name="attention_backward",
        grid_spec=pltpu.PrefetchScalarGridSpec(
            num_scalar_prefetch=1,
            grid=(1,),
            in_specs=[whole(a.shape) for a in ins],
            out_specs=[whole(o.shape) for o in outs],
            scratch_shapes=[
                pltpu.VMEM((heads, count, 256), BF),
                pltpu.VMEM((heads, 256, count), F32),
                pltpu.VMEM((count, LAT), F32),
            ],
        ),
        out_shape=outs,
        cost_estimate=pl.CostEstimate(
            flops=heads * count * total * 2 * 1400, bytes_accessed=24_000_000, transcendentals=0
        ),
        compiler_params=pltpu.CompilerParams(
            vmem_limit_bytes=VMEM_LIMIT, dimension_semantics=("arbitrary",)
        ),
    )(place, *ins)


def router_of(rows, router_weight, route_rows):
    logits = lax.dot_general(
        router_weight, rows, (((0,), (1,)), ((), ())), preferred_element_type=F32
    )
    named = jnp.any(
        route_rows.T[None, :, :] == jnp.arange(EXPERTS, dtype=jnp.int32)[:, None, None], axis=1
    )
    return jax.nn.softmax(logits, axis=0), named


def grouped(gates, steps):
    parts = EXPERTS // (steps - 1)
    gates = gates.reshape((steps - 1, parts) + gates.shape[1:])
    return jnp.concatenate([gates, jnp.ones((1,) + gates.shape[1:], F32)], axis=0)


def shards(
    tokens,
    cotangent,
    block_ids,
    routes,
    first_gain,
    query_weight,
    latent_down,
    latent_gain,
    latent_up,
    output_weight,
    second_gain,
    router_weight,
    gate_weight,
    up_weight,
    down_weight,
    shared_gate,
    shared_up,
    shared_down,
):
    count, model = tokens.shape
    key_count = block_ids.shape[0]
    heads = query_weight.shape[1] // (ND + RD)
    unit = gate_weight.shape[2]
    width = shared_down.shape[0]
    steps = EXPERTS * unit // width + 1
    chips = lax.axis_size("dpo")
    ranks = lax.axis_size("tensor")
    devices = chips * 2 * ranks
    chip, core, rank = lax.axis_index("dpo"), lax.axis_index("core"), lax.axis_index("tensor")
    place = chip * 2 + core
    quarter = count // ranks
    half = model // (2 * chips)
    routed_rows = EXPERTS * unit

    def mine(array):
        return lax.dynamic_slice_in_dim(array, rank * quarter, quarter, 0)

    weights = (
        jnp.swapaxes(gate_weight, 1, 2).reshape(routed_rows, model),
        jnp.swapaxes(up_weight, 1, 2).reshape(routed_rows, model),
        down_weight.reshape(routed_rows, model),
        shared_gate.T,
        shared_up.T,
        shared_down,
    )

    row_start = place * count
    cosine, sine_table = rotary_tables((row_start + jnp.arange(count, dtype=jnp.int32)) % key_count)
    own_blocks = lax.dynamic_slice_in_dim(block_ids, row_start, count, 0)
    rows_float = tokens.astype(F32)
    normed_first, first_factor = norm_rows(rows_float, first_gain)
    attention_input = normed_first.astype(BF)
    compressed = nn(attention_input, latent_down)
    latent_raw = compressed[:, :KVL]
    latent_float, latent_factor = norm_rows(latent_raw, latent_gain)
    key_rope = rotate(compressed[:, KVL:], cosine, sine_table)
    latent = jnp.concatenate(
        [latent_float, key_rope, jnp.zeros((count, LAT - KVL - RD), F32)], axis=1
    ).astype(BF)
    latents = lax.all_gather(mine(latent), ALL, axis=0, tiled=True)

    upstream_quarter = mine(cotangent)
    after = lax.optimization_barrier((latents, upstream_quarter, mine(routes)))
    latents = after[0]
    all_upstream = lax.all_gather(after[1], SPREAD, axis=0, tiled=True)
    all_routes = lax.all_gather(after[2], SPREAD, axis=0, tiled=True)

    query_raw = nn(attention_input, query_weight).reshape(count, heads, ND + RD)
    queries = jnp.concatenate(
        [
            query_raw[..., :ND],
            rotate(query_raw[..., ND:], cosine[:, None], sine_table[:, None]),
            jnp.zeros((count, heads, 256 - ND - RD), F32),
        ],
        axis=-1,
    ).astype(BF).reshape(count, heads * 256)
    place_arg = place.reshape(1).astype(jnp.int32)
    key_ids, query_ids = own_blocks[:, None], own_blocks[None, :]
    attended, lse = attention_forward(place_arg, queries, latents, latent_up, key_ids, query_ids)

    attention_part = nn(attended, output_weight).astype(BF)
    residual = mine(tokens).astype(F32) + lax.psum_scatter(
        attention_part, "tensor", scatter_dimension=0, tiled=True
    ).astype(F32)
    normed_second, second_factor = norm_rows(residual, second_gain)
    input_quarter = normed_second.astype(BF)
    expert_input = lax.all_gather(input_quarter, "tensor", axis=0, tiled=True)
    after = lax.optimization_barrier((expert_input, input_quarter))
    expert_input = after[0]
    all_input = lax.all_gather(after[1], SPREAD, axis=0, tiled=True)

    router, named = router_of(expert_input, router_weight, routes)
    own_gates = grouped(jnp.where(named, router, 0.0), steps)
    expert_part, input_back, kept_h, kept_g, kept_u, dots = own_experts(
        expert_input, cotangent, own_gates, weights
    )
    expert_total = lax.psum_scatter(
        expert_part.astype(BF), "tensor", scatter_dimension=0, tiled=True
    ).astype(F32)
    pair_grad = jnp.where(named, dots[: steps - 1].reshape(EXPERTS, count), 0.0)
    logit_grad = router * (pair_grad - jnp.sum(router * pair_grad, axis=0, keepdims=True))
    logit_low = logit_grad.astype(BF)
    grad_router = lax.dot_general(
        expert_input, logit_low, (((0,), (1,)), ((), ())), preferred_element_type=F32
    )
    input_back = input_back + lax.dot_general(
        logit_low, router_weight, (((0,), (1,)), ((), ())), preferred_element_type=F32
    )
    input_grad = lax.psum_scatter(
        input_back.astype(BF), "tensor", scatter_dimension=0, tiled=True
    ).astype(F32)
    residual_back, grad_second_gain = norm_back(residual, second_factor, second_gain, input_grad)
    residual_grad = residual_back + upstream_quarter.astype(F32)
    output_grad = lax.all_gather(residual_grad.astype(BF), "tensor", axis=0, tiled=True)
    result = lax.all_gather(
        (residual + expert_total).astype(BF), "tensor", axis=0, tiled=True
    )
    early = jnp.concatenate(
        [
            grad_router.reshape(devices, -1),
            jnp.repeat(grad_second_gain.reshape(2 * chips, -1), ranks, axis=0),
        ],
        axis=1,
    )
    early = lax.psum_scatter(early, ALL, scatter_dimension=0, tiled=True).reshape(-1)
    router_size = model // devices * EXPERTS
    grad_router = early[:router_size].reshape(-1, EXPERTS)
    grad_second_gain = early[router_size:]

    all_input = all_input.reshape(chips, count, model)
    all_upstream = all_upstream.reshape(chips, count, model)
    all_router, all_named = router_of(
        all_input.reshape(chips * count, model), router_weight, all_routes
    )
    all_gates = jnp.swapaxes(
        grouped(jnp.where(all_named, all_router, 0.0), steps).reshape(steps, -1, chips, count), 1, 2
    )

    def chip_columns(array):
        return jnp.concatenate(
            [
                lax.dynamic_slice_in_dim(array, (chip * 2 + c) * half, half, 2)
                for c in (core, 1 - core)
            ],
            axis=2,
        )

    grads = group_gradients(
        chip.reshape(1).astype(jnp.int32),
        all_input,
        all_upstream,
        chip_columns(all_input),
        chip_columns(all_upstream),
        all_gates,
        (kept_h, kept_g, kept_u),
        weights,
    )
    swap = [(0, 1), (1, 0)]
    grads = [near + lax.ppermute(far, "core", swap).astype(F32) for near, far in zip(grads[:3], grads[3:])]

    grad_output = tn(attended, output_grad)
    attended_grad = nt(output_grad, output_weight).astype(BF)
    delta = jnp.sum(
        (attended.astype(F32) * attended_grad.astype(F32)).reshape(count, heads, VD), axis=2
    ).T[:, None, :]
    query_back, grad_latent_up, latent_part = attention_backward(
        place_arg, queries, latents, latent_up, key_ids, query_ids, attended_grad, lse, delta
    )
    compressed_grad = lax.psum_scatter(
        latent_part, DP, scatter_dimension=0, tiled=True
    ).astype(F32)
    query_back = query_back.reshape(count, heads, 256)
    query_grad = jnp.concatenate(
        [
            query_back[..., :ND],
            rotate(query_back[..., ND : ND + RD], cosine[:, None], -sine_table[:, None]),
        ],
        axis=-1,
    ).astype(BF).reshape(count, heads * (ND + RD))
    grad_query = tn(attention_input, query_grad)
    latent_grad, grad_latent_gain = norm_back(
        latent_raw, latent_factor, latent_gain, compressed_grad[:, :KVL]
    )
    down_grad = jnp.concatenate(
        [latent_grad, rotate(compressed_grad[:, KVL : KVL + RD], cosine, -sine_table)], axis=1
    ).astype(BF)
    grad_latent_down = tn(attention_input, down_grad)
    attention_grad = nt(query_grad, query_weight) + nt(down_grad, latent_down)
    grad_first_gain = jnp.sum(attention_grad * rows_float * first_factor, axis=0)
    attention_grad = lax.psum_scatter(
        attention_grad.astype(BF), "tensor", scatter_dimension=0, tiled=True
    ).astype(F32)
    token_back, _ = norm_back(
        mine(tokens).astype(F32), mine(first_factor), first_gain, attention_grad
    )
    token_grad = lax.all_gather(
        (token_back + residual_grad).astype(BF), "tensor", axis=0, tiled=True
    )
    late = jnp.concatenate(
        [
            grad_latent_down.reshape(devices, -1),
            jnp.repeat(grad_first_gain.reshape(2 * chips, -1), ranks, axis=0),
            grad_latent_gain.reshape(devices, -1),
        ],
        axis=1,
    ).astype(BF)
    late = lax.psum_scatter(late, ALL, scatter_dimension=0, tiled=True).astype(F32).reshape(-1)
    down_size = model // devices * (KVL + RD)
    gain_size = model // (2 * chips)

    def scattered(array, dimension):
        return lax.psum_scatter(
            array.astype(BF), DP, scatter_dimension=dimension, tiled=True
        ).astype(F32)

    def routed_of(array):
        return array[:routed_rows].reshape(EXPERTS, unit, half)

    return (
        result,
        token_grad,
        late[down_size : down_size + gain_size],
        scattered(grad_query, 0),
        late[:down_size].reshape(-1, KVL + RD),
        late[down_size + gain_size :],
        scattered(grad_latent_up, 0),
        scattered(grad_output, 1),
        grad_second_gain,
        grad_router,
        jnp.swapaxes(routed_of(grads[0]), 1, 2),
        jnp.swapaxes(routed_of(grads[1]), 1, 2),
        routed_of(grads[2]),
        grads[0][routed_rows:].T,
        grads[1][routed_rows:].T,
        grads[2][routed_rows:],
    )


def solution(mesh):
    groups, ranks = mesh.devices.shape
    fine = Mesh(mesh.devices.reshape(groups // 2, 2, ranks), ("dpo", "core", "tensor"))
    in_specs = (
        P(DP, None),
        P(DP, None),
        P(),
        P(DP, None),
        P(),
        P(None, "tensor"),
        P(),
        P(),
        P(None, "tensor"),
        P("tensor", None),
        P(),
        P(),
        P(None, None, "tensor"),
        P(None, None, "tensor"),
        P(None, "tensor", None),
        P(None, "tensor"),
        P(None, "tensor"),
        P("tensor", None),
    )
    out_specs = (
        P(DP, None),
        P(DP, None),
        P(DP),
        P(DP, "tensor"),
        P(ALL, None),
        P(ALL),
        P(DP, "tensor"),
        P("tensor", DP),
        P(DP),
        P(ALL, None),
        P(None, DP, "tensor"),
        P(None, DP, "tensor"),
        P(None, "tensor", DP),
        P(DP, "tensor"),
        P(DP, "tensor"),
        P("tensor", DP),
    )
    return jax.shard_map(shards, mesh=fine, in_specs=in_specs, out_specs=out_specs, check_vma=False)
```

```python
import jax
import jax.numpy as jnp
from jax import lax
from jax.experimental import pallas as pl
from jax.experimental.pallas import tpu as pltpu
from jax.sharding import Mesh
from jax.sharding import PartitionSpec as P

ND = 128
RD = 64
VD = 128
KVL = 512
EXPERTS = 12
LAT = 640
EPSILON = 1e-06
LOG2E = 1.4426950408889634
BF = jnp.bfloat16
F32 = jnp.float32
VMEM_LIMIT = 60 * 1024 * 1024
DP = ("dpo", "core")
SPREAD = ("dpo", "tensor")
ALL = ("dpo", "core", "tensor")
MESH = pl.DeviceIdType.MESH


def nn(former, latter):
    return jnp.dot(former, latter, preferred_element_type=F32)


def nt(former, latter):
    return lax.dot_general(former, latter, (((1,), (1,)), ((), ())), preferred_element_type=F32)


def tn(former, latter):
    return lax.dot_general(former, latter, (((0,), (0,)), ((), ())), preferred_element_type=F32)


def rotary_tables(places):
    halfway = RD // 2
    frequency = 10000.0 ** (-jnp.arange(halfway, dtype=F32) * 2.0 / RD)
    angles = places.astype(F32)[:, None] * frequency[None, :]
    return jnp.cos(angles), jnp.sin(angles)


def rotate(values, cosine, sine_table):
    halfway = values.shape[-1] // 2
    leading = values[..., :halfway]
    trailing = values[..., halfway:]
    return jnp.concatenate(
        [leading * cosine - trailing * sine_table, trailing * cosine + leading * sine_table],
        axis=-1,
    )


def norm_rows(values, gain_row):
    factor = lax.rsqrt(jnp.mean(values * values, axis=-1, keepdims=True) + EPSILON)
    return values * factor * gain_row, factor


def norm_back(values, factor, gain_row, upstream):
    weighted = upstream * gain_row
    common = jnp.mean(weighted * values, axis=-1, keepdims=True)
    return (
        factor * weighted - values * factor * factor * factor * common,
        jnp.sum(upstream * values * factor, axis=0),
    )


def expert_unit(gate_pre, up_pre, hidden_grad, gate):
    sigmoid = 0.5 * jnp.tanh(0.5 * gate_pre) + 0.5
    silu = gate_pre * sigmoid
    hidden = silu * up_pre
    scaled = gate * hidden_grad
    d_up = scaled * silu
    d_gate = scaled * up_pre * (sigmoid + silu - silu * sigmoid)
    return (
        (gate * hidden).astype(BF),
        d_gate.astype(BF),
        d_up.astype(BF),
        hidden * hidden_grad,
    )


def weight_copies(routed, shared, held, sems, step, slot, steps, width, begin):
    def each(refs):
        for i, ref in enumerate(refs):
            copy = pltpu.make_async_copy(
                ref, held.at[slot, pl.ds(i * width, width)], sems.at[slot, i]
            )
            if begin:
                copy.start()
            else:
                copy.wait()

    @pl.when(step < steps - 1)
    def _():
        rows = pl.ds(pl.multiple_of(step * width, width), width)
        each([ref.at[rows] for ref in routed])

    @pl.when(step == steps - 1)
    def _():
        each(shared)


def gate_rows(gates, width):
    parts, columns = gates.shape
    return jnp.concatenate(
        [jnp.broadcast_to(gates[i : i + 1], (width // parts, columns)) for i in range(parts)],
        axis=0,
    )


def own_experts(rows, upstream, gates, weights):
    count, model = rows.shape
    steps, parts, _ = gates.shape
    width = weights[3].shape[0]
    unit = width // parts
    wide = 512

    def kernel(x_ref, c_ref, g_ref, gw, uw, dw, sg, su, sd, out, back, kept_h, kept_g, kept_u, dots, held, sems):
        step = pl.program_id(0)
        slot = lax.rem(step, 2)
        routed, shared = (gw, uw, dw), (sg, su, sd)

        @pl.when(step == 0)
        def _():
            weight_copies(routed, shared, held, sems, step, slot, steps, width, True)
            out[...] = jnp.zeros_like(out)
            back[...] = jnp.zeros_like(back)

        weight_copies(routed, shared, held, sems, step, slot, steps, width, False)

        @pl.when(step < steps - 1)
        def _():
            weight_copies(routed, shared, held, sems, step + 1, 1 - slot, steps, width, True)

        both = nt(held[slot, : 2 * width], x_ref[...])
        hidden_grad = nt(held[slot, 2 * width :], c_ref[...])
        hidden, d_gate, d_up, products = expert_unit(
            both[:width], both[width:], hidden_grad, gate_rows(g_ref[0], width)
        )
        kept_h[0] = hidden
        kept_g[0] = d_gate
        kept_u[0] = d_up
        dots[0] = jnp.concatenate(
            [
                jnp.sum(products[i * unit : (i + 1) * unit], axis=0, keepdims=True)
                for i in range(parts)
            ],
            axis=0,
        )
        turned = hidden.T
        turned_back = jnp.concatenate([d_gate, d_up], axis=0).T
        for at in range(0, model, wide):
            columns = slice(at, at + wide)
            out[:, columns] += nn(turned, held[slot, 2 * width :, columns])
            back[:, columns] += nn(turned_back, held[slot, : 2 * width, columns])

    def whole(shape):
        return pl.BlockSpec(shape, lambda p: (0,) * len(shape), pipeline_mode=pl.Buffered(1))

    def one(shape):
        return pl.BlockSpec((1,) + shape, lambda p: (p, 0, 0))

    kept = jax.ShapeDtypeStruct((steps, width, count), BF)
    total = jax.ShapeDtypeStruct((count, model), F32)
    return pl.pallas_call(
        kernel,
        name="own_experts",
        grid=(steps,),
        in_specs=[whole(rows.shape), whole(upstream.shape), one((parts, count))]
        + [pl.BlockSpec(memory_space=pl.ANY)] * 6,
        out_specs=[whole((count, model))] * 2 + [one((width, count))] * 3 + [one((parts, count))],
        out_shape=[total, total, kept, kept, kept, jax.ShapeDtypeStruct((steps, parts, count), F32)],
        scratch_shapes=[
            pltpu.VMEM((2, 3 * width, model), BF),
            pltpu.SemaphoreType.DMA((2, 3)),
        ],
        cost_estimate=pl.CostEstimate(
            flops=steps * 12 * count * model * width,
            bytes_accessed=steps * 6 * width * model + 24 * count * model,
            transcendentals=0,
        ),
        compiler_params=pltpu.CompilerParams(
            vmem_limit_bytes=VMEM_LIMIT, dimension_semantics=("arbitrary",)
        ),
    )(rows, upstream, gates, *weights)


def ring_of(axis):
    here = lax.axis_index(axis)
    size = lax.axis_size(axis)
    return here, [lax.rem(here + i, size) for i in range(size)]


def greet(devices):
    barrier = pltpu.get_barrier_semaphore()
    for device in devices:
        pl.semaphore_signal(barrier, inc=1, device_id=device, device_id_type=MESH)
    pl.semaphore_wait(barrier, len(devices))


def remote(source, target, send, receive, device):
    return pltpu.make_async_remote_copy(
        src_ref=source, dst_ref=target, send_sem=send, recv_sem=receive,
        device_id=device, device_id_type=MESH,
    )


class Scatter:
    def __init__(self, rows):
        ranks = lax.axis_size("tensor")
        quarter = rows.shape[0] // ranks
        self.ins = [rows.reshape(ranks, quarter, rows.shape[1])]
        self.in_specs = [pl.BlockSpec(memory_space=pl.ANY)]
        self.outs = [jax.ShapeDtypeStruct((ranks - 1, quarter, rows.shape[1]), rows.dtype)]
        self.out_specs = [pl.BlockSpec(memory_space=pl.ANY)]
        self.scratch = [pltpu.SemaphoreType.DMA((ranks,)), pltpu.SemaphoreType.DMA((ranks,))]

    def copies(self, refs):
        source, target, sends, receives = refs
        _, peers = ring_of("tensor")
        return [
            remote(source.at[peer], target.at[d - 1], sends.at[d], receives.at[d], {"tensor": peer})
            for d, peer in enumerate(peers)
            if d
        ]

    def begin(self, refs):
        _, peers = ring_of("tensor")
        greet([{"tensor": peer} for peer in peers[1:]])
        for copy in self.copies(refs):
            copy.start()

    def middle(self, refs, step, last):
        pass

    def end(self, refs):
        for copy in self.copies(refs):
            copy.wait()


class Gather(Scatter):
    def __init__(self, rows):
        ranks = lax.axis_size("tensor")
        self.ins = [rows]
        self.in_specs = [pl.BlockSpec(memory_space=pl.ANY)]
        self.outs = [jax.ShapeDtypeStruct((ranks,) + rows.shape, rows.dtype)]
        self.out_specs = [pl.BlockSpec(memory_space=pl.ANY)]
        self.scratch = [pltpu.SemaphoreType.DMA((ranks,)), pltpu.SemaphoreType.DMA((ranks,))]

    def copies(self, refs):
        source, target, sends, receives = refs
        rank, peers = ring_of("tensor")
        return [pltpu.make_async_copy(source, target.at[rank], sends.at[0])] + [
            remote(source, target.at[rank], sends.at[d], receives.at[d], {"tensor": peer})
            for d, peer in enumerate(peers)
            if d
        ]


class LineSum:
    def __init__(self, blocks):
        chips = lax.axis_size("dpo")
        self.chips = chips
        shape = blocks.shape[1:]
        self.ins = [blocks]
        self.in_specs = [pl.BlockSpec(memory_space=pl.ANY)]
        self.outs = [jax.ShapeDtypeStruct(shape, F32)]
        self.out_specs = [pl.BlockSpec(shape, lambda *_: (0, 0), pipeline_mode=pl.Buffered(1))]
        self.scratch = [
            pltpu.VMEM((chips,) + shape, blocks.dtype),
            pltpu.VMEM((chips,) + shape, blocks.dtype),
            pltpu.VMEM(shape, blocks.dtype),
        ] + [pltpu.SemaphoreType.DMA((chips,))] * 4 + [pltpu.SemaphoreType.DMA]

    def swap(self, refs, i):
        source, _, mate, _, _, sends, receives, _, _, _ = refs
        core = lax.axis_index("core")
        return remote(source.at[2 * i + 1 - core], mate.at[i], sends.at[i], receives.at[i], {"core": 1 - core})

    def onward(self, refs, i):
        _, _, mate, inbox, _, _, _, sends, receives, _ = refs
        chip = lax.axis_index("dpo")
        return remote(mate.at[i], inbox.at[i], sends.at[i], receives.at[i], {"dpo": lax.rem(chip + self.chips - 1, self.chips)})

    def begin(self, refs):
        chip, core = lax.axis_index("dpo"), lax.axis_index("core")
        barrier = pltpu.get_barrier_semaphore()
        pl.semaphore_signal(barrier, inc=1, device_id={"core": 1 - core}, device_id_type=MESH)

        @pl.when(chip < self.chips - 1)
        def _():
            pl.semaphore_signal(barrier, inc=1, device_id={"dpo": chip + 1}, device_id_type=MESH)

        pl.semaphore_wait(barrier, 1 + jnp.where(chip > 0, 1, 0))

        for i in range(self.chips):
            @pl.when(i <= chip)
            def _():
                self.swap(refs, i).start()

    def middle(self, refs, step, last):
        source, out, mate, inbox, mine, _, _, _, _, sem = refs
        chip, core = lax.axis_index("dpo"), lax.axis_index("core")
        for i in range(self.chips):
            due = jnp.minimum(1 + 3 * (self.chips - 1 - chip) + i, last)

            @pl.when((i <= chip) & (step == due))
            def _():
                local = pltpu.make_async_copy(source.at[2 * i + core], mine, sem)
                local.start()
                self.swap(refs, i).wait()
                local.wait()

                @pl.when(chip < self.chips - 1)
                def _():
                    self.onward(refs, i).wait_recv()
                    mate[i] = (
                        mate[i].astype(F32) + mine[...].astype(F32) + inbox[i].astype(F32)
                    ).astype(mate.dtype)

                @pl.when(chip == self.chips - 1)
                def _():
                    mate[i] = (mate[i].astype(F32) + mine[...].astype(F32)).astype(mate.dtype)

                @pl.when(chip > i)
                def _():
                    self.onward(refs, i).start()

                @pl.when(chip == i)
                def _():
                    out[...] = mate[i].astype(F32)

    def end(self, refs):
        chip = lax.axis_index("dpo")
        for i in range(self.chips):
            @pl.when(chip > i)
            def _():
                self.onward(refs, i).wait_send()


def settle(part, more, gain, finish, extra, collective):
    count, model = part.shape
    ranks = lax.axis_size("tensor")
    quarter = count // ranks
    n_more, n_extra = len(more), len(extra)

    def kernel(*refs):
        part_ref, gain_ref = refs[:2]
        more_refs = refs[2 : 2 + n_more]
        out_ref = refs[2 + n_more]
        extra_refs = refs[3 + n_more : 3 + n_more + n_extra]
        inbox, block, gathered, send, receive, send_on, receive_on = refs[3 + n_more + n_extra :]
        rank, peers = ring_of("tensor")

        def rows_of(i):
            return pl.ds(pl.multiple_of(i * quarter, quarter), quarter)

        greet([{"tensor": peer} for peer in peers[1:]])
        copies = [
            remote(part_ref.at[rows_of(peer)], inbox.at[d], send.at[d], receive.at[d], {"tensor": peer})
            for d, peer in enumerate(peers)
            if d
        ]
        for copy in copies:
            copy.start()
        total = part_ref[rows_of(rank)].astype(F32)
        for d, copy in enumerate(copies):
            copy.wait()
            total = total + inbox[d + 1].astype(F32)
        results = finish(total, gain_ref[...], [r[...] for r in more_refs])
        for ref, value in zip(extra_refs, results):
            ref[...] = value
        block[...] = results[-1]
        copies = [
            remote(block, gathered.at[d], send_on.at[d], receive_on.at[d], {"tensor": peer})
            for d, peer in enumerate(peers)
            if d
        ]
        for copy in copies:
            copy.start()
        out_ref[rows_of(rank)] = block[...]
        for d, copy in enumerate(copies):
            copy.wait()
            out_ref[rows_of(lax.rem(rank + ranks - d - 1, ranks))] = gathered[d + 1]

    vmem = pl.BlockSpec(memory_space=pltpu.VMEM)
    sems = [pltpu.SemaphoreType.DMA((ranks,))] * 4
    return pl.pallas_call(
        kernel,
        name="settle",
        in_specs=[vmem] * (2 + n_more),
        out_specs=[vmem] * (1 + n_extra),
        out_shape=[jax.ShapeDtypeStruct((count, model), BF)] + extra,
        scratch_shapes=[
            pltpu.VMEM((ranks, quarter, model), BF),
            pltpu.VMEM((quarter, model), BF),
            pltpu.VMEM((ranks, quarter, model), BF),
        ]
        + sems,
        cost_estimate=pl.CostEstimate(flops=1000, bytes_accessed=150_000_000, transcendentals=0),
        compiler_params=pltpu.CompilerParams(
            vmem_limit_bytes=VMEM_LIMIT, collective_id=collective, has_side_effects=True
        ),
    )(part, gain, *more)


def group_gradients(rows, upstream, row_cols, up_cols, gates, kept, weights, first, groups, held_back, beside, collective):
    chips, count, model = rows.shape
    steps, _, parts, _ = gates.shape
    width = weights[3].shape[0]
    half = row_cols.shape[2] // 2
    n_ins = len(beside.ins) if beside else 0
    n_outs = len(beside.outs) if beside else 0
    n_held = len(held_back)
    last = groups * chips - 1

    def kernel(*refs):
        refs = list(refs)

        def take(n):
            taken = refs[:n]
            del refs[:n]
            return taken

        x_ref, c_ref, xc, cc, g_ref, kept_h, kept_g, kept_u = take(8)
        routed, shared = take(3), take(3)
        take(n_held)
        link_refs = take(n_ins)
        own_g, own_u, own_d, far_g, far_u, far_d = take(6)
        link_refs += take(n_outs)
        held, sems, sum_g, sum_u, sum_d = take(5)
        link_refs += refs
        at_group = pl.program_id(0)
        turn = pl.program_id(1)
        step = at_group + first
        slot = lax.rem(at_group, 2)
        tick = at_group * chips + turn

        if beside:
            @pl.when(tick == 0)
            def _():
                beside.begin(link_refs)

        @pl.when(turn == 0)
        def _():
            @pl.when(at_group == 0)
            def _():
                weight_copies(routed, shared, held, sems, step, slot, steps, width, True)

            sum_g[...] = nn(kept_g[0], xc[0])
            sum_u[...] = nn(kept_u[0], xc[0])
            sum_d[...] = nn(kept_h[0], cc[0])
            weight_copies(routed, shared, held, sems, step, slot, steps, width, False)

            @pl.when(at_group < groups - 1)
            def _():
                weight_copies(routed, shared, held, sems, step + 1, 1 - slot, steps, width, True)

        @pl.when(turn > 0)
        def _():
            unit = width // 2
            x = x_ref[0]
            c = c_ref[0]
            gate = gate_rows(g_ref[0, 0], width)
            for at in range(0, width, unit):
                gate_pre = nt(held[slot, at : at + unit], x)
                up_pre = nt(held[slot, width + at : width + at + unit], x)
                hidden_grad = nt(held[slot, 2 * width + at : 2 * width + at + unit], c)
                hidden, d_gate, d_up, _ = expert_unit(
                    gate_pre, up_pre, hidden_grad, gate[at : at + unit]
                )
                sum_g[at : at + unit] += nn(d_gate, xc[0])
                sum_u[at : at + unit] += nn(d_up, xc[0])
                sum_d[at : at + unit] += nn(hidden, cc[0])

        @pl.when(turn == chips - 1)
        def _():
            for total, near, far in ((sum_g, own_g, far_g), (sum_u, own_u, far_u), (sum_d, own_d, far_d)):
                near[...] = total[:, :half]
                far[...] = total[:, half:].astype(BF)

        if beside:
            beside.middle(link_refs, tick, last)

            @pl.when(tick == last)
            def _():
                beside.end(link_refs)

    def chip_at(turn):
        return lax.rem(lax.axis_index("dpo") + turn, chips)

    def at_chip(shape):
        return pl.BlockSpec((1,) + shape, lambda p, k: (chip_at(k), 0, 0))

    def one(shape):
        return pl.BlockSpec((1,) + shape, lambda p, k: (p + first, 0, 0))

    anywhere = pl.BlockSpec(memory_space=pl.ANY)
    near_block = pl.BlockSpec((width, half), lambda p, k: (p + first, 0))
    far_block = pl.BlockSpec((width, half), lambda p, k: (p, 0))
    flops = groups * 2 * width * count * (3 * (chips - 1) * model + 6 * chips * half)
    return pl.pallas_call(
        kernel,
        name="group_gradients",
        grid_spec=pltpu.PrefetchScalarGridSpec(
            num_scalar_prefetch=0,
            grid=(groups, chips),
            in_specs=[at_chip((count, model))] * 2
            + [at_chip((count, 2 * half))] * 2
            + [pl.BlockSpec((1, 1, parts, count), lambda p, k: (p + first, chip_at(k), 0, 0))]
            + [one((width, count))] * 3
            + [anywhere] * (6 + n_held)
            + (beside.in_specs if beside else []),
            out_specs=[near_block] * 3 + [far_block] * 3 + (beside.out_specs if beside else []),
            scratch_shapes=[
                pltpu.VMEM((2, 3 * width, model), BF),
                pltpu.SemaphoreType.DMA((2, 3)),
            ]
            + [pltpu.VMEM((width, 2 * half), F32)] * 3
            + (beside.scratch if beside else []),
        ),
        out_shape=[jax.ShapeDtypeStruct((steps * width, half), F32)] * 3
        + [jax.ShapeDtypeStruct((groups * width, half), BF)] * 3
        + (beside.outs if beside else []),
        input_output_aliases={14 + i: i for i in range(n_held)},
        cost_estimate=pl.CostEstimate(
            flops=flops, bytes_accessed=groups * (6 * width * model + 4 * chips * count * model), transcendentals=0
        ),
        compiler_params=pltpu.CompilerParams(
            vmem_limit_bytes=VMEM_LIMIT,
            dimension_semantics=("arbitrary", "arbitrary"),
            **(dict(collective_id=collective, has_side_effects=True) if beside else {}),
        ),
    )(
        rows, upstream, row_cols, up_cols, gates, *kept, *weights, *held_back,
        *(beside.ins if beside else []),
    )


def attention_forward(queries, latent, latent_up, key_ids, query_ids, collective):
    count = queries.shape[0]
    heads = queries.shape[1] // 256
    chips = lax.axis_size("dpo")
    scale = (ND + RD) ** (-0.5) * LOG2E

    def kernel(q_ref, lat_ref, up_ref, kid_ref, qid_ref, att_ref, lse_ref, all_ref, keys, top, low, mix,
               local, send_right, take_left, send_mate, take_mate):
        chip, core = lax.axis_index("dpo"), lax.axis_index("core")
        place = chip * 2 + core
        right = lax.rem(chip + 1, chips)
        left = lax.rem(chip + chips - 1, chips)
        barrier = pltpu.get_barrier_semaphore()
        pl.semaphore_signal(barrier, inc=1, device_id={"core": 1 - core}, device_id_type=MESH)

        @pl.when(chip > 0)
        def _():
            pl.semaphore_signal(barrier, inc=1, device_id={"dpo": left}, device_id_type=MESH)

        pl.semaphore_wait(barrier, 1 + jnp.where(chip < chips - 1, 1, 0))

        def to_right(source, i):
            return remote(source, all_ref.at[2 * i + core], send_right.at[i], take_left.at[i], {"dpo": right})

        def to_mate(source, i):
            return remote(source, all_ref.at[2 * i + core], send_mate.at[i], take_mate.at[i], {"core": 1 - core})

        @pl.when(chip < chips - 1)
        def _():
            to_right(lat_ref, chip).start()

        to_mate(lat_ref, chip).start()
        keep = pltpu.make_async_copy(lat_ref, all_ref.at[place], local)
        keep.start()
        top[...] = jnp.full_like(top, -1e30)
        low[...] = jnp.zeros_like(low)
        mix[...] = jnp.zeros_like(mix)

        def chunk(source, masked):
            lat = source[:, :KVL]
            rope = source[:, KVL:]
            for h in range(heads):
                keys[h, :, ND:] = rope
                both = nn(lat, up_ref[:, h * 256 : (h + 1) * 256]).astype(BF)
                keys[h, :, :ND] = both[:, :ND]
                values = both[:, ND:].T
                scores = nt(keys[h], q_ref[:, h * 256 : (h + 1) * 256]) * scale
                if masked:
                    scores = jnp.where(kid_ref[...] <= qid_ref[...], scores, -1e30)
                before = top[h]
                highest = jnp.maximum(before, jnp.max(scores, axis=0, keepdims=True))
                weights = jnp.exp2(scores - highest)
                decay = jnp.exp2(before - highest)
                top[h] = highest
                low[h] = low[h] * decay + jnp.sum(weights, axis=0, keepdims=True)
                mix[h] = mix[h] * decay + nn(values, weights.astype(BF))

        chunk(lat_ref, True)
        keep.wait()
        to_mate(lat_ref, chip).wait()

        @pl.when(core == 1)
        def _():
            chunk(all_ref.at[place - 1], False)

        def earlier(i, carry):
            at = chip - 1 - i
            arrived = all_ref.at[2 * at + core]
            to_right(arrived, at).wait_recv()

            @pl.when(chip < chips - 1)
            def _():
                to_right(arrived, at).start()

            to_mate(arrived, at).start()
            chunk(arrived, False)
            to_mate(arrived, at).wait_recv()
            chunk(all_ref.at[2 * at + 1 - core], False)
            return carry

        lax.fori_loop(0, chip, earlier, 0)
        for h in range(heads):
            att_ref[:, h * VD : (h + 1) * VD] = (mix[h] / low[h]).T.astype(BF)
            lse_ref[h] = top[h] + jnp.log2(low[h])

        def sent(i, carry):
            to_mate(lat_ref, i).wait_send()
            return carry

        lax.fori_loop(0, chip, sent, 0)

        @pl.when(chip < chips - 1)
        def _():
            def sent_right(i, carry):
                to_right(lat_ref, i).wait_send()
                return carry

            lax.fori_loop(0, chip + 1, sent_right, 0)

    vmem = pl.BlockSpec(memory_space=pltpu.VMEM)
    sems = pltpu.SemaphoreType.DMA((chips,))
    return pl.pallas_call(
        kernel,
        name="attention_forward",
        in_specs=[vmem] * 5,
        out_specs=[vmem] * 3,
        out_shape=[
            jax.ShapeDtypeStruct((count, heads * VD), BF),
            jax.ShapeDtypeStruct((heads, 1, count), F32),
            jax.ShapeDtypeStruct((2 * chips, count, LAT), BF),
        ],
        scratch_shapes=[
            pltpu.VMEM((heads, count, 256), BF),
            pltpu.VMEM((heads, 1, count), F32),
            pltpu.VMEM((heads, 1, count), F32),
            pltpu.VMEM((heads, VD, count), F32),
            pltpu.SemaphoreType.DMA,
            sems,
            sems,
            sems,
            sems,
        ],
        cost_estimate=pl.CostEstimate(
            flops=1000, bytes_accessed=200_000_000, transcendentals=0
        ),
        compiler_params=pltpu.CompilerParams(
            vmem_limit_bytes=VMEM_LIMIT, collective_id=collective, has_side_effects=True
        ),
    )(queries, latent, latent_up, key_ids, query_ids)


def attention_backward(place, queries, latents, latent_up, key_ids, query_ids, mix_grad, lse, delta):
    count = queries.shape[0]
    heads = queries.shape[1] // 256
    total = latents.shape[0]
    factor = (ND + RD) ** (-0.5)
    scale = factor * LOG2E

    def kernel(place_ref, q_ref, lat_ref, up_ref, kid_ref, qid_ref, do_ref, lse_ref, delta_ref,
               dq_ref, dup_ref, dlat_ref, keys, dq, dlat):
        dq[...] = jnp.zeros_like(dq)
        dup_ref[...] = jnp.zeros_like(dup_ref)

        def chunk(at, masked):
            rows = pl.ds(pl.multiple_of(at * count, count), count)
            lat = lat_ref[rows, :KVL]
            turned = lat.T
            rope = lat_ref[rows, KVL:]
            dlat[...] = jnp.zeros_like(dlat)
            for h in range(heads):
                up = up_ref[:, h * 256 : (h + 1) * 256]
                query = q_ref[:, h * 256 : (h + 1) * 256]
                upstream = do_ref[:, h * VD : (h + 1) * VD]
                keys[h, :, ND:] = rope
                both = nn(lat, up).astype(BF)
                keys[h, :, :ND] = both[:, :ND]
                scores = nt(keys[h], query) * scale
                chances = jnp.exp2(scores - lse_ref[h])
                if masked:
                    chances = jnp.where(kid_ref[...] <= qid_ref[...], chances, 0.0)
                chance_grad = nt(both[:, ND:], upstream)
                score_grad = (chances * (chance_grad - delta_ref[h])).astype(BF)
                value_grad = nn(chances.astype(BF), upstream)
                key_grad = nn(score_grad, query) * factor
                dq[h] += nn(keys[h].T, score_grad)
                both_grad = jnp.concatenate([key_grad[:, :ND], value_grad], axis=1).astype(BF)
                dlat[:, :KVL] += nt(both_grad, up)
                dlat[:, KVL:] += key_grad[:, ND:]
                dup_ref[:, h * 256 : (h + 1) * 256] += nn(turned, both_grad)
            dlat_ref[rows, :] = dlat[...].astype(BF)

        place_at = place_ref[0]
        lax.fori_loop(0, place_at, lambda at, carry: (chunk(at, False), carry)[1], 0)
        chunk(place_at, True)

        def clear(at, carry):
            rows = pl.ds(pl.multiple_of(at * count, count), count)
            dlat_ref[rows, :] = jnp.zeros((count, LAT), BF)
            return carry

        lax.fori_loop(place_at + 1, total // count, clear, 0)
        for h in range(heads):
            dq_ref[:, h * 256 : (h + 1) * 256] = dq[h].T * factor

    def whole(shape):
        return pl.BlockSpec(shape, lambda i, z: (0,) * len(shape), pipeline_mode=pl.Buffered(1))

    ins = (queries, latents, latent_up, key_ids, query_ids, mix_grad, lse, delta)
    outs = [
        jax.ShapeDtypeStruct((count, heads * 256), F32),
        jax.ShapeDtypeStruct((KVL, heads * 256), F32),
        jax.ShapeDtypeStruct((total, LAT), BF),
    ]
    return pl.pallas_call(
        kernel,
        name="attention_backward",
        grid_spec=pltpu.PrefetchScalarGridSpec(
            num_scalar_prefetch=1,
            grid=(1,),
            in_specs=[whole(a.shape) for a in ins],
            out_specs=[whole(o.shape) for o in outs],
            scratch_shapes=[
                pltpu.VMEM((heads, count, 256), BF),
                pltpu.VMEM((heads, 256, count), F32),
                pltpu.VMEM((count, LAT), F32),
            ],
        ),
        out_shape=outs,
        cost_estimate=pl.CostEstimate(
            flops=heads * count * total * 2 * 1400, bytes_accessed=24_000_000, transcendentals=0
        ),
        compiler_params=pltpu.CompilerParams(
            vmem_limit_bytes=VMEM_LIMIT, dimension_semantics=("arbitrary",)
        ),
    )(place, *ins)


def router_of(rows, router_weight):
    logits = lax.dot_general(
        router_weight, rows, (((0,), (1,)), ((), ())), preferred_element_type=F32
    )
    return jax.nn.softmax(logits, axis=0)


def grouped(gates, steps):
    parts = EXPERTS // (steps - 1)
    gates = gates.reshape((steps - 1, parts) + gates.shape[1:])
    return jnp.concatenate([gates, jnp.ones((1,) + gates.shape[1:], F32)], axis=0)


def shards(
    tokens,
    cotangent,
    block_ids,
    routes,
    first_gain,
    query_weight,
    latent_down,
    latent_gain,
    latent_up,
    output_weight,
    second_gain,
    router_weight,
    gate_weight,
    up_weight,
    down_weight,
    shared_gate,
    shared_up,
    shared_down,
):
    count, model = tokens.shape
    key_count = block_ids.shape[0]
    heads = query_weight.shape[1] // (ND + RD)
    unit = gate_weight.shape[2]
    width = shared_down.shape[0]
    steps = EXPERTS * unit // width + 1
    chips = lax.axis_size("dpo")
    ranks = lax.axis_size("tensor")
    devices = chips * 2 * ranks
    chip, core, rank = lax.axis_index("dpo"), lax.axis_index("core"), lax.axis_index("tensor")
    place = chip * 2 + core
    quarter = count // ranks
    half = model // (2 * chips)
    routed_rows = EXPERTS * unit

    def mine(array):
        return lax.dynamic_slice_in_dim(array, rank * quarter, quarter, 0)

    weights = (
        jnp.swapaxes(gate_weight, 1, 2).reshape(routed_rows, model),
        jnp.swapaxes(up_weight, 1, 2).reshape(routed_rows, model),
        down_weight.reshape(routed_rows, model),
        shared_gate.T,
        shared_up.T,
        shared_down,
    )

    row_start = place * count
    cosine, sine_table = rotary_tables((row_start + jnp.arange(count, dtype=jnp.int32)) % key_count)
    own_blocks = lax.dynamic_slice_in_dim(block_ids, row_start, count, 0)
    rows_float = tokens.astype(F32)
    normed_first, first_factor = norm_rows(rows_float, first_gain)
    attention_input = normed_first.astype(BF)
    compressed = nn(attention_input, latent_down)
    latent_raw = compressed[:, :KVL]
    latent_float, latent_factor = norm_rows(latent_raw, latent_gain)
    key_rope = rotate(compressed[:, KVL:], cosine, sine_table)
    latent = jnp.concatenate(
        [latent_float, key_rope, jnp.zeros((count, LAT - KVL - RD), F32)], axis=1
    ).astype(BF)
    named = jnp.any(
        routes[:, :, None] == jnp.arange(EXPERTS, dtype=jnp.int32)[None, None, :], axis=1
    )
    upstream_quarter = mine(cotangent)
    all_upstream = lax.all_gather(
        jnp.concatenate(
            [upstream_quarter, jnp.pad(mine(named).astype(BF), ((0, 0), (0, 128 - EXPERTS)))], axis=1
        ),
        SPREAD,
        axis=0,
        tiled=True,
    ).reshape(chips, count, model + 128)

    query_raw = nn(attention_input, query_weight).reshape(count, heads, ND + RD)
    queries = jnp.concatenate(
        [
            query_raw[..., :ND],
            rotate(query_raw[..., ND:], cosine[:, None], sine_table[:, None]),
            jnp.zeros((count, heads, 256 - ND - RD), F32),
        ],
        axis=-1,
    ).astype(BF).reshape(count, heads * 256)
    key_ids, query_ids = own_blocks[:, None], own_blocks[None, :]
    attended, lse, latents = attention_forward(
        queries, latent, latent_up, key_ids, query_ids, 1
    )
    latents = latents.reshape(key_count, LAT)

    def second_norm(total, gain, more):
        residual = more[0].astype(F32) + total
        normed, _ = norm_rows(residual, gain)
        return residual, normed.astype(BF)

    token_quarter = mine(tokens)
    block = jax.ShapeDtypeStruct((quarter, model), F32)
    expert_input, residual = settle(
        nn(attended, output_weight).astype(BF),
        [token_quarter],
        second_gain[None],
        second_norm,
        [block],
        2,
    )
    all_input = lax.all_gather(mine(expert_input), SPREAD, axis=0, tiled=True)

    named = named.T
    router = router_of(expert_input, router_weight)
    own_gates = grouped(jnp.where(named, router, 0.0), steps)
    expert_part, input_back, kept_h, kept_g, kept_u, dots = own_experts(
        expert_input, cotangent, own_gates, weights
    )
    pair_grad = jnp.where(named, dots[: steps - 1].reshape(EXPERTS, count), 0.0)
    logit_grad = router * (pair_grad - jnp.sum(router * pair_grad, axis=0, keepdims=True))
    logit_low = logit_grad.astype(BF)
    grad_router = lax.dot_general(
        expert_input, logit_low, (((0,), (1,)), ((), ())), preferred_element_type=F32
    )
    input_back = (
        input_back
        + lax.dot_general(
            logit_low, router_weight, (((0,), (1,)), ((), ())), preferred_element_type=F32
        )
    ).astype(BF)

    all_input = all_input.reshape(chips, count, model)
    all_named = all_upstream[:, :, model : model + EXPERTS].reshape(chips * count, EXPERTS).T
    all_router = router_of(all_input.reshape(chips * count, model), router_weight)
    all_gates = jnp.swapaxes(
        grouped(all_router * all_named.astype(F32), steps).reshape(steps, -1, chips, count), 1, 2
    )

    def chip_columns(array):
        return jnp.concatenate(
            [
                lax.dynamic_slice_in_dim(array, (chip * 2 + c) * half, half, 2)
                for c in (core, 1 - core)
            ],
            axis=2,
        )

    input_cols, upstream_cols = chip_columns(all_input), chip_columns(all_upstream)
    near, far = [], []

    def piece(first, groups, beside, collective):
        made = group_gradients(
            all_input, all_upstream, input_cols, upstream_cols, all_gates,
            (kept_h, kept_g, kept_u), weights, first, groups, near, beside, collective,
        )
        near[:] = made[:3]
        far.append([lax.ppermute(f, "core", [(0, 1), (1, 0)]) for f in made[3:6]])
        return made[6:]

    def summed(rows, got):
        return mine(rows).astype(F32) + jnp.sum(got.astype(F32), axis=0)

    (got,) = piece(0, 1, Scatter(input_back), 3)
    second_factor = lax.rsqrt(jnp.mean(residual * residual, axis=-1, keepdims=True) + EPSILON)
    residual_back, grad_second_gain = norm_back(
        residual, second_factor, second_gain, summed(input_back, got)
    )
    residual_grad = residual_back + upstream_quarter.astype(F32)
    (output_grad,) = piece(1, 1, Gather(residual_grad.astype(BF)), 4)
    output_grad = output_grad.reshape(count, model)

    attended_grad = nt(output_grad, output_weight).astype(BF)
    delta = jnp.sum(
        (attended.astype(F32) * attended_grad.astype(F32)).reshape(count, heads, VD), axis=2
    ).T[:, None, :]
    place_arg = place.reshape(1).astype(jnp.int32)
    query_back, grad_latent_up, latent_part = attention_backward(
        place_arg, queries, latents, latent_up, key_ids, query_ids, attended_grad, lse, delta
    )
    (compressed_grad,) = piece(2, steps - 4, LineSum(latent_part.reshape(2 * chips, count, LAT)), 5)
    query_back = query_back.reshape(count, heads, 256)
    query_grad = jnp.concatenate(
        [
            query_back[..., :ND],
            rotate(query_back[..., ND : ND + RD], cosine[:, None], -sine_table[:, None]),
        ],
        axis=-1,
    ).astype(BF).reshape(count, heads * (ND + RD))
    latent_grad, grad_latent_gain = norm_back(
        latent_raw, latent_factor, latent_gain, compressed_grad[:, :KVL]
    )
    down_grad = jnp.concatenate(
        [latent_grad, rotate(compressed_grad[:, KVL : KVL + RD], cosine, -sine_table)], axis=1
    ).astype(BF)
    attention_grad = nt(query_grad, query_weight) + nt(down_grad, latent_down)
    grad_first_gain = jnp.sum(attention_grad * rows_float * first_factor, axis=0)
    attention_grad = attention_grad.astype(BF)
    (got,) = piece(steps - 2, 1, Scatter(attention_grad), 6)
    token_back, _ = norm_back(
        token_quarter.astype(F32), mine(first_factor), first_gain, summed(attention_grad, got)
    )
    (token_grad,) = piece(steps - 1, 1, Gather((token_back + residual_grad).astype(BF)), 7)
    token_grad = token_grad.reshape(count, model)
    grads = [
        n + jnp.concatenate([f[i] for f in far], axis=0).astype(F32) for i, n in enumerate(near)
    ]

    expert_total = lax.psum_scatter(
        expert_part.astype(BF), "tensor", scatter_dimension=0, tiled=True
    ).astype(F32)
    result = lax.all_gather(
        (residual + expert_total).astype(BF), "tensor", axis=0, tiled=True
    )
    grad_output = tn(attended, output_grad)
    grad_query = tn(attention_input, query_grad)
    grad_latent_down = tn(attention_input, down_grad)

    def packed(arrays, dtype):
        rows = jnp.concatenate([a.reshape(devices, -1).astype(dtype) for a in arrays], axis=1)
        rows = jnp.pad(rows, ((0, 0), (0, -rows.shape[1] % 2048)))
        return lax.psum_scatter(
            rows.reshape(-1, 128), ALL, scatter_dimension=0, tiled=True
        ).astype(F32).reshape(-1)

    def for_ranks(gain):
        return jnp.repeat(gain.reshape(2 * chips, -1), ranks, axis=0)

    gain_size = model // (2 * chips)
    early = packed([grad_router, for_ranks(grad_second_gain)], F32)
    router_size = model // devices * EXPERTS
    grad_router = early[:router_size].reshape(-1, EXPERTS)
    grad_second_gain = early[router_size : router_size + gain_size]
    late = packed([grad_latent_down, for_ranks(grad_first_gain), grad_latent_gain], BF)
    down_size = model // devices * (KVL + RD)
    latent_size = KVL // devices

    def scattered(array, dimension):
        return lax.psum_scatter(
            array.astype(BF), DP, scatter_dimension=dimension, tiled=True
        ).astype(F32)

    def routed_of(array):
        return array[:routed_rows].reshape(EXPERTS, unit, half)

    return (
        result,
        token_grad,
        late[down_size : down_size + gain_size],
        scattered(grad_query, 0),
        late[:down_size].reshape(-1, KVL + RD),
        late[down_size + gain_size : down_size + gain_size + latent_size],
        scattered(grad_latent_up, 0),
        scattered(grad_output, 1),
        grad_second_gain,
        grad_router,
        jnp.swapaxes(routed_of(grads[0]), 1, 2),
        jnp.swapaxes(routed_of(grads[1]), 1, 2),
        routed_of(grads[2]),
        grads[0][routed_rows:].T,
        grads[1][routed_rows:].T,
        grads[2][routed_rows:],
    )


def solution(mesh):
    groups, ranks = mesh.devices.shape
    fine = Mesh(mesh.devices.reshape(groups // 2, 2, ranks), ("dpo", "core", "tensor"))
    in_specs = (
        P(DP, None),
        P(DP, None),
        P(),
        P(DP, None),
        P(),
        P(None, "tensor"),
        P(),
        P(),
        P(None, "tensor"),
        P("tensor", None),
        P(),
        P(),
        P(None, None, "tensor"),
        P(None, None, "tensor"),
        P(None, "tensor", None),
        P(None, "tensor"),
        P(None, "tensor"),
        P("tensor", None),
    )
    out_specs = (
        P(DP, None),
        P(DP, None),
        P(DP),
        P(DP, "tensor"),
        P(ALL, None),
        P(ALL),
        P(DP, "tensor"),
        P("tensor", DP),
        P(DP),
        P(ALL, None),
        P(None, DP, "tensor"),
        P(None, DP, "tensor"),
        P(None, "tensor", DP),
        P(DP, "tensor"),
        P(DP, "tensor"),
        P("tensor", DP),
    )
    return jax.shard_map(shards, mesh=fine, in_specs=in_specs, out_specs=out_specs, check_vma=False)
```

```python
import jax
import jax.numpy as jnp
from jax import lax
from jax.experimental import pallas as pl
from jax.experimental.pallas import tpu as pltpu
from jax.sharding import Mesh
from jax.sharding import PartitionSpec as P

ND = 128
RD = 64
VD = 128
KVL = 512
EXPERTS = 12
LAT = 640
EPSILON = 1e-06
LOG2E = 1.4426950408889634
BF = jnp.bfloat16
F32 = jnp.float32
VMEM_LIMIT = 60 * 1024 * 1024
DP = ("dpo", "core")
ALL = ("dpo", "core", "tensor")
MESH = pl.DeviceIdType.MESH
SHORT = pl.CostEstimate(flops=1000, bytes_accessed=100_000, transcendentals=0)


def nn(former, latter):
    return jnp.dot(former, latter, preferred_element_type=F32)


def nt(former, latter):
    return lax.dot_general(former, latter, (((1,), (1,)), ((), ())), preferred_element_type=F32)


def tn(former, latter):
    return lax.dot_general(former, latter, (((0,), (0,)), ((), ())), preferred_element_type=F32)


def rotary_tables(places):
    halfway = RD // 2
    frequency = 10000.0 ** (-jnp.arange(halfway, dtype=F32) * 2.0 / RD)
    angles = places.astype(F32)[:, None] * frequency[None, :]
    return jnp.cos(angles), jnp.sin(angles)


def rotate(values, cosine, sine_table):
    halfway = values.shape[-1] // 2
    leading = values[..., :halfway]
    trailing = values[..., halfway:]
    return jnp.concatenate(
        [leading * cosine - trailing * sine_table, trailing * cosine + leading * sine_table],
        axis=-1,
    )


def norm_rows(values, gain_row):
    factor = lax.rsqrt(jnp.mean(values * values, axis=-1, keepdims=True) + EPSILON)
    return values * factor * gain_row, factor


def norm_back(values, factor, gain_row, upstream):
    weighted = upstream * gain_row
    common = jnp.mean(weighted * values, axis=-1, keepdims=True)
    return (
        factor * weighted - values * factor * factor * factor * common,
        jnp.sum(upstream * values * factor, axis=0),
    )


def expert_unit(gate_pre, up_pre, hidden_grad, gate):
    sigmoid = 0.5 * jnp.tanh(0.5 * gate_pre) + 0.5
    silu = gate_pre * sigmoid
    hidden = silu * up_pre
    scaled = gate * hidden_grad
    d_up = scaled * silu
    d_gate = scaled * up_pre * (sigmoid + silu - silu * sigmoid)
    return (
        (gate * hidden).astype(BF),
        d_gate.astype(BF),
        d_up.astype(BF),
        hidden * hidden_grad,
    )


def weight_copies(routed, shared, held, sems, step, slot, steps, width, begin):
    def each(refs):
        for i, ref in enumerate(refs):
            copy = pltpu.make_async_copy(
                ref, held.at[slot, pl.ds(i * width, width)], sems.at[slot, i]
            )
            if begin:
                copy.start()
            else:
                copy.wait()

    @pl.when(step < steps - 1)
    def _():
        rows = pl.ds(pl.multiple_of(step * width, width), width)
        each([ref.at[rows] for ref in routed])

    @pl.when(step == steps - 1)
    def _():
        each(shared)


def gate_rows(gates, width):
    parts, columns = gates.shape
    return jnp.concatenate(
        [jnp.broadcast_to(gates[i : i + 1], (width // parts, columns)) for i in range(parts)],
        axis=0,
    )


def own_experts(rows, upstream, gates, weights):
    count, model = upstream.shape
    steps, parts, _ = gates.shape
    width = weights[3].shape[0]
    unit = width // parts
    wide = 512

    def kernel(x_ref, c_ref, g_ref, gw, uw, dw, sg, su, sd, out_low, back, kept_h, kept_g, kept_u, dots, held, sems, out):
        step = pl.program_id(0)
        slot = lax.rem(step, 2)
        routed, shared = (gw, uw, dw), (sg, su, sd)

        @pl.when(step == 0)
        def _():
            weight_copies(routed, shared, held, sems, step, slot, steps, width, True)
            out[...] = jnp.zeros_like(out)
            back[...] = jnp.zeros_like(back)

        weight_copies(routed, shared, held, sems, step, slot, steps, width, False)

        @pl.when(step < steps - 1)
        def _():
            weight_copies(routed, shared, held, sems, step + 1, 1 - slot, steps, width, True)

        both = nt(held[slot, : 2 * width], x_ref[...])
        hidden_grad = nt(held[slot, 2 * width :], c_ref[...])
        hidden, d_gate, d_up, products = expert_unit(
            both[:width], both[width:], hidden_grad, gate_rows(g_ref[0], width)
        )
        kept_h[0] = hidden
        kept_g[0] = d_gate
        kept_u[0] = d_up
        dots[0] = jnp.concatenate(
            [
                jnp.sum(products[i * unit : (i + 1) * unit], axis=0, keepdims=True)
                for i in range(parts)
            ],
            axis=0,
        )
        turned = hidden.T
        turned_back = jnp.concatenate([d_gate, d_up], axis=0).T
        for at in range(0, model, wide):
            columns = slice(at, at + wide)
            out[:, columns] += nn(turned, held[slot, 2 * width :, columns])
            back[:, columns] += nn(turned_back, held[slot, : 2 * width, columns])

        @pl.when(step == steps - 1)
        def _():
            out_low[...] = out[...].astype(BF)

    def whole(shape):
        return pl.BlockSpec(shape, lambda p: (0,) * len(shape), pipeline_mode=pl.Buffered(1))

    def one(shape):
        return pl.BlockSpec((1,) + shape, lambda p: (p, 0, 0))

    kept = jax.ShapeDtypeStruct((steps, width, count), BF)
    total = jax.ShapeDtypeStruct((count, model), F32)
    return pl.pallas_call(
        kernel,
        name="own_experts",
        grid=(steps,),
        in_specs=[whole((count, model)), whole((count, model)), one((parts, count))]
        + [pl.BlockSpec(memory_space=pl.ANY)] * 6,
        out_specs=[whole((count, model))] * 2 + [one((width, count))] * 3 + [one((parts, count))],
        out_shape=[jax.ShapeDtypeStruct((count, model), BF), total, kept, kept, kept, jax.ShapeDtypeStruct((steps, parts, count), F32)],
        scratch_shapes=[
            pltpu.VMEM((2, 3 * width, model), BF),
            pltpu.SemaphoreType.DMA((2, 3)),
            pltpu.VMEM((count, model), F32),
        ],
        cost_estimate=SHORT,
        compiler_params=pltpu.CompilerParams(
            vmem_limit_bytes=VMEM_LIMIT, dimension_semantics=("arbitrary",)
        ),
    )(rows, upstream, gates, *weights)


def ring_of(axis):
    here = lax.axis_index(axis)
    size = lax.axis_size(axis)
    return here, [lax.rem(here + i, size) for i in range(size)]


def greet(friends):
    barrier = pltpu.get_barrier_semaphore()
    total = 0
    for device, present in friends.values():
        if present is None:
            pl.semaphore_signal(barrier, inc=1, device_id=device, device_id_type=MESH)
            total = total + 1
            continue

        @pl.when(present)
        def _():
            pl.semaphore_signal(barrier, inc=1, device_id=device, device_id_type=MESH)

        total = total + jnp.where(present, 1, 0)
    pl.semaphore_wait(barrier, total)


def mate_friend():
    return {"mate": ({"core": 1 - lax.axis_index("core")}, None)}


def rank_friends():
    _, peers = ring_of("tensor")
    return {f"rank{d}": ({"tensor": peer}, None) for d, peer in enumerate(peers) if d}


def line_friends():
    chip, chips = lax.axis_index("dpo"), lax.axis_size("dpo")
    return {
        "left": ({"dpo": lax.rem(chip + chips - 1, chips)}, chip > 0),
        "right": ({"dpo": lax.rem(chip + 1, chips)}, chip < chips - 1),
    }


def remote(source, target, send, receive, device):
    return pltpu.make_async_remote_copy(
        src_ref=source, dst_ref=target, send_sem=send, recv_sem=receive,
        device_id=device, device_id_type=MESH,
    )


class Scatter:
    def __init__(self, rows):
        ranks = lax.axis_size("tensor")
        quarter = rows.shape[0] // ranks
        self.ins = [rows.reshape(ranks, quarter, rows.shape[1])]
        self.in_specs = [pl.BlockSpec(memory_space=pl.ANY)]
        self.outs = [jax.ShapeDtypeStruct((ranks - 1, quarter, rows.shape[1]), rows.dtype)]
        self.out_specs = [pl.BlockSpec(memory_space=pl.ANY)]
        self.scratch = [pltpu.SemaphoreType.DMA((ranks,)), pltpu.SemaphoreType.DMA((ranks,))]

    def copies(self, refs):
        source, target, sends, receives = refs
        _, peers = ring_of("tensor")
        return [
            remote(source.at[peer], target.at[d - 1], sends.at[d], receives.at[d], {"tensor": peer})
            for d, peer in enumerate(peers)
            if d
        ]

    def friends(self):
        return rank_friends()

    def begin(self, refs):
        for copy in self.copies(refs):
            copy.start()

    def middle(self, refs, step, last):
        pass

    def end(self, refs):
        for copy in self.copies(refs):
            copy.wait()


class Gather(Scatter):
    def __init__(self, rows):
        ranks = lax.axis_size("tensor")
        self.ins = [rows]
        self.in_specs = [pl.BlockSpec(memory_space=pl.ANY)]
        self.outs = [jax.ShapeDtypeStruct((ranks,) + rows.shape, rows.dtype)]
        self.out_specs = [pl.BlockSpec(memory_space=pl.ANY)]
        self.scratch = [pltpu.SemaphoreType.DMA((ranks,)), pltpu.SemaphoreType.DMA((ranks,))]

    def copies(self, refs):
        source, target, sends, receives = refs
        rank, peers = ring_of("tensor")
        return [pltpu.make_async_copy(source, target.at[rank], sends.at[0])] + [
            remote(source, target.at[rank], sends.at[d], receives.at[d], {"tensor": peer})
            for d, peer in enumerate(peers)
            if d
        ]


class Many(Scatter):
    def __init__(self, transfers):
        self.transfers = transfers
        self.ins = [x for t in transfers for x in t.ins]
        self.in_specs = [x for t in transfers for x in t.in_specs]
        self.outs = [x for t in transfers for x in t.outs]
        self.out_specs = [x for t in transfers for x in t.out_specs]
        self.scratch = [x for t in transfers for x in t.scratch]

    def copies(self, refs):
        n = len(self.transfers)
        copies = []
        for i, t in enumerate(self.transfers):
            own = [refs[i], refs[n + i], refs[2 * n + 2 * i], refs[2 * n + 2 * i + 1]]
            copies += t.copies(own)
        return copies


class LineSum:
    def __init__(self, blocks):
        chips = lax.axis_size("dpo")
        self.chips = chips
        shape = blocks.shape[1:]
        self.ins = [blocks]
        self.in_specs = [pl.BlockSpec(memory_space=pl.ANY)]
        self.outs = [jax.ShapeDtypeStruct(shape, F32)]
        self.out_specs = [pl.BlockSpec(shape, lambda *_: (0, 0), pipeline_mode=pl.Buffered(1))]
        self.scratch = [
            pltpu.VMEM((chips,) + shape, blocks.dtype),
            pltpu.VMEM((chips,) + shape, blocks.dtype),
            pltpu.VMEM(shape, blocks.dtype),
        ] + [pltpu.SemaphoreType.DMA((chips,))] * 4 + [pltpu.SemaphoreType.DMA]

    def swap(self, refs, i):
        source, _, mate, _, _, sends, receives, _, _, _ = refs
        core = lax.axis_index("core")
        return remote(source.at[2 * i + 1 - core], mate.at[i], sends.at[i], receives.at[i], {"core": 1 - core})

    def onward(self, refs, i):
        _, _, mate, inbox, _, _, _, sends, receives, _ = refs
        chip = lax.axis_index("dpo")
        return remote(mate.at[i], inbox.at[i], sends.at[i], receives.at[i], {"dpo": lax.rem(chip + self.chips - 1, self.chips)})

    def friends(self):
        return line_friends()

    def begin(self, refs):
        chip = lax.axis_index("dpo")
        for i in range(self.chips):
            @pl.when(i <= chip)
            def _():
                self.swap(refs, i).start()

    def middle(self, refs, step, last):
        source, out, mate, inbox, mine, _, _, _, _, sem = refs
        chip, core = lax.axis_index("dpo"), lax.axis_index("core")
        for i in range(self.chips):
            due = jnp.minimum(1 + 3 * (self.chips - 1 - chip) + i, last)

            @pl.when((i <= chip) & (step == due))
            def _():
                local = pltpu.make_async_copy(source.at[2 * i + core], mine, sem)
                local.start()
                self.swap(refs, i).wait()
                local.wait()

                @pl.when(chip < self.chips - 1)
                def _():
                    self.onward(refs, i).wait_recv()
                    mate[i] = (
                        mate[i].astype(F32) + mine[...].astype(F32) + inbox[i].astype(F32)
                    ).astype(mate.dtype)

                @pl.when(chip == self.chips - 1)
                def _():
                    mate[i] = (mate[i].astype(F32) + mine[...].astype(F32)).astype(mate.dtype)

                @pl.when(chip > i)
                def _():
                    self.onward(refs, i).start()

                @pl.when(chip == i)
                def _():
                    out[...] = mate[i].astype(F32)

    def end(self, refs):
        chip = lax.axis_index("dpo")
        for i in range(self.chips):
            @pl.when(chip > i)
            def _():
                self.onward(refs, i).wait_send()


class LineSpread(LineSum):
    def __init__(self, arrays):
        chips = lax.axis_size("dpo")
        self.chips = chips
        self.dimensions = [d for _, d in arrays]
        self.shapes = [
            tuple(n // (2 * chips) if i == d else n for i, n in enumerate(a.shape)) for a, d in arrays
        ]
        n = len(arrays)
        self.ins = [a for a, _ in arrays]
        self.in_specs = [pl.BlockSpec(memory_space=pl.ANY)] * n
        self.outs = [jax.ShapeDtypeStruct(shape, F32) for shape in self.shapes]
        self.out_specs = [
            pl.BlockSpec(shape, lambda *_: (0, 0), pipeline_mode=pl.Buffered(1)) for shape in self.shapes
        ]
        self.scratch = []
        for shape in self.shapes:
            self.scratch += [
                pltpu.VMEM((chips,) + shape, BF),
                pltpu.VMEM((chips + 1,) + shape, BF),
                pltpu.VMEM(shape, BF),
            ]
        self.scratch += [
            pltpu.SemaphoreType.DMA((n, chips)),
            pltpu.SemaphoreType.DMA((n, chips)),
            pltpu.SemaphoreType.DMA((n, chips)),
            pltpu.SemaphoreType.DMA((n, chips + 1)),
            pltpu.SemaphoreType.DMA((n,)),
        ]

    def parts(self, refs):
        n = len(self.shapes)
        buffers = refs[2 * n : 5 * n]
        return [(refs[j], refs[n + j]) + tuple(buffers[3 * j : 3 * j + 3]) for j in range(n)], refs[5 * n :]

    def block(self, j, source, place):
        size = self.shapes[j][self.dimensions[j]]
        part = pl.ds(pl.multiple_of(place * size, size), size)
        return source.at[part] if self.dimensions[j] == 0 else source.at[:, part]

    def swaps(self, refs, i):
        parts, sems = self.parts(refs)
        core = lax.axis_index("core")
        return [
            remote(
                self.block(j, source, 2 * i + 1 - core), mate.at[i], sems[0].at[j, i], sems[1].at[j, i],
                {"core": 1 - core},
            )
            for j, (source, _, mate, _, _) in enumerate(parts)
        ]

    def onwards(self, refs, i, slot, step):
        parts, sems = self.parts(refs)
        chip = lax.axis_index("dpo")
        to = lax.rem(chip + step + self.chips, self.chips)
        return [
            remote(mate.at[i], inbox.at[slot], sems[2].at[j, i], sems[3].at[j, slot], {"dpo": to})
            for j, (_, _, mate, inbox, _) in enumerate(parts)
        ]

    def begin(self, refs):
        for i in range(self.chips):
            for copy in self.swaps(refs, i):
                copy.start()

    def middle(self, refs, step, last):
        chip, core = lax.axis_index("dpo"), lax.axis_index("core")
        parts, sems = self.parts(refs)
        end = self.chips - 1

        def arrive(i, slot):
            for copy in self.onwards(refs, i, slot, 0):
                copy.wait_recv()
            for _, _, mate, inbox, _ in parts:
                mate[i] = (mate[i].astype(F32) + inbox[slot].astype(F32)).astype(BF)

        for i in range(self.chips):
            due = jnp.minimum(1 + 3 * (end - jnp.abs(chip - i)), last)

            @pl.when(step == due)
            def _():
                locals_ = [
                    pltpu.make_async_copy(self.block(j, source, 2 * i + core), mine, sems[4].at[j])
                    for j, (source, _, _, _, mine) in enumerate(parts)
                ]
                for copy in locals_:
                    copy.start()
                for copy in self.swaps(refs, i) + locals_:
                    copy.wait()
                for _, _, mate, _, mine in parts:
                    mate[i] = (mate[i].astype(F32) + mine[...].astype(F32)).astype(BF)

                @pl.when((i <= chip) & (chip < end))
                def _():
                    arrive(i, i)

                @pl.when((i > chip) & (chip > 0))
                def _():
                    arrive(i, i)

                @pl.when((i == chip) & (chip > 0))
                def _():
                    arrive(i, self.chips)

                @pl.when(i < chip)
                def _():
                    for copy in self.onwards(refs, i, i, -1):
                        copy.start()

                @pl.when(i == chip + 1)
                def _():
                    for copy in self.onwards(refs, i, self.chips, 1):
                        copy.start()

                @pl.when(i > chip + 1)
                def _():
                    for copy in self.onwards(refs, i, i, 1):
                        copy.start()

                @pl.when(i == chip)
                def _():
                    for _, out, mate, _, _ in parts:
                        out[...] = mate[i].astype(F32)

    def end(self, refs):
        chip = lax.axis_index("dpo")
        for i in range(self.chips):
            @pl.when(chip != i)
            def _():
                for copy in self.onwards(refs, i, i, 0):
                    copy.wait_send()


class Beside:
    def __init__(self, former, latter):
        self.pair = (former, latter)
        self.ins = former.ins + latter.ins
        self.in_specs = former.in_specs + latter.in_specs
        self.outs = former.outs + latter.outs
        self.out_specs = former.out_specs + latter.out_specs
        self.scratch = former.scratch + latter.scratch

    def split(self, refs):
        refs = list(refs)
        lists = ([], [])
        for name in ("ins", "outs", "scratch"):
            for t, held in zip(self.pair, lists):
                n = len(getattr(t, name))
                held += refs[:n]
                del refs[:n]
        return zip(self.pair, lists)

    def friends(self):
        return {**self.pair[0].friends(), **self.pair[1].friends()}

    def begin(self, refs):
        for t, held in self.split(refs):
            t.begin(held)

    def middle(self, refs, step, last):
        for t, held in self.split(refs):
            t.middle(held, step, last)

    def end(self, refs):
        for t, held in self.split(refs):
            t.end(held)


def settle(part, more, finish, extra, wide, collective):
    count, model = part.shape
    ranks = lax.axis_size("tensor")
    quarter = count // ranks
    n_more, n_extra = len(more), len(extra)

    def kernel(*refs):
        part_ref = refs[0]
        more_refs = refs[1 : 1 + n_more]
        out_ref = refs[1 + n_more]
        extra_refs = refs[2 + n_more : 2 + n_more + n_extra]
        inbox, block, gathered, send, receive, send_on, receive_on = refs[2 + n_more + n_extra :]
        rank, peers = ring_of("tensor")

        def rows_of(i):
            return pl.ds(pl.multiple_of(i * quarter, quarter), quarter)

        greet(rank_friends())
        copies = [
            remote(part_ref.at[rows_of(peer)], inbox.at[d], send.at[d], receive.at[d], {"tensor": peer})
            for d, peer in enumerate(peers)
            if d
        ]
        for copy in copies:
            copy.start()
        total = part_ref[rows_of(rank)].astype(F32)
        for d, copy in enumerate(copies):
            copy.wait()
            total = total + inbox[d + 1].astype(F32)
        results = finish(total, [r[...] for r in more_refs])
        for ref, value in zip(extra_refs, results):
            ref[...] = value
        block[...] = results[-1]
        copies = [
            remote(block, gathered.at[d], send_on.at[d], receive_on.at[d], {"tensor": peer})
            for d, peer in enumerate(peers)
            if d
        ]
        for copy in copies:
            copy.start()
        out_ref[rows_of(rank)] = block[...]
        for d, copy in enumerate(copies):
            copy.wait()
            out_ref[rows_of(lax.rem(rank + ranks - d - 1, ranks))] = gathered[d + 1]

    vmem = pl.BlockSpec(memory_space=pltpu.VMEM)
    sems = [pltpu.SemaphoreType.DMA((ranks,))] * 4
    return pl.pallas_call(
        kernel,
        name="settle",
        in_specs=[vmem] * (1 + n_more),
        out_specs=[vmem] * (1 + n_extra),
        out_shape=[jax.ShapeDtypeStruct((count, wide), BF)] + extra,
        scratch_shapes=[
            pltpu.VMEM((ranks, quarter, model), BF),
            pltpu.VMEM((quarter, wide), BF),
            pltpu.VMEM((ranks, quarter, wide), BF),
        ]
        + sems,
        cost_estimate=SHORT,
        compiler_params=pltpu.CompilerParams(
            vmem_limit_bytes=VMEM_LIMIT, collective_id=collective, has_side_effects=True
        ),
    )(part, *more)


def group_gradients(rows, upstream, row_cols, up_cols, gates, kept, weights, first, groups, held_back, beside, collective):
    chips, count, model = upstream.shape
    steps, _, parts, _ = gates.shape
    width = weights[3].shape[0]
    half = row_cols.shape[2] // 2
    unit = width // 2
    n_ins, n_outs, n_held = len(beside.ins), len(beside.outs), len(held_back)
    last = groups * chips - 1
    ends = first + groups == steps

    def kernel(*refs):
        refs = list(refs)

        def take(n):
            taken = refs[:n]
            del refs[:n]
            return taken

        x_ref, c_ref, xc, cc, g_ref, kept_h, kept_g, kept_u = take(8)
        routed, shared = take(3), take(3)
        take(n_held)
        link_refs = take(n_ins)
        outs = take(3)
        shared_outs = take(3) if ends else None
        link_refs += take(n_outs)
        held, sems, sum_g, sum_u, sum_d, outbox, inbox, sends, receives = take(9)
        link_refs += refs
        at_group = pl.program_id(0)
        turn = pl.program_id(1)
        step = at_group + first
        slot = lax.rem(at_group, 2)
        tick = at_group * chips + turn
        sums = (sum_g, sum_u, sum_d)

        def swap(i):
            part = pl.ds(i * unit, unit)
            return remote(
                outbox.at[:, part], inbox.at[slot, :, part], sends.at[slot, i], receives.at[slot, i],
                {"core": 1 - lax.axis_index("core")},
            )

        @pl.when(tick == 0)
        def _():
            greet({**mate_friend(), **beside.friends()})
            beside.begin(link_refs)

        @pl.when(turn == 0)
        def _():
            @pl.when(at_group == 0)
            def _():
                weight_copies(routed, shared, held, sems, step, slot, steps, width, True)

            sum_g[...] = nn(kept_g[0], xc[0])
            sum_u[...] = nn(kept_u[0], xc[0])
            sum_d[...] = nn(kept_h[0], cc[0])
            weight_copies(routed, shared, held, sems, step, slot, steps, width, False)

            @pl.when(at_group < groups - 1)
            def _():
                weight_copies(routed, shared, held, sems, step + 1, 1 - slot, steps, width, True)

        def work(final):
            x = x_ref[0]
            c = c_ref[0]
            gate = gate_rows(g_ref[0, 0], width)
            for i in range(2):
                at = i * unit
                part = slice(at, at + unit)
                gate_pre = nt(held[slot, at : at + unit], x)
                up_pre = nt(held[slot, width + at : width + at + unit], x)
                hidden_grad = nt(held[slot, 2 * width + at : 2 * width + at + unit], c)
                hidden, d_gate, d_up, _ = expert_unit(gate_pre, up_pre, hidden_grad, gate[part])
                sum_g[part] += nn(d_gate, xc[0])
                sum_u[part] += nn(d_up, xc[0])
                sum_d[part] += nn(hidden, cc[0])
                if final:
                    for j, total in enumerate(sums):
                        outbox[j, part] = total[part, half:].astype(BF)
                    swap(i).start()

        @pl.when((turn > 0) & (turn < chips - 1))
        def _():
            work(False)

        @pl.when(turn == chips - 1)
        def _():
            work(True)
            for i in range(2):
                swap(i).wait()
                part = slice(i * unit, (i + 1) * unit)
                for j, total in enumerate(sums):
                    value = (total[part, :half] + inbox[slot, j, part].astype(F32)).astype(BF)
                    if not ends:
                        outs[j][part] = value
                        continue

                    @pl.when(step < steps - 1)
                    def _():
                        outs[j][part] = value

                    @pl.when(step == steps - 1)
                    def _():
                        shared_outs[j][part] = value

        beside.middle(link_refs, tick, last)

        @pl.when(tick == last)
        def _():
            beside.end(link_refs)

    def chip_at(turn):
        return lax.rem(lax.axis_index("dpo") + turn, chips)

    def at_chip(shape):
        return pl.BlockSpec((1,) + shape, lambda p, k: (chip_at(k), 0, 0))

    def one(shape):
        return pl.BlockSpec((1,) + shape, lambda p, k: (p + first, 0, 0))

    anywhere = pl.BlockSpec(memory_space=pl.ANY)
    block = pl.BlockSpec((width, half), lambda p, k: (jnp.minimum(p + first, steps - 2), 0))
    shared_block = pl.BlockSpec((width, half), lambda p, k: (0, 0))
    return pl.pallas_call(
        kernel,
        name="group_gradients",
        grid_spec=pltpu.PrefetchScalarGridSpec(
            num_scalar_prefetch=0,
            grid=(groups, chips),
            in_specs=[at_chip((count, model))] * 2
            + [at_chip((count, 2 * half))] * 2
            + [pl.BlockSpec((1, 1, parts, count), lambda p, k: (p + first, chip_at(k), 0, 0))]
            + [one((width, count))] * 3
            + [anywhere] * (6 + n_held)
            + beside.in_specs,
            out_specs=[block] * 3 + ([shared_block] * 3 if ends else []) + beside.out_specs,
            scratch_shapes=[
                pltpu.VMEM((2, 3 * width, model), BF),
                pltpu.SemaphoreType.DMA((2, 3)),
            ]
            + [pltpu.VMEM((width, 2 * half), F32)] * 3
            + [
                pltpu.VMEM((3, width, half), BF),
                pltpu.VMEM((2, 3, width, half), BF),
                pltpu.SemaphoreType.DMA((2, 2)),
                pltpu.SemaphoreType.DMA((2, 2)),
            ]
            + beside.scratch,
        ),
        out_shape=[jax.ShapeDtypeStruct(((steps - 1) * width, half), BF)] * 3
        + ([jax.ShapeDtypeStruct((width, half), BF)] * 3 if ends else [])
        + beside.outs,
        input_output_aliases={14 + i: i for i in range(n_held)},
        cost_estimate=pl.CostEstimate(
            flops=groups * 2 * width * count * (3 * (chips - 1) * model + 6 * chips * half),
            bytes_accessed=groups * (6 * width * model + 4 * chips * count * model),
            transcendentals=0,
        ),
        compiler_params=pltpu.CompilerParams(
            vmem_limit_bytes=VMEM_LIMIT,
            dimension_semantics=("arbitrary", "arbitrary"),
            collective_id=collective,
            has_side_effects=True,
        ),
    )(
        rows, upstream, row_cols, up_cols, gates, *kept, *weights, *held_back, *beside.ins,
    )


def attention_forward(queries, latent, latent_up, key_ids, query_ids, collective):
    count = queries.shape[0]
    heads = queries.shape[1] // 256
    chips = lax.axis_size("dpo")
    scale = (ND + RD) ** (-0.5) * LOG2E

    def kernel(q_ref, lat_ref, up_ref, kid_ref, qid_ref, att_ref, lse_ref, all_ref, keys, top, low, mix,
               local, send_right, take_left, send_mate, take_mate):
        chip, core = lax.axis_index("dpo"), lax.axis_index("core")
        place = chip * 2 + core
        right = lax.rem(chip + 1, chips)
        greet({**mate_friend(), **line_friends()})

        def to_right(source, i):
            return remote(source, all_ref.at[2 * i + core], send_right.at[i], take_left.at[i], {"dpo": right})

        def to_mate(source, i):
            return remote(source, all_ref.at[2 * i + core], send_mate.at[i], take_mate.at[i], {"core": 1 - core})

        @pl.when(chip < chips - 1)
        def _():
            to_right(lat_ref, chip).start()

        to_mate(lat_ref, chip).start()
        keep = pltpu.make_async_copy(lat_ref, all_ref.at[place], local)
        keep.start()
        top[...] = jnp.full_like(top, -1e30)
        low[...] = jnp.zeros_like(low)
        mix[...] = jnp.zeros_like(mix)

        def chunk(source, masked):
            lat = source[:, :KVL]
            rope = source[:, KVL:]
            for h in range(heads):
                keys[h, :, ND:] = rope
                both = nn(lat, up_ref[:, h * 256 : (h + 1) * 256]).astype(BF)
                keys[h, :, :ND] = both[:, :ND]
                values = both[:, ND:].T
                scores = nt(keys[h], q_ref[:, h * 256 : (h + 1) * 256]) * scale
                if masked:
                    scores = jnp.where(kid_ref[...] <= qid_ref[...], scores, -1e30)
                before = top[h]
                highest = jnp.maximum(before, jnp.max(scores, axis=0, keepdims=True))
                weights = jnp.exp2(scores - highest)
                decay = jnp.exp2(before - highest)
                top[h] = highest
                low[h] = low[h] * decay + jnp.sum(weights, axis=0, keepdims=True)
                mix[h] = mix[h] * decay + nn(values, weights.astype(BF))

        chunk(lat_ref, True)
        keep.wait()
        to_mate(lat_ref, chip).wait()

        @pl.when(core == 1)
        def _():
            chunk(all_ref.at[place - 1], False)

        def earlier(i, carry):
            at = chip - 1 - i
            arrived = all_ref.at[2 * at + core]
            to_right(arrived, at).wait_recv()

            @pl.when(chip < chips - 1)
            def _():
                to_right(arrived, at).start()

            to_mate(arrived, at).start()
            chunk(arrived, False)
            to_mate(arrived, at).wait_recv()
            chunk(all_ref.at[2 * at + 1 - core], False)
            return carry

        lax.fori_loop(0, chip, earlier, 0)
        for h in range(heads):
            att_ref[:, h * VD : (h + 1) * VD] = (mix[h] / low[h]).T.astype(BF)
            lse_ref[h] = top[h] + jnp.log2(low[h])

        def sent(i, carry):
            to_mate(lat_ref, i).wait_send()
            return carry

        lax.fori_loop(0, chip, sent, 0)

        @pl.when(chip < chips - 1)
        def _():
            def sent_right(i, carry):
                to_right(lat_ref, i).wait_send()
                return carry

            lax.fori_loop(0, chip + 1, sent_right, 0)

    vmem = pl.BlockSpec(memory_space=pltpu.VMEM)
    sems = pltpu.SemaphoreType.DMA((chips,))
    return pl.pallas_call(
        kernel,
        name="attention_forward",
        in_specs=[vmem] * 5,
        out_specs=[vmem] * 3,
        out_shape=[
            jax.ShapeDtypeStruct((count, heads * VD), BF),
            jax.ShapeDtypeStruct((heads, 1, count), F32),
            jax.ShapeDtypeStruct((2 * chips, count, LAT), BF),
        ],
        scratch_shapes=[
            pltpu.VMEM((heads, count, 256), BF),
            pltpu.VMEM((heads, 1, count), F32),
            pltpu.VMEM((heads, 1, count), F32),
            pltpu.VMEM((heads, VD, count), F32),
            pltpu.SemaphoreType.DMA,
            sems,
            sems,
            sems,
            sems,
        ],
        cost_estimate=SHORT,
        compiler_params=pltpu.CompilerParams(
            vmem_limit_bytes=VMEM_LIMIT, collective_id=collective, has_side_effects=True
        ),
    )(queries, latent, latent_up, key_ids, query_ids)


def attention_backward(place, queries, latents, latent_up, key_ids, query_ids, mix_grad, lse, delta):
    count = queries.shape[0]
    heads = queries.shape[1] // 256
    total = latents.shape[0]
    factor = (ND + RD) ** (-0.5)
    scale = factor * LOG2E

    def kernel(place_ref, q_ref, lat_ref, up_ref, kid_ref, qid_ref, do_ref, lse_ref, delta_ref,
               dq_ref, dup_ref, dlat_ref, keys, dq, dlat):
        dq[...] = jnp.zeros_like(dq)
        dup_ref[...] = jnp.zeros_like(dup_ref)

        def chunk(at, masked):
            rows = pl.ds(pl.multiple_of(at * count, count), count)
            lat = lat_ref[rows, :KVL]
            turned = lat.T
            rope = lat_ref[rows, KVL:]
            dlat[...] = jnp.zeros_like(dlat)
            for h in range(heads):
                up = up_ref[:, h * 256 : (h + 1) * 256]
                query = q_ref[:, h * 256 : (h + 1) * 256]
                upstream = do_ref[:, h * VD : (h + 1) * VD]
                keys[h, :, ND:] = rope
                both = nn(lat, up).astype(BF)
                keys[h, :, :ND] = both[:, :ND]
                scores = nt(keys[h], query) * scale
                chances = jnp.exp2(scores - lse_ref[h])
                if masked:
                    chances = jnp.where(kid_ref[...] <= qid_ref[...], chances, 0.0)
                chance_grad = nt(both[:, ND:], upstream)
                score_grad = (chances * (chance_grad - delta_ref[h])).astype(BF)
                value_grad = nn(chances.astype(BF), upstream)
                key_grad = nn(score_grad, query) * factor
                dq[h] += nn(keys[h].T, score_grad)
                both_grad = jnp.concatenate([key_grad[:, :ND], value_grad], axis=1).astype(BF)
                dlat[:, :KVL] += nt(both_grad, up)
                dlat[:, KVL:] += key_grad[:, ND:]
                dup_ref[:, h * 256 : (h + 1) * 256] += nn(turned, both_grad)
            dlat_ref[rows, :] = dlat[...].astype(BF)

        place_at = place_ref[0]
        lax.fori_loop(0, place_at, lambda at, carry: (chunk(at, False), carry)[1], 0)
        chunk(place_at, True)

        def clear(at, carry):
            rows = pl.ds(pl.multiple_of(at * count, count), count)
            dlat_ref[rows, :] = jnp.zeros((count, LAT), BF)
            return carry

        lax.fori_loop(place_at + 1, total // count, clear, 0)
        for h in range(heads):
            dq_ref[:, h * 256 : (h + 1) * 256] = dq[h].T * factor

    def whole(shape):
        return pl.BlockSpec(shape, lambda i, z: (0,) * len(shape), pipeline_mode=pl.Buffered(1))

    ins = (queries, latents, latent_up, key_ids, query_ids, mix_grad, lse, delta)
    outs = [
        jax.ShapeDtypeStruct((count, heads * 256), F32),
        jax.ShapeDtypeStruct((KVL, heads * 256), F32),
        jax.ShapeDtypeStruct((total, LAT), BF),
    ]
    return pl.pallas_call(
        kernel,
        name="attention_backward",
        grid_spec=pltpu.PrefetchScalarGridSpec(
            num_scalar_prefetch=1,
            grid=(1,),
            in_specs=[whole(a.shape) for a in ins],
            out_specs=[whole(o.shape) for o in outs],
            scratch_shapes=[
                pltpu.VMEM((heads, count, 256), BF),
                pltpu.VMEM((heads, 256, count), F32),
                pltpu.VMEM((count, LAT), F32),
            ],
        ),
        out_shape=outs,
        cost_estimate=SHORT,
        compiler_params=pltpu.CompilerParams(
            vmem_limit_bytes=VMEM_LIMIT, dimension_semantics=("arbitrary",)
        ),
    )(place, *ins)


def router_of(rows, router_weight):
    logits = lax.dot_general(
        router_weight, rows, (((0,), (1,)), ((), ())), preferred_element_type=F32
    )
    return jax.nn.softmax(logits, axis=0)


def grouped(gates, steps):
    parts = EXPERTS // (steps - 1)
    gates = gates.reshape((steps - 1, parts) + gates.shape[1:])
    return jnp.concatenate([gates, jnp.ones((1,) + gates.shape[1:], F32)], axis=0)


def shards(
    tokens,
    cotangent,
    block_ids,
    routes,
    first_gain,
    query_weight,
    latent_down,
    latent_gain,
    latent_up,
    output_weight,
    second_gain,
    router_weight,
    gate_weight,
    up_weight,
    down_weight,
    shared_gate,
    shared_up,
    shared_down,
):
    count, model = tokens.shape
    key_count = block_ids.shape[0]
    heads = query_weight.shape[1] // (ND + RD)
    unit = gate_weight.shape[2]
    width = shared_down.shape[0]
    steps = EXPERTS * unit // width + 1
    chips = lax.axis_size("dpo")
    ranks = lax.axis_size("tensor")
    devices = chips * 2 * ranks
    chip, core, rank = lax.axis_index("dpo"), lax.axis_index("core"), lax.axis_index("tensor")
    place = chip * 2 + core
    quarter = count // ranks
    half = model // (2 * chips)
    routed_rows = EXPERTS * unit

    def mine(array):
        return lax.dynamic_slice_in_dim(array, rank * quarter, quarter, 0)

    weights = (
        jnp.swapaxes(gate_weight, 1, 2).reshape(routed_rows, model),
        jnp.swapaxes(up_weight, 1, 2).reshape(routed_rows, model),
        down_weight.reshape(routed_rows, model),
        shared_gate.T,
        shared_up.T,
        shared_down,
    )

    row_start = place * count
    cosine, sine_table = rotary_tables((row_start + jnp.arange(count, dtype=jnp.int32)) % key_count)
    own_blocks = lax.dynamic_slice_in_dim(block_ids, row_start, count, 0)
    rows_float = tokens.astype(F32)
    normed_first, first_factor = norm_rows(rows_float, first_gain)
    attention_input = normed_first.astype(BF)
    compressed = nn(attention_input, latent_down)
    latent_raw = compressed[:, :KVL]
    latent_float, latent_factor = norm_rows(latent_raw, latent_gain)
    key_rope = rotate(compressed[:, KVL:], cosine, sine_table)
    latent = jnp.concatenate(
        [latent_float, key_rope, jnp.zeros((count, LAT - KVL - RD), F32)], axis=1
    ).astype(BF)
    query_raw = nn(attention_input, query_weight).reshape(count, heads, ND + RD)
    queries = jnp.concatenate(
        [
            query_raw[..., :ND],
            rotate(query_raw[..., ND:], cosine[:, None], sine_table[:, None]),
            jnp.zeros((count, heads, 256 - ND - RD), F32),
        ],
        axis=-1,
    ).astype(BF).reshape(count, heads * 256)
    key_ids, query_ids = own_blocks[:, None], own_blocks[None, :]
    attended, lse, latents = attention_forward(
        queries, latent, latent_up, key_ids, query_ids, 1
    )
    latents = latents.reshape(key_count, LAT)

    attended, upstream = lax.optimization_barrier((attended, cotangent))
    all_upstream = lax.all_gather(upstream, "dpo", axis=0, tiled=True)

    named = jnp.any(
        routes[:, :, None] == jnp.arange(128, dtype=jnp.int32)[None, None, :], axis=1
    ).astype(F32)
    token_quarter = mine(tokens)

    def second_norm(total, more):
        rows, gain, router_columns, mask = more
        residual = rows.astype(F32) + total
        normed, _ = norm_rows(residual, gain)
        normed = normed.astype(BF)
        logits = nn(normed, router_columns)
        lane = lax.broadcasted_iota(jnp.int32, logits.shape, 1)
        logits = jnp.where(lane < EXPERTS, logits, -1e30)
        odds = jnp.exp(logits - jnp.max(logits, axis=1, keepdims=True))
        gates = mask * odds / jnp.sum(odds, axis=1, keepdims=True)
        return residual, jnp.concatenate([normed, gates.astype(BF)], axis=1)

    wide_input, residual = settle(
        nn(attended, output_weight).astype(BF),
        [
            token_quarter,
            second_gain[None],
            jnp.pad(router_weight, ((0, 0), (0, 128 - EXPERTS))),
            mine(named),
        ],
        second_norm,
        [jax.ShapeDtypeStruct((quarter, model), F32)],
        model + 128,
        2,
    )
    expert_input = wide_input[:, :model]
    all_input = lax.all_gather(wide_input, "dpo", axis=0, tiled=True)
    all_input = all_input.reshape(chips, count, model + 128)

    named = named[:, :EXPERTS].T
    router = router_of(expert_input, router_weight)
    own_gates = grouped(named * router, steps)
    expert_part, input_back, kept_h, kept_g, kept_u, dots = own_experts(
        wide_input, cotangent, own_gates, weights
    )
    pair_grad = named * dots[: steps - 1].reshape(EXPERTS, count)
    logit_grad = router * (pair_grad - jnp.sum(router * pair_grad, axis=0, keepdims=True))
    logit_low = logit_grad.astype(BF)
    input_back = (
        input_back
        + lax.dot_general(
            logit_low, router_weight, (((0,), (1,)), ((), ())), preferred_element_type=F32
        )
    ).astype(BF)

    def second_norm_back(total, more):
        rows, gain, upstream_rows = more
        factor = lax.rsqrt(jnp.mean(rows * rows, axis=-1, keepdims=True) + EPSILON)
        back, gain_grad = norm_back(rows, factor, gain, total)
        back = back + upstream_rows.astype(F32)
        return back, gain_grad[None], back.astype(BF)

    input_back, all_upstream = lax.optimization_barrier((input_back, all_upstream))
    output_grad, residual_grad, grad_second_gain = settle(
        input_back,
        [residual, second_gain[None], mine(cotangent)],
        second_norm_back,
        [
            jax.ShapeDtypeStruct((quarter, model), F32),
            jax.ShapeDtypeStruct((1, model), F32),
        ],
        model,
        3,
    )
    grad_second_gain = grad_second_gain[0]

    all_gates = grouped(
        jnp.transpose(all_input[:, :, model : model + EXPERTS].astype(F32), (2, 0, 1)), steps
    )
    all_gates = jnp.swapaxes(all_gates, 1, 2)

    def chip_columns(array):
        return jnp.concatenate(
            [
                lax.dynamic_slice_in_dim(array, (chip * 2 + c) * half, half, 2)
                for c in (core, 1 - core)
            ],
            axis=2,
        )

    all_upstream = all_upstream.reshape(chips, count, model)
    input_cols, upstream_cols = chip_columns(all_input), chip_columns(all_upstream)
    routed_grads = []

    def piece(first, groups, beside, collective):
        made = group_gradients(
            all_input, all_upstream, input_cols, upstream_cols, all_gates,
            (kept_h, kept_g, kept_u), weights, first, groups, routed_grads, beside, collective,
        )
        routed_grads[:] = made[:3]
        return made[3:]

    def summed(rows, got):
        return mine(rows).astype(F32) + jnp.sum(got.astype(F32), axis=0)

    attended_grad = nt(output_grad, output_weight).astype(BF)
    grad_output = tn(attended, output_grad).astype(BF)
    delta = jnp.sum(
        (attended.astype(F32) * attended_grad.astype(F32)).reshape(count, heads, VD), axis=2
    ).T[:, None, :]
    place_arg = place.reshape(1).astype(jnp.int32)
    query_back, grad_latent_up, latent_part = attention_backward(
        place_arg, queries, latents, latent_up, key_ids, query_ids, attended_grad, lse, delta
    )
    query_back = query_back.reshape(count, heads, 256)
    query_grad = jnp.concatenate(
        [
            query_back[..., :ND],
            rotate(query_back[..., ND : ND + RD], cosine[:, None], -sine_table[:, None]),
        ],
        axis=-1,
    ).astype(BF).reshape(count, heads * (ND + RD))
    grad_query = tn(attention_input, query_grad).astype(BF)
    query_part = nt(query_grad, query_weight)
    latent_part, grad_query, query_part = lax.optimization_barrier(
        (latent_part, grad_query, query_part)
    )
    (compressed_grad,) = piece(0, 2, LineSum(latent_part.reshape(2 * chips, count, LAT)), 5)
    latent_grad, grad_latent_gain = norm_back(
        latent_raw, latent_factor, latent_gain, compressed_grad[:, :KVL]
    )
    down_grad = jnp.concatenate(
        [latent_grad, rotate(compressed_grad[:, KVL : KVL + RD], cosine, -sine_table)], axis=1
    ).astype(BF)
    attention_grad = query_part + nt(down_grad, latent_down)
    grad_first_gain = jnp.sum(attention_grad * rows_float * first_factor, axis=0)
    attention_grad = attention_grad.astype(BF)
    grad_latent_down = lax.psum_scatter(
        tn(attention_input, down_grad).astype(BF), DP, scatter_dimension=0, tiled=True
    )
    grad_query, grad_latent_up, grad_output, got, got_result = piece(
        2,
        steps - 4,
        Beside(
            LineSpread([(grad_query, 0), (grad_latent_up.astype(BF), 0), (grad_output, 1)]),
            Many([Scatter(attention_grad), Scatter(expert_part)]),
        ),
        6,
    )
    token_back, _ = norm_back(
        token_quarter.astype(F32), mine(first_factor), first_gain, summed(attention_grad, got)
    )
    *shared_grads, token_grad, result = piece(
        steps - 2,
        2,
        Many(
            [
                Gather((token_back + residual_grad).astype(BF)),
                Gather((residual + summed(expert_part, got_result)).astype(BF)),
            ]
        ),
        7,
    )
    token_grad, result = token_grad.reshape(count, model), result.reshape(count, model)

    grad_router = lax.dot_general(
        expert_input, logit_low, (((0,), (1,)), ((), ())), preferred_element_type=F32
    )

    def over_ranks(array):
        blocks = array.reshape((ranks, -1) + array.shape[1:])

        def block(d):
            return lax.dynamic_index_in_dim(blocks, lax.rem(rank + d, ranks), 0, keepdims=False)

        total = block(0).astype(F32)
        for d in range(1, ranks):
            route = [(i, (i + d) % ranks) for i in range(ranks)]
            total = total + lax.ppermute(block(d), "tensor", route).astype(F32)
        return total

    def for_ranks(gain):
        return jnp.repeat(gain.reshape(2 * chips, -1), ranks, axis=0)

    small = jnp.concatenate(
        [
            grad_router.reshape(devices, -1),
            for_ranks(grad_second_gain),
            for_ranks(grad_first_gain),
            grad_latent_gain.reshape(devices, -1),
        ],
        axis=1,
    )
    small = jnp.pad(small, ((0, 0), (0, -small.shape[1] % 1024)))
    small = lax.psum_scatter(small.reshape(-1, 128), DP, scatter_dimension=0, tiled=True)
    small = over_ranks(small).reshape(-1)
    router_size = model // devices * EXPERTS
    gain_size = model // (2 * chips)
    latent_size = KVL // devices
    grad_router = small[:router_size].reshape(-1, EXPERTS)
    small = small[router_size:]

    def routed_of(array):
        return array.reshape(EXPERTS, unit, half).astype(F32)

    return (
        result,
        token_grad,
        small[gain_size : 2 * gain_size],
        grad_query,
        over_ranks(grad_latent_down),
        small[2 * gain_size : 2 * gain_size + latent_size],
        grad_latent_up,
        grad_output,
        small[:gain_size],
        grad_router,
        jnp.swapaxes(routed_of(routed_grads[0]), 1, 2),
        jnp.swapaxes(routed_of(routed_grads[1]), 1, 2),
        routed_of(routed_grads[2]),
        shared_grads[0].astype(F32).T,
        shared_grads[1].astype(F32).T,
        shared_grads[2].astype(F32),
    )


def solution(mesh):
    groups, ranks = mesh.devices.shape
    fine = Mesh(mesh.devices.reshape(groups // 2, 2, ranks), ("dpo", "core", "tensor"))
    in_specs = (
        P(DP, None),
        P(DP, None),
        P(),
        P(DP, None),
        P(),
        P(None, "tensor"),
        P(),
        P(),
        P(None, "tensor"),
        P("tensor", None),
        P(),
        P(),
        P(None, None, "tensor"),
        P(None, None, "tensor"),
        P(None, "tensor", None),
        P(None, "tensor"),
        P(None, "tensor"),
        P("tensor", None),
    )
    out_specs = (
        P(DP, None),
        P(DP, None),
        P(DP),
        P(DP, "tensor"),
        P(ALL, None),
        P(ALL),
        P(DP, "tensor"),
        P("tensor", DP),
        P(DP),
        P(ALL, None),
        P(None, DP, "tensor"),
        P(None, DP, "tensor"),
        P(None, "tensor", DP),
        P(DP, "tensor"),
        P(DP, "tensor"),
        P("tensor", DP),
    )
    return jax.shard_map(shards, mesh=fine, in_specs=in_specs, out_specs=out_specs, check_vma=False)
```

```python
import jax
import jax.numpy as jnp
from jax import lax
from jax.experimental import pallas as pl
from jax.experimental.pallas import tpu as pltpu
from jax.sharding import Mesh
from jax.sharding import PartitionSpec as P

ND = 128
RD = 64
VD = 128
KVL = 512
EXPERTS = 12
LAT = 640
EPSILON = 1e-06
LOG2E = 1.4426950408889634
BF = jnp.bfloat16
F32 = jnp.float32
VMEM_LIMIT = 60 * 1024 * 1024
DP = ("dpo", "core")
ALL = ("dpo", "core", "tensor")
MESH = pl.DeviceIdType.MESH
SHORT = pl.CostEstimate(flops=1000, bytes_accessed=100_000, transcendentals=0)


def nn(former, latter):
    return jnp.dot(former, latter, preferred_element_type=F32)


def nt(former, latter):
    return lax.dot_general(former, latter, (((1,), (1,)), ((), ())), preferred_element_type=F32)


def tn(former, latter):
    return lax.dot_general(former, latter, (((0,), (0,)), ((), ())), preferred_element_type=F32)


def rotary_tables(places):
    halfway = RD // 2
    frequency = 10000.0 ** (-jnp.arange(halfway, dtype=F32) * 2.0 / RD)
    angles = places.astype(F32)[:, None] * frequency[None, :]
    return jnp.cos(angles), jnp.sin(angles)


def rotate(values, cosine, sine_table):
    halfway = values.shape[-1] // 2
    leading = values[..., :halfway]
    trailing = values[..., halfway:]
    return jnp.concatenate(
        [leading * cosine - trailing * sine_table, trailing * cosine + leading * sine_table],
        axis=-1,
    )


def norm_rows(values, gain_row):
    factor = lax.rsqrt(jnp.mean(values * values, axis=-1, keepdims=True) + EPSILON)
    return values * factor * gain_row, factor


def norm_back(values, factor, gain_row, upstream):
    weighted = upstream * gain_row
    common = jnp.mean(weighted * values, axis=-1, keepdims=True)
    return (
        factor * weighted - values * factor * factor * factor * common,
        jnp.sum(upstream * values * factor, axis=0),
    )


def expert_unit(gate_pre, up_pre, hidden_grad, gate):
    sigmoid = 0.5 * jnp.tanh(0.5 * gate_pre) + 0.5
    silu = gate_pre * sigmoid
    hidden = silu * up_pre
    scaled = gate * hidden_grad
    d_up = scaled * silu
    d_gate = scaled * up_pre * (sigmoid + silu - silu * sigmoid)
    return (
        (gate * hidden).astype(BF),
        d_gate.astype(BF),
        d_up.astype(BF),
        hidden * hidden_grad,
    )


def weight_copies(routed, shared, held, sems, step, slot, steps, width, begin):
    def each(refs):
        for i, ref in enumerate(refs):
            copy = pltpu.make_async_copy(
                ref, held.at[slot, pl.ds(i * width, width)], sems.at[slot, i]
            )
            if begin:
                copy.start()
            else:
                copy.wait()

    @pl.when(step < steps - 1)
    def _():
        rows = pl.ds(pl.multiple_of(step * width, width), width)
        each([ref.at[rows] for ref in routed])

    @pl.when(step == steps - 1)
    def _():
        each(shared)


def gate_rows(gates, width):
    parts, columns = gates.shape
    return jnp.concatenate(
        [jnp.broadcast_to(gates[i : i + 1], (width // parts, columns)) for i in range(parts)],
        axis=0,
    )


def own_experts(rows, upstream, router_rows, weights):
    count, model = upstream.shape
    width = weights[3].shape[0]
    steps = weights[0].shape[0] // width + 1
    parts = EXPERTS // (steps - 1)
    unit = width // parts
    wide = 512

    def kernel(x_ref, tail_ref, c_ref, router_ref, gw, uw, dw, sg, su, sd, out_low, back_low, kept_h, kept_g, kept_u, lg_ref,
               held, sems, out, back, gates, router, dots):
        step = pl.program_id(0)
        slot = lax.rem(step, 2)
        routed, shared = (gw, uw, dw), (sg, su, sd)

        @pl.when(step == 0)
        def _():
            weight_copies(routed, shared, held, sems, step, slot, steps, width, True)
            out[...] = jnp.zeros_like(out)
            back[...] = jnp.zeros_like(back)
            tail = tail_ref[...].astype(F32).T
            for p in range(steps):
                gates[p] = tail[p * parts : (p + 1) * parts]
            router[...] = tail[16:32]

        weight_copies(routed, shared, held, sems, step, slot, steps, width, False)

        @pl.when(step < steps - 1)
        def _():
            weight_copies(routed, shared, held, sems, step + 1, 1 - slot, steps, width, True)

        both = nt(held[slot, : 2 * width], x_ref[...])
        hidden_grad = nt(held[slot, 2 * width :], c_ref[...])
        hidden, d_gate, d_up, products = expert_unit(
            both[:width], both[width:], hidden_grad, gate_rows(gates[step], width)
        )
        kept_h[0] = hidden
        kept_g[0] = d_gate
        kept_u[0] = d_up
        dots[step] = jnp.concatenate(
            [
                jnp.sum(products[i * unit : (i + 1) * unit], axis=0, keepdims=True)
                for i in range(parts)
            ],
            axis=0,
        )
        turned = hidden.T
        turned_back = jnp.concatenate([d_gate, d_up], axis=0).T
        for at in range(0, model, wide):
            columns = slice(at, at + wide)
            out[:, columns] += nn(turned, held[slot, 2 * width :, columns])
            back[:, columns] += nn(turned_back, held[slot, : 2 * width, columns])

        @pl.when(step == steps - 1)
        def _():
            out_low[...] = out[...].astype(BF)
            spare = jnp.zeros((16 - EXPERTS, count), F32)
            pair_grad = jnp.concatenate([dots[p] for p in range(steps - 1)] + [spare], axis=0)
            named = jnp.concatenate([gates[p] for p in range(steps - 1)] + [spare], axis=0) > 0
            pair_grad = jnp.where(named, pair_grad, 0.0)
            odds = router[...]
            logit_grad = odds * (pair_grad - jnp.sum(odds * pair_grad, axis=0, keepdims=True))
            lg_ref[...] = logit_grad
            turned_logits = logit_grad.T.astype(BF)
            for at in range(0, model, wide):
                columns = slice(at, at + wide)
                back_low[:, columns] = (
                    back[:, columns] + nn(turned_logits, router_ref[:, columns])
                ).astype(BF)

    def whole(shape):
        return pl.BlockSpec(shape, lambda p: (0,) * len(shape), pipeline_mode=pl.Buffered(1))

    def one(shape):
        return pl.BlockSpec((1,) + shape, lambda p: (p, 0, 0))

    kept = jax.ShapeDtypeStruct((steps, width, count), BF)
    total = jax.ShapeDtypeStruct((count, model), BF)
    return pl.pallas_call(
        kernel,
        name="own_experts",
        grid=(steps,),
        in_specs=[
            whole((count, model)),
            pl.BlockSpec((count, 128), lambda p: (0, model // 128), pipeline_mode=pl.Buffered(1)),
            whole((count, model)),
            whole((16, model)),
        ]
        + [pl.BlockSpec(memory_space=pl.ANY)] * 6,
        out_specs=[whole((count, model))] * 2 + [one((width, count))] * 3 + [whole((16, count))],
        out_shape=[total, total, kept, kept, kept, jax.ShapeDtypeStruct((16, count), F32)],
        scratch_shapes=[
            pltpu.VMEM((2, 3 * width, model), BF),
            pltpu.SemaphoreType.DMA((2, 3)),
            pltpu.VMEM((count, model), F32),
            pltpu.VMEM((count, model), F32),
            pltpu.VMEM((steps, parts, count), F32),
            pltpu.VMEM((16, count), F32),
            pltpu.VMEM((steps, parts, count), F32),
        ],
        cost_estimate=SHORT,
        compiler_params=pltpu.CompilerParams(
            vmem_limit_bytes=VMEM_LIMIT, dimension_semantics=("arbitrary",)
        ),
    )(rows, rows, upstream, router_rows, *weights)


def ring_of(axis):
    here = lax.axis_index(axis)
    size = lax.axis_size(axis)
    return here, [lax.rem(here + i, size) for i in range(size)]


def greet(friends):
    barrier = pltpu.get_barrier_semaphore()
    total = 0
    for device, present in friends.values():
        if present is None:
            pl.semaphore_signal(barrier, inc=1, device_id=device, device_id_type=MESH)
            total = total + 1
            continue

        @pl.when(present)
        def _():
            pl.semaphore_signal(barrier, inc=1, device_id=device, device_id_type=MESH)

        total = total + jnp.where(present, 1, 0)
    pl.semaphore_wait(barrier, total)


def mate_friend():
    return {"mate": ({"core": 1 - lax.axis_index("core")}, None)}


def rank_friends():
    _, peers = ring_of("tensor")
    return {f"rank{d}": ({"tensor": peer}, None) for d, peer in enumerate(peers) if d}


def line_friends():
    chip, chips = lax.axis_index("dpo"), lax.axis_size("dpo")
    return {
        "left": ({"dpo": lax.rem(chip + chips - 1, chips)}, chip > 0),
        "right": ({"dpo": lax.rem(chip + 1, chips)}, chip < chips - 1),
    }


def remote(source, target, send, receive, device):
    return pltpu.make_async_remote_copy(
        src_ref=source, dst_ref=target, send_sem=send, recv_sem=receive,
        device_id=device, device_id_type=MESH,
    )


class Scatter:
    def __init__(self, rows):
        ranks = lax.axis_size("tensor")
        quarter = rows.shape[0] // ranks
        self.ins = [rows.reshape(ranks, quarter, rows.shape[1])]
        self.in_specs = [pl.BlockSpec(memory_space=pl.ANY)]
        self.outs = [jax.ShapeDtypeStruct((ranks - 1, quarter, rows.shape[1]), rows.dtype)]
        self.out_specs = [pl.BlockSpec(memory_space=pl.ANY)]
        self.scratch = [pltpu.SemaphoreType.DMA((ranks,)), pltpu.SemaphoreType.DMA((ranks,))]

    def copies(self, refs):
        source, target, sends, receives = refs
        _, peers = ring_of("tensor")
        return [
            remote(source.at[peer], target.at[d - 1], sends.at[d], receives.at[d], {"tensor": peer})
            for d, peer in enumerate(peers)
            if d
        ]

    def friends(self):
        return rank_friends()

    def begin(self, refs):
        for copy in self.copies(refs):
            copy.start()

    def middle(self, refs, step, last):
        pass

    def end(self, refs):
        for copy in self.copies(refs):
            copy.wait()


class Gather(Scatter):
    def __init__(self, rows):
        ranks = lax.axis_size("tensor")
        self.ins = [rows]
        self.in_specs = [pl.BlockSpec(memory_space=pl.ANY)]
        self.outs = [jax.ShapeDtypeStruct((ranks,) + rows.shape, rows.dtype)]
        self.out_specs = [pl.BlockSpec(memory_space=pl.ANY)]
        self.scratch = [pltpu.SemaphoreType.DMA((ranks,)), pltpu.SemaphoreType.DMA((ranks,))]

    def copies(self, refs):
        source, target, sends, receives = refs
        rank, peers = ring_of("tensor")
        return [pltpu.make_async_copy(source, target.at[rank], sends.at[0])] + [
            remote(source, target.at[rank], sends.at[d], receives.at[d], {"tensor": peer})
            for d, peer in enumerate(peers)
            if d
        ]


class Many(Scatter):
    def __init__(self, transfers):
        self.transfers = transfers
        self.ins = [x for t in transfers for x in t.ins]
        self.in_specs = [x for t in transfers for x in t.in_specs]
        self.outs = [x for t in transfers for x in t.outs]
        self.out_specs = [x for t in transfers for x in t.out_specs]
        self.scratch = [x for t in transfers for x in t.scratch]

    def copies(self, refs):
        n = len(self.transfers)
        copies = []
        for i, t in enumerate(self.transfers):
            own = [refs[i], refs[n + i], refs[2 * n + 2 * i], refs[2 * n + 2 * i + 1]]
            copies += t.copies(own)
        return copies


class LineSum:
    def __init__(self, blocks):
        chips = lax.axis_size("dpo")
        self.chips = chips
        shape = blocks.shape[1:]
        self.ins = [blocks]
        self.in_specs = [pl.BlockSpec(memory_space=pl.ANY)]
        self.outs = [jax.ShapeDtypeStruct(shape, F32)]
        self.out_specs = [pl.BlockSpec(shape, lambda *_: (0, 0), pipeline_mode=pl.Buffered(1))]
        self.scratch = [
            pltpu.VMEM((chips,) + shape, blocks.dtype),
            pltpu.VMEM((chips,) + shape, blocks.dtype),
            pltpu.VMEM(shape, blocks.dtype),
        ] + [pltpu.SemaphoreType.DMA((chips,))] * 4 + [pltpu.SemaphoreType.DMA]

    def swap(self, refs, i):
        source, _, mate, _, _, sends, receives, _, _, _ = refs
        core = lax.axis_index("core")
        return remote(source.at[2 * i + 1 - core], mate.at[i], sends.at[i], receives.at[i], {"core": 1 - core})

    def onward(self, refs, i):
        _, _, mate, inbox, _, _, _, sends, receives, _ = refs
        chip = lax.axis_index("dpo")
        return remote(mate.at[i], inbox.at[i], sends.at[i], receives.at[i], {"dpo": lax.rem(chip + self.chips - 1, self.chips)})

    def friends(self):
        return line_friends()

    def begin(self, refs):
        chip = lax.axis_index("dpo")
        for i in range(self.chips):
            @pl.when(i <= chip)
            def _():
                self.swap(refs, i).start()

    def middle(self, refs, step, last):
        source, out, mate, inbox, mine, _, _, _, _, sem = refs
        chip, core = lax.axis_index("dpo"), lax.axis_index("core")
        for i in range(self.chips):
            due = jnp.minimum(1 + 3 * (self.chips - 1 - chip) + i, last)

            @pl.when((i <= chip) & (step == due))
            def _():
                local = pltpu.make_async_copy(source.at[2 * i + core], mine, sem)
                local.start()
                self.swap(refs, i).wait()
                local.wait()

                @pl.when(chip < self.chips - 1)
                def _():
                    self.onward(refs, i).wait_recv()
                    mate[i] = (
                        mate[i].astype(F32) + mine[...].astype(F32) + inbox[i].astype(F32)
                    ).astype(mate.dtype)

                @pl.when(chip == self.chips - 1)
                def _():
                    mate[i] = (mate[i].astype(F32) + mine[...].astype(F32)).astype(mate.dtype)

                @pl.when(chip > i)
                def _():
                    self.onward(refs, i).start()

                @pl.when(chip == i)
                def _():
                    out[...] = mate[i].astype(F32)

    def end(self, refs):
        chip = lax.axis_index("dpo")
        for i in range(self.chips):
            @pl.when(chip > i)
            def _():
                self.onward(refs, i).wait_send()


class LineSpread(LineSum):
    def __init__(self, arrays):
        chips = lax.axis_size("dpo")
        self.chips = chips
        self.dimensions = [d for _, d in arrays]
        self.shapes = [
            tuple(n // (2 * chips) if i == d else n for i, n in enumerate(a.shape)) for a, d in arrays
        ]
        n = len(arrays)
        self.ins = [a for a, _ in arrays]
        self.in_specs = [pl.BlockSpec(memory_space=pl.ANY)] * n
        self.outs = [jax.ShapeDtypeStruct(shape, F32) for shape in self.shapes]
        self.out_specs = [
            pl.BlockSpec(shape, lambda *_: (0, 0), pipeline_mode=pl.Buffered(1)) for shape in self.shapes
        ]
        self.scratch = []
        for shape in self.shapes:
            self.scratch += [
                pltpu.VMEM((chips,) + shape, BF),
                pltpu.VMEM((chips + 1,) + shape, BF),
                pltpu.VMEM(shape, BF),
            ]
        self.scratch += [
            pltpu.SemaphoreType.DMA((n, chips)),
            pltpu.SemaphoreType.DMA((n, chips)),
            pltpu.SemaphoreType.DMA((n, chips)),
            pltpu.SemaphoreType.DMA((n, chips + 1)),
            pltpu.SemaphoreType.DMA((n,)),
        ]

    def parts(self, refs):
        n = len(self.shapes)
        buffers = refs[2 * n : 5 * n]
        return [(refs[j], refs[n + j]) + tuple(buffers[3 * j : 3 * j + 3]) for j in range(n)], refs[5 * n :]

    def block(self, j, source, place):
        size = self.shapes[j][self.dimensions[j]]
        part = pl.ds(pl.multiple_of(place * size, size), size)
        return source.at[part] if self.dimensions[j] == 0 else source.at[:, part]

    def swaps(self, refs, i):
        parts, sems = self.parts(refs)
        core = lax.axis_index("core")
        return [
            remote(
                self.block(j, source, 2 * i + 1 - core), mate.at[i], sems[0].at[j, i], sems[1].at[j, i],
                {"core": 1 - core},
            )
            for j, (source, _, mate, _, _) in enumerate(parts)
        ]

    def onwards(self, refs, i, slot, step):
        parts, sems = self.parts(refs)
        chip = lax.axis_index("dpo")
        to = lax.rem(chip + step + self.chips, self.chips)
        return [
            remote(mate.at[i], inbox.at[slot], sems[2].at[j, i], sems[3].at[j, slot], {"dpo": to})
            for j, (_, _, mate, inbox, _) in enumerate(parts)
        ]

    def begin(self, refs):
        for i in range(self.chips):
            for copy in self.swaps(refs, i):
                copy.start()

    def middle(self, refs, step, last):
        chip, core = lax.axis_index("dpo"), lax.axis_index("core")
        parts, sems = self.parts(refs)
        end = self.chips - 1

        def arrive(i, slot):
            for copy in self.onwards(refs, i, slot, 0):
                copy.wait_recv()
            for _, _, mate, inbox, _ in parts:
                mate[i] = (mate[i].astype(F32) + inbox[slot].astype(F32)).astype(BF)

        for i in range(self.chips):
            due = jnp.minimum(1 + 3 * (end - jnp.abs(chip - i)), last)

            @pl.when(step == due)
            def _():
                locals_ = [
                    pltpu.make_async_copy(self.block(j, source, 2 * i + core), mine, sems[4].at[j])
                    for j, (source, _, _, _, mine) in enumerate(parts)
                ]
                for copy in locals_:
                    copy.start()
                for copy in self.swaps(refs, i) + locals_:
                    copy.wait()
                for _, _, mate, _, mine in parts:
                    mate[i] = (mate[i].astype(F32) + mine[...].astype(F32)).astype(BF)

                @pl.when((i <= chip) & (chip < end))
                def _():
                    arrive(i, i)

                @pl.when((i > chip) & (chip > 0))
                def _():
                    arrive(i, i)

                @pl.when((i == chip) & (chip > 0))
                def _():
                    arrive(i, self.chips)

                @pl.when(i < chip)
                def _():
                    for copy in self.onwards(refs, i, i, -1):
                        copy.start()

                @pl.when(i == chip + 1)
                def _():
                    for copy in self.onwards(refs, i, self.chips, 1):
                        copy.start()

                @pl.when(i > chip + 1)
                def _():
                    for copy in self.onwards(refs, i, i, 1):
                        copy.start()

                @pl.when(i == chip)
                def _():
                    for _, out, mate, _, _ in parts:
                        out[...] = mate[i].astype(F32)

    def end(self, refs):
        chip = lax.axis_index("dpo")
        for i in range(self.chips):
            @pl.when(chip != i)
            def _():
                for copy in self.onwards(refs, i, i, 0):
                    copy.wait_send()


class Beside:
    def __init__(self, former, latter):
        self.pair = (former, latter)
        self.ins = former.ins + latter.ins
        self.in_specs = former.in_specs + latter.in_specs
        self.outs = former.outs + latter.outs
        self.out_specs = former.out_specs + latter.out_specs
        self.scratch = former.scratch + latter.scratch

    def split(self, refs):
        refs = list(refs)
        lists = ([], [])
        for name in ("ins", "outs", "scratch"):
            for t, held in zip(self.pair, lists):
                n = len(getattr(t, name))
                held += refs[:n]
                del refs[:n]
        return zip(self.pair, lists)

    def friends(self):
        return {**self.pair[0].friends(), **self.pair[1].friends()}

    def begin(self, refs):
        for t, held in self.split(refs):
            t.begin(held)

    def middle(self, refs, step, last):
        for t, held in self.split(refs):
            t.middle(held, step, last)

    def end(self, refs):
        for t, held in self.split(refs):
            t.end(held)


def settle(part, more, finish, extra, wide, collective):
    count, model = part[0].shape[0], part[-1].shape[1]
    ranks = lax.axis_size("tensor")
    quarter = count // ranks
    n_part, n_more, n_extra = len(part), len(more), len(extra)

    def kernel(*refs):
        refs = list(refs)

        def take(n):
            taken = refs[:n]
            del refs[:n]
            return taken

        part_refs, more_refs = take(n_part), take(n_more)
        (out_ref,), extra_refs = take(1), take(n_extra)
        inbox, block, gathered, send, receive, send_on, receive_on = take(7)
        part_ref = refs[0] if refs else part_refs[0]
        rank, peers = ring_of("tensor")

        def rows_of(i):
            return pl.ds(pl.multiple_of(i * quarter, quarter), quarter)

        def make(i):
            if n_part == 2:
                part_ref[rows_of(i)] = nn(part_refs[0][rows_of(i)], part_refs[1][...]).astype(BF)

        greet(rank_friends())
        copies = []
        for d, peer in enumerate(peers):
            if d:
                make(peer)
                copies.append(
                    remote(part_ref.at[rows_of(peer)], inbox.at[d], send.at[d], receive.at[d], {"tensor": peer})
                )
                copies[-1].start()
        make(rank)
        total = part_ref[rows_of(rank)].astype(F32)
        for d, copy in enumerate(copies):
            copy.wait()
            total = total + inbox[d + 1].astype(F32)
        results = finish(total, [r[...] for r in more_refs])
        for ref, value in zip(extra_refs, results):
            ref[...] = value
        block[...] = results[-1]
        copies = [
            remote(block, gathered.at[d], send_on.at[d], receive_on.at[d], {"tensor": peer})
            for d, peer in enumerate(peers)
            if d
        ]
        for copy in copies:
            copy.start()
        out_ref[rows_of(rank)] = block[...]
        for d, copy in enumerate(copies):
            copy.wait()
            out_ref[rows_of(lax.rem(rank + ranks - d - 1, ranks))] = gathered[d + 1]

    vmem = pl.BlockSpec(memory_space=pltpu.VMEM)
    sems = [pltpu.SemaphoreType.DMA((ranks,))] * 4
    return pl.pallas_call(
        kernel,
        name="settle",
        in_specs=[vmem] * (n_part + n_more),
        out_specs=[vmem] * (1 + n_extra),
        out_shape=[jax.ShapeDtypeStruct((count, wide), BF)] + extra,
        scratch_shapes=[
            pltpu.VMEM((ranks, quarter, model), BF),
            pltpu.VMEM((quarter, wide), BF),
            pltpu.VMEM((ranks, quarter, wide), BF),
        ]
        + sems
        + ([pltpu.VMEM((count, model), BF)] if n_part == 2 else []),
        cost_estimate=SHORT,
        compiler_params=pltpu.CompilerParams(
            vmem_limit_bytes=VMEM_LIMIT, collective_id=collective, has_side_effects=True
        ),
    )(*part, *more)


def group_gradients(rows, upstream, row_cols, up_cols, gates, kept, weights, first, groups, held_back, beside, collective):
    chips, count, model = upstream.shape
    steps, _, parts, _ = gates.shape
    width = weights[3].shape[0]
    half = row_cols.shape[2] // 2
    unit = width // 2
    n_ins, n_outs, n_held = len(beside.ins), len(beside.outs), len(held_back)
    last = groups * chips - 1
    ends = first + groups == steps

    def kernel(*refs):
        refs = list(refs)

        def take(n):
            taken = refs[:n]
            del refs[:n]
            return taken

        x_ref, c_ref, xc, cc, g_ref, kept_h, kept_g, kept_u = take(8)
        routed, shared = take(3), take(3)
        take(n_held)
        link_refs = take(n_ins)
        outs = take(3)
        shared_outs = take(3) if ends else None
        link_refs += take(n_outs)
        held, sems, sum_g, sum_u, sum_d, outbox, inbox, sends, receives = take(9)
        link_refs += refs
        at_group = pl.program_id(0)
        turn = pl.program_id(1)
        step = at_group + first
        slot = lax.rem(at_group, 2)
        tick = at_group * chips + turn
        sums = (sum_g, sum_u, sum_d)

        def swap(i):
            part = pl.ds(i * unit, unit)
            return remote(
                outbox.at[:, part], inbox.at[slot, :, part], sends.at[slot, i], receives.at[slot, i],
                {"core": 1 - lax.axis_index("core")},
            )

        @pl.when(tick == 0)
        def _():
            greet({**mate_friend(), **beside.friends()})
            beside.begin(link_refs)

        @pl.when(turn == 0)
        def _():
            @pl.when(at_group == 0)
            def _():
                weight_copies(routed, shared, held, sems, step, slot, steps, width, True)

            sum_g[...] = nn(kept_g[0], xc[0])
            sum_u[...] = nn(kept_u[0], xc[0])
            sum_d[...] = nn(kept_h[0], cc[0])
            weight_copies(routed, shared, held, sems, step, slot, steps, width, False)

            @pl.when(at_group < groups - 1)
            def _():
                weight_copies(routed, shared, held, sems, step + 1, 1 - slot, steps, width, True)

        def work(final):
            x = x_ref[0]
            c = c_ref[0]
            gate = gate_rows(g_ref[0, 0], width)
            for i in range(2):
                at = i * unit
                part = slice(at, at + unit)
                gate_pre = nt(held[slot, at : at + unit], x)
                up_pre = nt(held[slot, width + at : width + at + unit], x)
                hidden_grad = nt(held[slot, 2 * width + at : 2 * width + at + unit], c)
                hidden, d_gate, d_up, _ = expert_unit(gate_pre, up_pre, hidden_grad, gate[part])
                sum_g[part] += nn(d_gate, xc[0])
                sum_u[part] += nn(d_up, xc[0])
                sum_d[part] += nn(hidden, cc[0])
                if final:
                    for j, total in enumerate(sums):
                        outbox[j, part] = total[part, half:].astype(BF)
                    swap(i).start()

        @pl.when((turn > 0) & (turn < chips - 1))
        def _():
            work(False)

        @pl.when(turn == chips - 1)
        def _():
            work(True)
            for i in range(2):
                swap(i).wait()
                part = slice(i * unit, (i + 1) * unit)
                for j, total in enumerate(sums):
                    value = (total[part, :half] + inbox[slot, j, part].astype(F32)).astype(BF)
                    if not ends:
                        outs[j][part] = value
                        continue

                    @pl.when(step < steps - 1)
                    def _():
                        outs[j][part] = value

                    @pl.when(step == steps - 1)
                    def _():
                        shared_outs[j][part] = value

        beside.middle(link_refs, tick, last)

        @pl.when(tick == last)
        def _():
            beside.end(link_refs)

    def chip_at(turn):
        return lax.rem(lax.axis_index("dpo") + turn, chips)

    def at_chip(shape):
        return pl.BlockSpec((1,) + shape, lambda p, k: (chip_at(k), 0, 0))

    def one(shape):
        return pl.BlockSpec((1,) + shape, lambda p, k: (p + first, 0, 0))

    anywhere = pl.BlockSpec(memory_space=pl.ANY)
    block = pl.BlockSpec((width, half), lambda p, k: (jnp.minimum(p + first, steps - 2), 0))
    shared_block = pl.BlockSpec((width, half), lambda p, k: (0, 0))
    return pl.pallas_call(
        kernel,
        name="group_gradients",
        grid_spec=pltpu.PrefetchScalarGridSpec(
            num_scalar_prefetch=0,
            grid=(groups, chips),
            in_specs=[at_chip((count, model))] * 2
            + [at_chip((count, 2 * half))] * 2
            + [pl.BlockSpec((1, 1, parts, count), lambda p, k: (p + first, chip_at(k), 0, 0))]
            + [one((width, count))] * 3
            + [anywhere] * (6 + n_held)
            + beside.in_specs,
            out_specs=[block] * 3 + ([shared_block] * 3 if ends else []) + beside.out_specs,
            scratch_shapes=[
                pltpu.VMEM((2, 3 * width, model), BF),
                pltpu.SemaphoreType.DMA((2, 3)),
            ]
            + [pltpu.VMEM((width, 2 * half), F32)] * 3
            + [
                pltpu.VMEM((3, width, half), BF),
                pltpu.VMEM((2, 3, width, half), BF),
                pltpu.SemaphoreType.DMA((2, 2)),
                pltpu.SemaphoreType.DMA((2, 2)),
            ]
            + beside.scratch,
        ),
        out_shape=[jax.ShapeDtypeStruct(((steps - 1) * width, half), BF)] * 3
        + ([jax.ShapeDtypeStruct((width, half), BF)] * 3 if ends else [])
        + beside.outs,
        input_output_aliases={14 + i: i for i in range(n_held)},
        cost_estimate=pl.CostEstimate(
            flops=groups * 2 * width * count * (3 * (chips - 1) * model + 6 * chips * half),
            bytes_accessed=groups * (6 * width * model + 4 * chips * count * model),
            transcendentals=0,
        ),
        compiler_params=pltpu.CompilerParams(
            vmem_limit_bytes=VMEM_LIMIT,
            dimension_semantics=("arbitrary", "arbitrary"),
            collective_id=collective,
            has_side_effects=True,
        ),
    )(
        rows, upstream, row_cols, up_cols, gates, *kept, *weights, *held_back, *beside.ins,
    )


def turn_pairs(values, even, odd):
    lane = lax.broadcasted_iota(jnp.int32, values.shape, 1)
    other = jnp.where(lane < RD // 2, pltpu.roll(values, 128 - RD // 2, 1), pltpu.roll(values, RD // 2, 1))
    return values * even + other * odd


def attention_forward(tokens, gain, query_weight, latent_rows, latent_gain, latent_up, even, odd, key_ids, query_ids, collective):
    count, model = tokens.shape
    heads = latent_up.shape[1] // 256
    chips = lax.axis_size("dpo")
    ranks = lax.axis_size("tensor")
    quarter = count // ranks
    scale = (ND + RD) ** (-0.5) * LOG2E

    def kernel(x_ref, gain_ref, qw_ref, ld_ref, lg_ref, up_ref, even_ref, odd_ref, kid_ref, qid_ref,
               att_ref, lse_ref, all_ref, in_ref, raw_ref, q_ref, lat_ref, rope_ref, keys, top, low, mix,
               send_right, take_left, send_mate, take_mate, send_rank, take_rank):
        chip, core = lax.axis_index("dpo"), lax.axis_index("core")
        rank, peers = ring_of("tensor")
        place = chip * 2 + core
        right = lax.rem(chip + 1, chips)
        own_rows = pl.ds(pl.multiple_of(rank * quarter, quarter), quarter)
        greet({**mate_friend(), **line_friends(), **rank_friends()})

        def to_right(i):
            return remote(
                all_ref.at[2 * i + core, own_rows], all_ref.at[2 * i + core, own_rows],
                send_right.at[i], take_left.at[i], {"dpo": right},
            )

        def to_mate(i):
            return remote(
                all_ref.at[2 * i + core], all_ref.at[2 * i + core],
                send_mate.at[i], take_mate.at[i], {"core": 1 - core},
            )

        def to_ranks(i):
            return [
                remote(
                    all_ref.at[2 * i + core, own_rows], all_ref.at[2 * i + core, own_rows],
                    send_rank.at[i, d], take_rank.at[i, d], {"tensor": peer},
                )
                for d, peer in enumerate(peers)
                if d
            ]

        x = x_ref[...].astype(F32)
        normed, _ = norm_rows(x, gain_ref[...])
        in_ref[...] = normed.astype(BF)
        raw = nt(in_ref[...], ld_ref[:KVL])
        raw_ref[...] = raw
        rope_ref[...] = jnp.zeros_like(rope_ref)
        rope_ref[:, :RD] = nt(in_ref[...], ld_ref[KVL:])
        latent, _ = norm_rows(raw, lg_ref[...])
        lat_ref[:, :KVL] = latent.astype(BF)
        lat_ref[:, KVL:] = turn_pairs(rope_ref[...], even_ref[...], odd_ref[...]).astype(BF)
        all_ref[place] = lat_ref[...]

        @pl.when(chip < chips - 1)
        def _():
            to_right(chip).start()

        to_mate(chip).start()
        raw_q = nn(in_ref[...], qw_ref[...])
        lane = lax.broadcasted_iota(jnp.int32, (count, 128), 1)
        for h in range(0, heads, 2):
            at = h * (ND + RD)
            former, between, latter = (raw_q[:, at + i : at + i + 128] for i in (0, 128, 256))
            rolled = pltpu.roll(latter, 64, 1)
            nope = jnp.where(lane < 64, pltpu.roll(between, 64, 1), rolled)
            for i, (plain, rope) in enumerate(((former, between), (nope, rolled))):
                to = (h + i) * 256
                q_ref[:, to : to + ND] = plain.astype(BF)
                q_ref[:, to + ND : to + 256] = turn_pairs(rope, even_ref[...], odd_ref[...]).astype(BF)
        top[...] = jnp.full_like(top, -1e30)
        low[...] = jnp.zeros_like(low)
        mix[...] = jnp.zeros_like(mix)

        def chunk(source, masked):
            lat = source[:, :KVL]
            rope = source[:, KVL:]
            for h in range(heads):
                keys[h, :, ND:] = rope
                both = nn(lat, up_ref[:, h * 256 : (h + 1) * 256]).astype(BF)
                keys[h, :, :ND] = both[:, :ND]
                values = both[:, ND:].T
                scores = nt(keys[h], q_ref[:, h * 256 : (h + 1) * 256]) * scale
                if masked:
                    scores = jnp.where(kid_ref[...] <= qid_ref[...], scores, -1e30)
                before = top[h]
                highest = jnp.maximum(before, jnp.max(scores, axis=0, keepdims=True))
                weights = jnp.exp2(scores - highest)
                decay = jnp.exp2(before - highest)
                top[h] = highest
                low[h] = low[h] * decay + jnp.sum(weights, axis=0, keepdims=True)
                mix[h] = mix[h] * decay + nn(values, weights.astype(BF))

        def intake(i):
            to_right(i).wait_recv()

            @pl.when(chip < chips - 1)
            def _():
                to_right(i).start()

            for copy in to_ranks(i):
                copy.start()

        chunk(lat_ref, True)

        @pl.when(chip > 0)
        def _():
            intake(chip - 1)

        to_mate(chip).wait()

        @pl.when(core == 1)
        def _():
            chunk(all_ref.at[place - 1], False)

        def earlier(i, carry):
            at = chip - 1 - i

            @pl.when(at > 0)
            def _():
                intake(at - 1)

            for copy in to_ranks(at):
                copy.wait_recv()
            to_mate(at).start()
            chunk(all_ref.at[2 * at + core], False)
            to_mate(at).wait_recv()
            chunk(all_ref.at[2 * at + 1 - core], False)
            return carry

        lax.fori_loop(0, chip, earlier, 0)
        for h in range(heads):
            att_ref[:, h * VD : (h + 1) * VD] = (mix[h] / low[h]).T.astype(BF)
            lse_ref[h] = top[h] + jnp.log2(low[h])

        def sent(i, carry):
            to_mate(i).wait_send()
            for copy in to_ranks(i):
                copy.wait_send()
            return carry

        lax.fori_loop(0, chip, sent, 0)

        @pl.when(chip < chips - 1)
        def _():
            def sent_right(i, carry):
                to_right(i).wait_send()
                return carry

            lax.fori_loop(0, chip + 1, sent_right, 0)

    vmem = pl.BlockSpec(memory_space=pltpu.VMEM)
    sems = pltpu.SemaphoreType.DMA((chips,))
    rank_sems = pltpu.SemaphoreType.DMA((chips, ranks))
    return pl.pallas_call(
        kernel,
        name="attention_forward",
        in_specs=[vmem] * 10,
        out_specs=[vmem] * 6,
        out_shape=[
            jax.ShapeDtypeStruct((count, heads * VD), BF),
            jax.ShapeDtypeStruct((heads, 1, count), F32),
            jax.ShapeDtypeStruct((2 * chips, count, LAT), BF),
            jax.ShapeDtypeStruct((count, model), BF),
            jax.ShapeDtypeStruct((count, KVL), F32),
            jax.ShapeDtypeStruct((count, heads * 256), BF),
        ],
        scratch_shapes=[
            pltpu.VMEM((count, LAT), BF),
            pltpu.VMEM((count, 128), F32),
            pltpu.VMEM((heads, count, 256), BF),
            pltpu.VMEM((heads, 1, count), F32),
            pltpu.VMEM((heads, 1, count), F32),
            pltpu.VMEM((heads, VD, count), F32),
            sems,
            sems,
            sems,
            sems,
            rank_sems,
            rank_sems,
        ],
        cost_estimate=SHORT,
        compiler_params=pltpu.CompilerParams(
            vmem_limit_bytes=VMEM_LIMIT, collective_id=collective, has_side_effects=True
        ),
    )(tokens, gain, query_weight, latent_rows, latent_gain, latent_up, even, odd, key_ids, query_ids)


def attention_backward(queries, latents, latent_up, key_ids, query_ids, attended, output_grad, output_weight, lse, even, odd):
    count = queries.shape[0]
    heads = queries.shape[1] // 256
    blocks = latents.shape[0]
    factor = (ND + RD) ** (-0.5)
    scale = factor * LOG2E

    def kernel(q_ref, lat_ref, up_ref, kid_ref, qid_ref, att_ref, og_ref, ow_ref, lse_ref, even_ref, odd_ref,
               dq_ref, dup_ref, dlat_ref, do_ref, delta, keys, dq, dup, dlat):
        place = lax.axis_index("dpo") * 2 + lax.axis_index("core")
        dq[...] = jnp.zeros_like(dq)
        dup[...] = jnp.zeros_like(dup)
        do_ref[...] = nt(og_ref[...], ow_ref[...]).astype(BF)
        for h in range(heads):
            part = slice(h * VD, (h + 1) * VD)
            products = do_ref[:, part].astype(F32) * att_ref[:, part].astype(F32)
            delta[h] = jnp.sum(products.T, axis=0, keepdims=True)

        def chunk(at, masked):
            lat = lat_ref[at, :, :KVL]
            turned = lat.T
            rope = lat_ref[at, :, KVL:]
            dlat[...] = jnp.zeros_like(dlat)
            for h in range(heads):
                up = up_ref[:, h * 256 : (h + 1) * 256]
                query = q_ref[:, h * 256 : (h + 1) * 256]
                upstream = do_ref[:, h * VD : (h + 1) * VD]
                keys[h, :, ND:] = rope
                both = nn(lat, up).astype(BF)
                keys[h, :, :ND] = both[:, :ND]
                scores = nt(keys[h], query) * scale
                chances = jnp.exp2(scores - lse_ref[h])
                if masked:
                    chances = jnp.where(kid_ref[...] <= qid_ref[...], chances, 0.0)
                chance_grad = nt(both[:, ND:], upstream)
                score_grad = (chances * (chance_grad - delta[h])).astype(BF)
                value_grad = nn(chances.astype(BF), upstream)
                key_grad = nn(score_grad, query) * factor
                dq[h] += nn(keys[h].T, score_grad)
                both_grad = jnp.concatenate([key_grad[:, :ND], value_grad], axis=1).astype(BF)
                dlat[:, :KVL] += nt(both_grad, up)
                dlat[:, KVL:] += key_grad[:, ND:]
                dup[:, h * 256 : (h + 1) * 256] += nn(turned, both_grad)
            dlat_ref[at] = dlat[...].astype(BF)

        lax.fori_loop(0, place, lambda at, carry: (chunk(at, False), carry)[1], 0)
        chunk(place, True)

        def clear(at, carry):
            dlat_ref[at] = jnp.zeros((count, LAT), BF)
            return carry

        lax.fori_loop(place + 1, blocks, clear, 0)
        dup_ref[...] = dup[...].astype(BF)
        lane = lax.broadcasted_iota(jnp.int32, (count, 128), 1)
        for h in range(0, heads, 2):
            plain, ropes = [], []
            for i in range(2):
                back = dq[h + i].T * factor
                plain.append(back[:, :ND])
                ropes.append(turn_pairs(back[:, ND:], even_ref[...], -odd_ref[...]))
            moved = pltpu.roll(plain[1], 64, 1)
            at = h * (ND + RD)
            dq_ref[:, at : at + 128] = plain[0].astype(BF)
            dq_ref[:, at + 128 : at + 256] = jnp.where(lane < 64, ropes[0], moved).astype(BF)
            dq_ref[:, at + 256 : at + 384] = jnp.where(
                lane < 64, moved, pltpu.roll(ropes[1], 64, 1)
            ).astype(BF)

    vmem = pl.BlockSpec(memory_space=pltpu.VMEM)
    return pl.pallas_call(
        kernel,
        name="attention_backward",
        in_specs=[vmem] * 11,
        out_specs=[vmem] * 3,
        out_shape=[
            jax.ShapeDtypeStruct((count, heads * (ND + RD)), BF),
            jax.ShapeDtypeStruct((KVL, heads * 256), BF),
            jax.ShapeDtypeStruct((blocks, count, LAT), BF),
        ],
        scratch_shapes=[
            pltpu.VMEM((count, heads * VD), BF),
            pltpu.VMEM((heads, 1, count), F32),
            pltpu.VMEM((heads, count, 256), BF),
            pltpu.VMEM((heads, 256, count), F32),
            pltpu.VMEM((KVL, heads * 256), F32),
            pltpu.VMEM((count, LAT), F32),
        ],
        cost_estimate=SHORT,
        compiler_params=pltpu.CompilerParams(vmem_limit_bytes=VMEM_LIMIT),
    )(queries, latents, latent_up, key_ids, query_ids, attended, output_grad, output_weight, lse, even, odd)


def grouped(gates, steps):
    parts = EXPERTS // (steps - 1)
    gates = gates.reshape((steps - 1, parts) + gates.shape[1:])
    return jnp.concatenate([gates, jnp.ones((1,) + gates.shape[1:], F32)], axis=0)


def shards(
    tokens,
    cotangent,
    block_ids,
    routes,
    first_gain,
    query_weight,
    latent_down,
    latent_gain,
    latent_up,
    output_weight,
    second_gain,
    router_weight,
    gate_weight,
    up_weight,
    down_weight,
    shared_gate,
    shared_up,
    shared_down,
):
    count, model = tokens.shape
    key_count = block_ids.shape[0]
    heads = query_weight.shape[1] // (ND + RD)
    unit = gate_weight.shape[2]
    width = shared_down.shape[0]
    steps = EXPERTS * unit // width + 1
    chips = lax.axis_size("dpo")
    ranks = lax.axis_size("tensor")
    devices = chips * 2 * ranks
    chip, core, rank = lax.axis_index("dpo"), lax.axis_index("core"), lax.axis_index("tensor")
    place = chip * 2 + core
    quarter = count // ranks
    half = model // (2 * chips)
    routed_rows = EXPERTS * unit

    def mine(array):
        return lax.dynamic_slice_in_dim(array, rank * quarter, quarter, 0)

    weights = (
        jnp.swapaxes(gate_weight, 1, 2).reshape(routed_rows, model),
        jnp.swapaxes(up_weight, 1, 2).reshape(routed_rows, model),
        down_weight.reshape(routed_rows, model),
        shared_gate.T,
        shared_up.T,
        shared_down,
    )

    row_start = place * count
    cosine, sine_table = rotary_tables((row_start + jnp.arange(count, dtype=jnp.int32)) % key_count)
    own_blocks = lax.dynamic_slice_in_dim(block_ids, row_start, count, 0)
    rest = jnp.zeros((count, 128 - RD), F32)
    even = jnp.concatenate([cosine, cosine, rest], axis=1)
    odd = jnp.concatenate([-sine_table, sine_table, rest], axis=1)
    key_ids, query_ids = own_blocks[:, None], own_blocks[None, :]
    all_upstream = lax.all_gather(cotangent, "dpo", axis=0, tiled=True)
    attended, lse, latents, attention_input, latent_raw, queries = attention_forward(
        tokens, first_gain[None], query_weight, latent_down.T, latent_gain[None], latent_up,
        even, odd, key_ids, query_ids, 1,
    )

    named = jnp.any(
        routes[:, :, None] == jnp.arange(128, dtype=jnp.int32)[None, None, :], axis=1
    )
    named = (named | (jnp.arange(128) >= EXPERTS)[None, :]).astype(F32)
    token_quarter = mine(tokens)
    parts = EXPERTS // (steps - 1)

    def second_norm(total, more):
        rows, gain, router_columns, mask = more
        residual = rows.astype(F32) + total
        normed, _ = norm_rows(residual, gain)
        normed = normed.astype(BF)
        logits = nn(normed, router_columns)
        lane = lax.broadcasted_iota(jnp.int32, logits.shape, 1)
        first = lane < EXPERTS
        logits = jnp.where(first | ((lane >= 16) & (lane < 16 + EXPERTS)), logits, -1e30)
        odds = jnp.exp(logits - jnp.max(logits, axis=1, keepdims=True))
        odds = odds / jnp.sum(jnp.where(first, odds, 0.0), axis=1, keepdims=True)
        gates = jnp.where((lane >= EXPERTS) & (lane < EXPERTS + parts), 1.0, mask * odds)
        return residual, jnp.concatenate([normed, gates.astype(BF)], axis=1)

    twice = jnp.pad(router_weight, ((0, 0), (0, 16 - EXPERTS)))
    wide_input, residual = settle(
        [attended, output_weight],
        [
            token_quarter,
            second_gain[None],
            jnp.pad(jnp.concatenate([twice, twice], axis=1), ((0, 0), (0, 96))),
            mine(named),
        ],
        second_norm,
        [jax.ShapeDtypeStruct((quarter, model), F32)],
        model + 128,
        2,
    )
    all_input = lax.all_gather(wide_input, "dpo", axis=0, tiled=True)
    all_input = all_input.reshape(chips, count, model + 128)

    expert_part, input_back, kept_h, kept_g, kept_u, logit_grad = own_experts(
        wide_input, cotangent, twice.T, weights
    )

    def second_norm_back(total, more):
        rows, gain, upstream_rows = more
        factor = lax.rsqrt(jnp.mean(rows * rows, axis=-1, keepdims=True) + EPSILON)
        back, gain_grad = norm_back(rows, factor, gain, total)
        back = back + upstream_rows.astype(F32)
        return back, gain_grad[None], back.astype(BF)

    input_back, all_upstream = lax.optimization_barrier((input_back, all_upstream))
    output_grad, residual_grad, grad_second_gain = settle(
        [input_back],
        [residual, second_gain[None], mine(cotangent)],
        second_norm_back,
        [
            jax.ShapeDtypeStruct((quarter, model), F32),
            jax.ShapeDtypeStruct((1, model), F32),
        ],
        model,
        3,
    )
    grad_second_gain = grad_second_gain[0]

    all_gates = grouped(
        jnp.transpose(all_input[:, :, model : model + EXPERTS].astype(F32), (2, 0, 1)), steps
    )
    all_gates = jnp.swapaxes(all_gates, 1, 2)

    def chip_columns(array):
        return jnp.concatenate(
            [
                lax.dynamic_slice_in_dim(array, (chip * 2 + c) * half, half, 2)
                for c in (core, 1 - core)
            ],
            axis=2,
        )

    all_upstream = all_upstream.reshape(chips, count, model)
    input_cols, upstream_cols = chip_columns(all_input), chip_columns(all_upstream)
    routed_grads = []

    def piece(first, groups, beside, collective):
        made = group_gradients(
            all_input, all_upstream, input_cols, upstream_cols, all_gates,
            (kept_h, kept_g, kept_u), weights, first, groups, routed_grads, beside, collective,
        )
        routed_grads[:] = made[:3]
        return made[3:]

    def summed(rows, got):
        return mine(rows).astype(F32) + jnp.sum(got.astype(F32), axis=0)

    query_grad, grad_latent_up, latent_part = attention_backward(
        queries, latents, latent_up, key_ids, query_ids, attended, output_grad, output_weight, lse, even, odd
    )
    grad_output = tn(attended, output_grad).astype(BF)
    grad_query = tn(attention_input, query_grad).astype(BF)
    query_part = nt(query_grad, query_weight)
    latent_part, grad_query, query_part = lax.optimization_barrier(
        (latent_part, grad_query, query_part)
    )
    (compressed_grad,) = piece(0, 2, LineSum(latent_part), 5)
    _, latent_factor = norm_rows(latent_raw, latent_gain)
    latent_grad, grad_latent_gain = norm_back(
        latent_raw, latent_factor, latent_gain, compressed_grad[:, :KVL]
    )
    down_grad = jnp.concatenate(
        [latent_grad, rotate(compressed_grad[:, KVL : KVL + RD], cosine, -sine_table)], axis=1
    ).astype(BF)
    attention_grad = query_part + nt(down_grad, latent_down)
    rows_float = tokens.astype(F32)
    _, first_factor = norm_rows(rows_float, first_gain)
    grad_first_gain = jnp.sum(attention_grad * rows_float * first_factor, axis=0)
    attention_grad = attention_grad.astype(BF)
    grad_latent_down = lax.psum_scatter(
        tn(attention_input, down_grad).astype(BF), DP, scatter_dimension=0, tiled=True
    )
    grad_query, grad_latent_up, grad_output, got, got_result = piece(
        2,
        steps - 4,
        Beside(
            LineSpread([(grad_query, 0), (grad_latent_up, 0), (grad_output, 1)]),
            Many([Scatter(attention_grad), Scatter(expert_part)]),
        ),
        6,
    )
    token_back, _ = norm_back(
        token_quarter.astype(F32), mine(first_factor), first_gain, summed(attention_grad, got)
    )
    *shared_grads, token_grad, result = piece(
        steps - 2,
        2,
        Many(
            [
                Gather((token_back + residual_grad).astype(BF)),
                Gather((residual + summed(expert_part, got_result)).astype(BF)),
            ]
        ),
        7,
    )
    token_grad, result = token_grad.reshape(count, model), result.reshape(count, model)

    grad_router = lax.dot_general(
        wide_input[:, :model], logit_grad[:EXPERTS].astype(BF), (((0,), (1,)), ((), ())),
        preferred_element_type=F32,
    )

    def over_ranks(array):
        blocks = array.reshape((ranks, -1) + array.shape[1:])

        def block(d):
            return lax.dynamic_index_in_dim(blocks, lax.rem(rank + d, ranks), 0, keepdims=False)

        total = block(0).astype(F32)
        for d in range(1, ranks):
            route = [(i, (i + d) % ranks) for i in range(ranks)]
            total = total + lax.ppermute(block(d), "tensor", route).astype(F32)
        return total

    def for_ranks(gain):
        return jnp.repeat(gain.reshape(2 * chips, -1), ranks, axis=0)

    small = jnp.concatenate(
        [
            grad_router.reshape(devices, -1),
            for_ranks(grad_second_gain),
            for_ranks(grad_first_gain),
            grad_latent_gain.reshape(devices, -1),
        ],
        axis=1,
    )
    small = jnp.pad(small, ((0, 0), (0, -small.shape[1] % 1024)))
    small = lax.psum_scatter(small.reshape(-1, 128), DP, scatter_dimension=0, tiled=True)
    small = over_ranks(small).reshape(-1)
    router_size = model // devices * EXPERTS
    gain_size = model // (2 * chips)
    latent_size = KVL // devices
    grad_router = small[:router_size].reshape(-1, EXPERTS)
    small = small[router_size:]

    def routed_of(array):
        return array.reshape(EXPERTS, unit, half).astype(F32)

    return (
        result,
        token_grad,
        small[gain_size : 2 * gain_size],
        grad_query,
        over_ranks(grad_latent_down),
        small[2 * gain_size : 2 * gain_size + latent_size],
        grad_latent_up,
        grad_output,
        small[:gain_size],
        grad_router,
        jnp.swapaxes(routed_of(routed_grads[0]), 1, 2),
        jnp.swapaxes(routed_of(routed_grads[1]), 1, 2),
        routed_of(routed_grads[2]),
        shared_grads[0].astype(F32).T,
        shared_grads[1].astype(F32).T,
        shared_grads[2].astype(F32),
    )


def solution(mesh):
    groups, ranks = mesh.devices.shape
    fine = Mesh(mesh.devices.reshape(groups // 2, 2, ranks), ("dpo", "core", "tensor"))
    in_specs = (
        P(DP, None),
        P(DP, None),
        P(),
        P(DP, None),
        P(),
        P(None, "tensor"),
        P(),
        P(),
        P(None, "tensor"),
        P("tensor", None),
        P(),
        P(),
        P(None, None, "tensor"),
        P(None, None, "tensor"),
        P(None, "tensor", None),
        P(None, "tensor"),
        P(None, "tensor"),
        P("tensor", None),
    )
    out_specs = (
        P(DP, None),
        P(DP, None),
        P(DP),
        P(DP, "tensor"),
        P(ALL, None),
        P(ALL),
        P(DP, "tensor"),
        P("tensor", DP),
        P(DP),
        P(ALL, None),
        P(None, DP, "tensor"),
        P(None, DP, "tensor"),
        P(None, "tensor", DP),
        P(DP, "tensor"),
        P(DP, "tensor"),
        P("tensor", DP),
    )
    return jax.shard_map(shards, mesh=fine, in_specs=in_specs, out_specs=out_specs, check_vma=False)
```

```python
import jax
import jax.numpy as jnp
from jax import lax
from jax.experimental import pallas as pl
from jax.experimental.pallas import tpu as pltpu
from jax.sharding import Mesh
from jax.sharding import PartitionSpec as P

ND = 128
RD = 64
VD = 128
KVL = 512
EXPERTS = 12
LAT = 640
EPSILON = 1e-06
LOG2E = 1.4426950408889634
BF = jnp.bfloat16
F32 = jnp.float32
VMEM_LIMIT = 60 * 1024 * 1024
DP = ("dpo", "core")
ALL = ("dpo", "core", "tensor")
MESH = pl.DeviceIdType.MESH
SHORT = pl.CostEstimate(flops=1000, bytes_accessed=100_000, transcendentals=0)


def nn(former, latter):
    return jnp.dot(former, latter, preferred_element_type=F32)


def nt(former, latter):
    return lax.dot_general(former, latter, (((1,), (1,)), ((), ())), preferred_element_type=F32)


def tn(former, latter):
    return lax.dot_general(former, latter, (((0,), (0,)), ((), ())), preferred_element_type=F32)


def rotary_tables(places):
    halfway = RD // 2
    frequency = 10000.0 ** (-jnp.arange(halfway, dtype=F32) * 2.0 / RD)
    angles = places.astype(F32)[:, None] * frequency[None, :]
    return jnp.cos(angles), jnp.sin(angles)


def rotate(values, cosine, sine_table):
    halfway = values.shape[-1] // 2
    leading = values[..., :halfway]
    trailing = values[..., halfway:]
    return jnp.concatenate(
        [leading * cosine - trailing * sine_table, trailing * cosine + leading * sine_table],
        axis=-1,
    )


def norm_rows(values, gain_row):
    factor = lax.rsqrt(jnp.mean(values * values, axis=-1, keepdims=True) + EPSILON)
    return values * factor * gain_row, factor


def norm_back(values, factor, gain_row, upstream):
    weighted = upstream * gain_row
    common = jnp.mean(weighted * values, axis=-1, keepdims=True)
    return (
        factor * weighted - values * factor * factor * factor * common,
        jnp.sum(upstream * values * factor, axis=0),
    )


def expert_unit(gate_pre, up_pre, hidden_grad, gate):
    sigmoid = 0.5 * jnp.tanh(0.5 * gate_pre) + 0.5
    silu = gate_pre * sigmoid
    hidden = silu * up_pre
    scaled = gate * hidden_grad
    d_up = scaled * silu
    d_gate = scaled * up_pre * (sigmoid + silu - silu * sigmoid)
    return (
        (gate * hidden).astype(BF),
        d_gate.astype(BF),
        d_up.astype(BF),
        hidden * hidden_grad,
    )


def weight_copies(routed, shared, held, sems, step, slot, steps, width, begin):
    def each(refs):
        for i, ref in enumerate(refs):
            copy = pltpu.make_async_copy(
                ref, held.at[slot, pl.ds(i * width, width)], sems.at[slot, i]
            )
            if begin:
                copy.start()
            else:
                copy.wait()

    @pl.when(step < steps - 1)
    def _():
        rows = pl.ds(pl.multiple_of(step * width, width), width)
        each([ref.at[rows] for ref in routed])

    @pl.when(step == steps - 1)
    def _():
        each(shared)


def gate_rows(gates, width):
    parts, columns = gates.shape
    return jnp.concatenate(
        [jnp.broadcast_to(gates[i : i + 1], (width // parts, columns)) for i in range(parts)],
        axis=0,
    )


def own_experts(rows, products_back, router_rows, weights):
    steps, _, width, count = products_back.shape
    model = rows.shape[1] - 128
    parts = EXPERTS // (steps - 1)
    unit = width // parts
    wide = 512

    def kernel(x_ref, tail_ref, b_ref, router_ref, gw, uw, dw, sg, su, sd, out_low, back_low, kept_h, kept_g, kept_u, lg_ref,
               held, sems, out, back, gates, router, dots):
        step = pl.program_id(0)
        slot = lax.rem(step, 2)
        routed, shared = (gw, uw, dw), (sg, su, sd)

        @pl.when(step == 0)
        def _():
            weight_copies(routed, shared, held, sems, step, slot, steps, width, True)
            out[...] = jnp.zeros_like(out)
            back[...] = jnp.zeros_like(back)
            tail = tail_ref[...].astype(F32).T
            for p in range(steps):
                gates[p] = tail[p * parts : (p + 1) * parts]
            router[...] = tail[16:32]

        weight_copies(routed, shared, held, sems, step, slot, steps, width, False)

        @pl.when(step < steps - 1)
        def _():
            weight_copies(routed, shared, held, sems, step + 1, 1 - slot, steps, width, True)

        both = nt(held[slot, : 2 * width], x_ref[...])
        hidden, d_gate, d_up, products = expert_unit(
            both[:width], both[width:], b_ref[0, 0].astype(F32), gate_rows(gates[step], width)
        )
        kept_h[0] = hidden
        kept_g[0] = d_gate
        kept_u[0] = d_up
        dots[step] = jnp.concatenate(
            [
                jnp.sum(products[i * unit : (i + 1) * unit], axis=0, keepdims=True)
                for i in range(parts)
            ],
            axis=0,
        )
        turned = hidden.T
        turned_back = jnp.concatenate([d_gate, d_up], axis=0).T
        for at in range(0, model, wide):
            columns = slice(at, at + wide)
            out[:, columns] += nn(turned, held[slot, 2 * width :, columns])
            back[:, columns] += nn(turned_back, held[slot, : 2 * width, columns])

        @pl.when(step == steps - 1)
        def _():
            out_low[...] = out[...].astype(BF)
            spare = jnp.zeros((16 - EXPERTS, count), F32)
            pair_grad = jnp.concatenate([dots[p] for p in range(steps - 1)] + [spare], axis=0)
            named = jnp.concatenate([gates[p] for p in range(steps - 1)] + [spare], axis=0) > 0
            pair_grad = jnp.where(named, pair_grad, 0.0)
            odds = router[...]
            logit_grad = odds * (pair_grad - jnp.sum(odds * pair_grad, axis=0, keepdims=True))
            lg_ref[...] = logit_grad
            turned_logits = logit_grad.T.astype(BF)
            for at in range(0, model, wide):
                columns = slice(at, at + wide)
                back_low[:, columns] = (
                    back[:, columns] + nn(turned_logits, router_ref[:, columns])
                ).astype(BF)

    def whole(shape):
        return pl.BlockSpec(shape, lambda p: (0,) * len(shape), pipeline_mode=pl.Buffered(1))

    def one(shape):
        return pl.BlockSpec((1,) + shape, lambda p: (p, 0, 0))

    kept = jax.ShapeDtypeStruct((steps, width, count), BF)
    total = jax.ShapeDtypeStruct((count, model), BF)
    return pl.pallas_call(
        kernel,
        name="own_experts",
        grid=(steps,),
        in_specs=[
            whole((count, model)),
            pl.BlockSpec((count, 128), lambda p: (0, model // 128), pipeline_mode=pl.Buffered(1)),
            pl.BlockSpec((1, 1, width, count), lambda p: (p, 0, 0, 0)),
            whole((16, model)),
        ]
        + [pl.BlockSpec(memory_space=pl.ANY)] * 6,
        out_specs=[whole((count, model))] * 2 + [one((width, count))] * 3 + [whole((16, count))],
        out_shape=[total, total, kept, kept, kept, jax.ShapeDtypeStruct((16, count), F32)],
        scratch_shapes=[
            pltpu.VMEM((2, 3 * width, model), BF),
            pltpu.SemaphoreType.DMA((2, 3)),
            pltpu.VMEM((count, model), F32),
            pltpu.VMEM((count, model), F32),
            pltpu.VMEM((steps, parts, count), F32),
            pltpu.VMEM((16, count), F32),
            pltpu.VMEM((steps, parts, count), F32),
        ],
        cost_estimate=SHORT,
        compiler_params=pltpu.CompilerParams(
            vmem_limit_bytes=VMEM_LIMIT, dimension_semantics=("arbitrary",)
        ),
    )(rows, rows, products_back, router_rows, *weights)


def ring_of(axis):
    here = lax.axis_index(axis)
    size = lax.axis_size(axis)
    return here, [lax.rem(here + i, size) for i in range(size)]


def greet(friends):
    barrier = pltpu.get_barrier_semaphore()
    total = 0
    for device, present in friends.values():
        if present is None:
            pl.semaphore_signal(barrier, inc=1, device_id=device, device_id_type=MESH)
            total = total + 1
            continue

        @pl.when(present)
        def _():
            pl.semaphore_signal(barrier, inc=1, device_id=device, device_id_type=MESH)

        total = total + jnp.where(present, 1, 0)
    pl.semaphore_wait(barrier, total)


def mate_friend():
    return {"mate": ({"core": 1 - lax.axis_index("core")}, None)}


def rank_friends():
    _, peers = ring_of("tensor")
    return {f"rank{d}": ({"tensor": peer}, None) for d, peer in enumerate(peers) if d}


def line_friends():
    chip, chips = lax.axis_index("dpo"), lax.axis_size("dpo")
    return {
        "left": ({"dpo": lax.rem(chip + chips - 1, chips)}, chip > 0),
        "right": ({"dpo": lax.rem(chip + 1, chips)}, chip < chips - 1),
    }


def remote(source, target, send, receive, device):
    return pltpu.make_async_remote_copy(
        src_ref=source, dst_ref=target, send_sem=send, recv_sem=receive,
        device_id=device, device_id_type=MESH,
    )


class Scatter:
    def __init__(self, rows):
        ranks = lax.axis_size("tensor")
        quarter = rows.shape[0] // ranks
        self.ins = [rows.reshape(ranks, quarter, rows.shape[1])]
        self.in_specs = [pl.BlockSpec(memory_space=pl.ANY)]
        self.outs = [jax.ShapeDtypeStruct((ranks - 1, quarter, rows.shape[1]), rows.dtype)]
        self.out_specs = [pl.BlockSpec(memory_space=pl.ANY)]
        self.scratch = [pltpu.SemaphoreType.DMA((ranks,)), pltpu.SemaphoreType.DMA((ranks,))]

    def copies(self, refs):
        source, target, sends, receives = refs
        _, peers = ring_of("tensor")
        return [
            remote(source.at[peer], target.at[d - 1], sends.at[d], receives.at[d], {"tensor": peer})
            for d, peer in enumerate(peers)
            if d
        ]

    def friends(self):
        return rank_friends()

    def begin(self, refs):
        for copy in self.copies(refs):
            copy.start()

    def middle(self, refs, step, last):
        pass

    def end(self, refs):
        for copy in self.copies(refs):
            copy.wait()


class Gather(Scatter):
    def __init__(self, rows):
        ranks = lax.axis_size("tensor")
        self.ins = [rows]
        self.in_specs = [pl.BlockSpec(memory_space=pl.ANY)]
        self.outs = [jax.ShapeDtypeStruct((ranks,) + rows.shape, rows.dtype)]
        self.out_specs = [pl.BlockSpec(memory_space=pl.ANY)]
        self.scratch = [pltpu.SemaphoreType.DMA((ranks,)), pltpu.SemaphoreType.DMA((ranks,))]

    def copies(self, refs):
        source, target, sends, receives = refs
        rank, peers = ring_of("tensor")
        return [pltpu.make_async_copy(source, target.at[rank], sends.at[0])] + [
            remote(source, target.at[rank], sends.at[d], receives.at[d], {"tensor": peer})
            for d, peer in enumerate(peers)
            if d
        ]


class Many(Scatter):
    def __init__(self, transfers):
        self.transfers = transfers
        self.ins = [x for t in transfers for x in t.ins]
        self.in_specs = [x for t in transfers for x in t.in_specs]
        self.outs = [x for t in transfers for x in t.outs]
        self.out_specs = [x for t in transfers for x in t.out_specs]
        self.scratch = [x for t in transfers for x in t.scratch]

    def copies(self, refs):
        n = len(self.transfers)
        copies = []
        for i, t in enumerate(self.transfers):
            own = [refs[i], refs[n + i], refs[2 * n + 2 * i], refs[2 * n + 2 * i + 1]]
            copies += t.copies(own)
        return copies


class LineSum:
    def __init__(self, blocks):
        chips = lax.axis_size("dpo")
        self.chips = chips
        shape = blocks.shape[1:]
        self.rows = shape[0] // 2
        self.ins = [blocks]
        self.in_specs = [pl.BlockSpec(memory_space=pl.ANY)]
        self.outs = [jax.ShapeDtypeStruct(shape, F32)]
        self.out_specs = [pl.BlockSpec(shape, lambda *_: (0, 0), pipeline_mode=pl.Buffered(1))]
        self.scratch = [
            pltpu.VMEM((chips,) + shape, blocks.dtype),
            pltpu.VMEM((chips,) + shape, blocks.dtype),
            pltpu.VMEM(shape, blocks.dtype),
        ] + [pltpu.SemaphoreType.DMA((chips, 2))] * 4 + [pltpu.SemaphoreType.DMA((2,))]

    def friends(self):
        return line_friends()

    def part(self, s):
        return pl.ds(s * self.rows, self.rows)

    def swap(self, refs, i, s):
        source, _, mate, _, _, sends, receives, _, _, _ = refs
        core = lax.axis_index("core")
        return remote(
            source.at[2 * i + 1 - core, self.part(s)], mate.at[i, self.part(s)],
            sends.at[i, s], receives.at[i, s], {"core": 1 - core},
        )

    def onward(self, refs, i, s):
        _, _, mate, inbox, _, _, _, sends, receives, _ = refs
        left = lax.rem(lax.axis_index("dpo") + self.chips - 1, self.chips)
        return remote(
            mate.at[i, self.part(s)], inbox.at[i, self.part(s)], sends.at[i, s], receives.at[i, s], {"dpo": left}
        )

    def begin(self, refs):
        chip = lax.axis_index("dpo")
        for i in range(self.chips):
            @pl.when(i <= chip)
            def _():
                for s in range(2):
                    self.swap(refs, i, s).start()

    def middle(self, refs, step, last):
        source, out, mate, inbox, mine, _, _, _, _, sems = refs
        chip, core = lax.axis_index("dpo"), lax.axis_index("core")
        for i in range(self.chips):
            for s in range(2):
                self.one(refs, step, last, i, s)

    def one(self, refs, step, last, i, s):
        source, out, mate, inbox, mine, _, _, _, _, sems = refs
        chip, core = lax.axis_index("dpo"), lax.axis_index("core")
        part = self.part(s)
        due = 1 + 2 * (self.chips - 1 - chip) + 2 * i + s
        local = pltpu.make_async_copy(source.at[2 * i + core, part], mine.at[part], sems.at[s])

        @pl.when((i <= chip) & (step == due - 1) & (due <= last))
        def _():
            local.start()

        @pl.when((i <= chip) & (step == jnp.minimum(due, last)))
        def _():
            @pl.when(due > last)
            def _():
                local.start()

            self.swap(refs, i, s).wait()
            local.wait()

            @pl.when(chip == self.chips - 1)
            def _():
                mate[i, part] = (mate[i, part].astype(F32) + mine[part].astype(F32)).astype(mate.dtype)

            @pl.when(chip < self.chips - 1)
            def _():
                self.onward(refs, i, s).wait_recv()
                mate[i, part] = (
                    mate[i, part].astype(F32) + mine[part].astype(F32) + inbox[i, part].astype(F32)
                ).astype(mate.dtype)

            @pl.when(chip > i)
            def _():
                self.onward(refs, i, s).start()

            @pl.when(chip == i)
            def _():
                out[part] = mate[i, part].astype(F32)

    def end(self, refs):
        chip = lax.axis_index("dpo")
        for i in range(self.chips):
            @pl.when(chip > i)
            def _():
                for s in range(2):
                    self.onward(refs, i, s).wait_send()


class LineFlow:
    def __init__(self, arrays, rightward, first, hop):
        chips = lax.axis_size("dpo")
        self.chips, self.rightward, self.first, self.hop = chips, rightward, first, hop
        self.dimensions = [d for _, d in arrays]
        self.shapes = [
            tuple(n // (2 * chips) if i == d else n for i, n in enumerate(a.shape)) for a, d in arrays
        ]
        n = len(arrays)
        self.ins = [a for a, _ in arrays]
        self.in_specs = [pl.BlockSpec(memory_space=pl.ANY)] * n
        self.outs = [jax.ShapeDtypeStruct(shape, BF if rightward else F32) for shape in self.shapes]
        self.out_specs = [
            pl.BlockSpec(shape, lambda *_: (0, 0), pipeline_mode=pl.Buffered(1)) for shape in self.shapes
        ]
        self.scratch = []
        for shape in self.shapes:
            self.scratch += [
                pltpu.VMEM((chips,) + shape, BF),
                pltpu.VMEM((chips,) + shape, BF),
                pltpu.VMEM(shape, BF),
            ]
        self.scratch += [pltpu.SemaphoreType.DMA((n, chips))] * 4 + [pltpu.SemaphoreType.DMA((n,))]

    def friends(self):
        return line_friends()

    def parts(self, refs):
        n = len(self.shapes)
        buffers = refs[2 * n : 5 * n]
        return [(refs[j], refs[n + j]) + tuple(buffers[3 * j : 3 * j + 3]) for j in range(n)], refs[5 * n :]

    def block(self, j, source, place):
        size = self.shapes[j][self.dimensions[j]]
        part = pl.ds(pl.multiple_of(place * size, size), size)
        return source.at[part] if self.dimensions[j] == 0 else source.at[:, part]

    def distance(self, i):
        chip = lax.axis_index("dpo")
        return i - chip if self.rightward else chip - i

    def swap(self, refs, i, j):
        parts, sems = self.parts(refs)
        source, _, mate, _, _ = parts[j]
        core = lax.axis_index("core")
        return remote(
            self.block(j, source, 2 * i + 1 - core), mate.at[i], sems[0].at[j, i], sems[1].at[j, i],
            {"core": 1 - core},
        )

    def onward(self, refs, i, j):
        parts, sems = self.parts(refs)
        _, _, mate, inbox, _ = parts[j]
        step = 1 if self.rightward else self.chips - 1
        to = lax.rem(lax.axis_index("dpo") + step, self.chips)
        return remote(mate.at[i], inbox.at[i], sems[2].at[j, i], sems[3].at[j, i], {"dpo": to})

    def begin(self, refs):
        for i in range(self.chips):
            @pl.when(self.distance(i) >= (1 if self.rightward else 0))
            def _():
                for j in range(len(self.shapes)):
                    self.swap(refs, i, j).start()

    def middle(self, refs, step, last):
        order = range(self.chips - 1, -1, -1) if self.rightward else range(self.chips)
        for i in order:
            for j in range(len(self.shapes)):
                self.one(refs, step, last, i, j)

    def one(self, refs, step, last, i, j):
        chip, core = lax.axis_index("dpo"), lax.axis_index("core")
        parts, sems = self.parts(refs)
        source, out, mate, inbox, mine = parts[j]
        end = self.chips - 1
        away = self.distance(i)
        begins = chip == (0 if self.rightward else end)
        adds = away >= (1 if self.rightward else 0)
        due = self.first + self.hop * (end - away) + min(j, 1)
        ahead = pltpu.make_async_copy(self.block(j, source, 2 * i + core), mine, sems[4].at[j])

        @pl.when(adds & (step == due - 1) & (due <= last))
        def _():
            ahead.start()

        @pl.when(adds & (step == jnp.minimum(due, last)))
        def _():
            @pl.when(due > last)
            def _():
                ahead.start()

            self.swap(refs, i, j).wait()
            ahead.wait()

            @pl.when(begins)
            def _():
                mate[i] = (mate[i].astype(F32) + mine[...].astype(F32)).astype(BF)

        @pl.when((away >= 0) & (step == jnp.minimum(due, last)))
        def _():
            @pl.when(jnp.logical_not(begins))
            def _():
                self.onward(refs, i, j).wait_recv()

            @pl.when(jnp.logical_not(begins) & adds)
            def _():
                mate[i] = (
                    mate[i].astype(F32) + mine[...].astype(F32) + inbox[i].astype(F32)
                ).astype(BF)

            @pl.when(away > 0)
            def _():
                self.onward(refs, i, j).start()

            @pl.when(away == 0)
            def _():
                if not self.rightward:
                    out[...] = mate[i].astype(F32)
                    return

                @pl.when(begins)
                def _():
                    out[...] = jnp.zeros_like(out)

                @pl.when(jnp.logical_not(begins))
                def _():
                    out[...] = inbox[i]

    def end(self, refs):
        for i in range(self.chips):
            @pl.when(self.distance(i) > 0)
            def _():
                for j in range(len(self.shapes)):
                    self.onward(refs, i, j).wait_send()


class Beside:
    def __init__(self, former, latter):
        self.pair = (former, latter)
        self.ins = former.ins + latter.ins
        self.in_specs = former.in_specs + latter.in_specs
        self.outs = former.outs + latter.outs
        self.out_specs = former.out_specs + latter.out_specs
        self.scratch = former.scratch + latter.scratch

    def split(self, refs):
        refs = list(refs)
        lists = ([], [])
        for name in ("ins", "outs", "scratch"):
            for t, held in zip(self.pair, lists):
                n = len(getattr(t, name))
                held += refs[:n]
                del refs[:n]
        return zip(self.pair, lists)

    def friends(self):
        return {**self.pair[0].friends(), **self.pair[1].friends()}

    def begin(self, refs):
        for t, held in self.split(refs):
            t.begin(held)

    def middle(self, refs, step, last):
        for t, held in self.split(refs):
            t.middle(held, step, last)

    def end(self, refs):
        for t, held in self.split(refs):
            t.end(held)


class DownProducts:
    def __init__(self, upstream, count, block_of, down, shared_down):
        _, rows, model = upstream.shape
        self.width = shared_down.shape[0]
        self.steps = down.shape[0] // self.width + 1
        self.count, self.block_of, self.units = count, block_of, self.steps * count
        self.ins = [upstream, down, shared_down]
        self.outs = [jax.ShapeDtypeStruct((self.steps, count, self.width, rows), BF)]
        self.scratch = [
            pltpu.VMEM((2, self.width, model), BF),
            pltpu.VMEM((count, rows, model), BF),
            pltpu.VMEM((2, self.width, rows), BF),
            pltpu.SemaphoreType.DMA((2, 1)),
            pltpu.SemaphoreType.DMA((count,)),
            pltpu.SemaphoreType.DMA((2,)),
        ]

    def load(self, refs, step, begin):
        _, down, shared, _, held, _, _, sems, _, _ = refs
        weight_copies((down,), (shared,), held, sems, step, lax.rem(step, 2), self.steps, self.width, begin)

    def block(self, refs, i):
        source, _, _, _, _, rows, _, _, sems, _ = refs
        return pltpu.make_async_copy(source.at[self.block_of(i)], rows.at[i], sems.at[i])

    def put(self, refs, unit):
        out, stage, sems = refs[3], refs[6], refs[9]
        slot = lax.rem(unit, 2)
        return pltpu.make_async_copy(
            stage.at[slot], out.at[unit // self.count, lax.rem(unit, self.count)], sems.at[slot]
        )

    def begin(self, refs):
        self.load(refs, 0, True)
        for i in range(self.count):
            self.block(refs, i).start()

    def run(self, refs, first, last):
        held, rows, stage = refs[4], refs[5], refs[6]

        def one(unit, carry):
            step, i = unit // self.count, lax.rem(unit, self.count)

            @pl.when(i == 0)
            def _():
                self.load(refs, step, False)

                @pl.when(step < self.steps - 1)
                def _():
                    self.load(refs, step + 1, True)

            @pl.when(step == 0)
            def _():
                self.block(refs, i).wait()

            @pl.when(unit >= 2)
            def _():
                self.put(refs, unit - 2).wait()

            stage[lax.rem(unit, 2)] = nt(held[lax.rem(step, 2)], rows[i]).astype(BF)
            self.put(refs, unit).start()
            return carry

        lax.fori_loop(first, last, one, 0)

    def end(self, refs):
        for unit in (self.units - 2, self.units - 1):
            self.put(refs, unit).wait()


def settle(part, more, finish, extra, wide, fill, splits, collective):
    count, model = part[0].shape[0], part[-1].shape[1]
    ranks = lax.axis_size("tensor")
    quarter = count // ranks
    size = quarter // 2
    n_part, n_more, n_extra = len(part), len(more), len(extra)

    def kernel(*refs):
        refs = list(refs)

        def take(n):
            taken = refs[:n]
            del refs[:n]
            return taken

        part_refs, more_refs = take(n_part), take(n_more)
        fill_refs = take(len(fill.ins))
        (out_ref,), extra_refs = take(1), take(n_extra)
        fill_refs += take(len(fill.outs))
        inbox, block, gathered, send, receive, send_on, receive_on = take(7)
        fill_refs += take(len(fill.scratch))
        part_ref = refs[0] if refs else part_refs[0]
        rank, peers = ring_of("tensor")

        def rows_of(i, s):
            return pl.ds(pl.multiple_of(i * quarter + s * size, size), size)

        fill.begin(fill_refs)
        greet(rank_friends())
        first, then = [[], []], [[], []]
        for s in range(2):
            own = pl.ds(s * size, size)
            for d, peer in enumerate(peers):
                rows = rows_of(peer, s)
                if n_part == 2:
                    part_ref[rows] = nn(part_refs[0][rows], part_refs[1][...]).astype(BF)
                if d:
                    first[s].append(
                        remote(part_ref.at[rows], inbox.at[d, own], send.at[s, d], receive.at[s, d], {"tensor": peer})
                    )
                    first[s][-1].start()
                    then[s].append(
                        remote(block.at[own], gathered.at[d, own], send_on.at[s, d], receive_on.at[s, d], {"tensor": peer})
                    )
        for s in range(2):
            own = pl.ds(s * size, size)
            rows = rows_of(rank, s)
            fill.run(fill_refs, splits[s], splits[s + 1])
            total = part_ref[rows].astype(F32)
            for d, copy in enumerate(first[s]):
                copy.wait()
                total = total + inbox[d + 1, own].astype(F32)
            results = finish(
                total,
                [
                    r[rows] if r.shape[0] == count else r[own] if r.shape[0] == quarter else r[...]
                    for r in more_refs
                ],
            )
            for ref, value in zip(extra_refs, results):
                if ref.shape[0] > 1:
                    ref[own] = value
                elif s:
                    ref[...] += value
                else:
                    ref[...] = value
            block[own] = results[-1]
            for copy in then[s]:
                copy.start()
            out_ref[rows] = block[own]
        fill.run(fill_refs, splits[2], fill.units)
        fill.end(fill_refs)
        for s in range(2):
            for d, copy in enumerate(then[s]):
                copy.wait()
                out_ref[rows_of(lax.rem(rank + ranks - d - 1, ranks), s)] = gathered[d + 1, pl.ds(s * size, size)]

    vmem = pl.BlockSpec(memory_space=pltpu.VMEM)
    anywhere = pl.BlockSpec(memory_space=pl.ANY)
    sems = [pltpu.SemaphoreType.DMA((2, ranks))] * 4
    return pl.pallas_call(
        kernel,
        name="settle",
        in_specs=[vmem] * (n_part + n_more) + [anywhere] * len(fill.ins),
        out_specs=[vmem] * (1 + n_extra) + [anywhere] * len(fill.outs),
        out_shape=[jax.ShapeDtypeStruct((count, wide), BF)] + extra + fill.outs,
        scratch_shapes=[
            pltpu.VMEM((ranks, quarter, model), BF),
            pltpu.VMEM((quarter, wide), BF),
            pltpu.VMEM((ranks, quarter, wide), BF),
        ]
        + sems
        + fill.scratch
        + ([pltpu.VMEM((count, model), BF)] if n_part == 2 else []),
        cost_estimate=SHORT,
        compiler_params=pltpu.CompilerParams(
            vmem_limit_bytes=VMEM_LIMIT, collective_id=collective, has_side_effects=True
        ),
    )(*part, *more, *fill.ins)


def group_gradients(rows, upstream, products_back, gates, kept, weights, first, groups, held_back, beside, collective):
    chips, count, model = upstream.shape
    steps, _, parts, _ = gates.shape
    width = weights[3].shape[0]
    half = model // (2 * chips)
    unit = width // 2
    weights = weights[:2] + weights[3:5]
    n_ins, n_outs = len(beside.ins), len(beside.outs)
    last = groups * chips - 1
    ends, routes = first + groups == steps, first < steps - 1
    held_back = held_back if routes else []
    n_held = len(held_back)

    def kernel(*refs):
        refs = list(refs)

        def take(n):
            taken = refs[:n]
            del refs[:n]
            return taken

        x_ref, xc, cc, b_ref, g_ref, kept_h, kept_g, kept_u = take(8)
        routed, shared = take(2), take(2)
        take(n_held)
        link_refs = take(n_ins)
        outs = take(3) if routes else None
        shared_outs = take(3) if ends else None
        link_refs += take(n_outs)
        held, sems, sum_g, sum_u, sum_d, outbox, inbox, sends, receives = take(9)
        link_refs += refs
        at_group = pl.program_id(0)
        turn = pl.program_id(1)
        step = at_group + first
        slot = lax.rem(at_group, 2)
        tick = at_group * chips + turn
        sums = (sum_g, sum_u, sum_d)
        core = lax.axis_index("core")

        def columns_of(i):
            return pl.ds(pl.multiple_of(i * half, half), half)

        def swap(i):
            part = pl.ds(i * unit, unit)
            return remote(
                outbox.at[:, part], inbox.at[slot, :, part], sends.at[slot, i], receives.at[slot, i],
                {"core": 1 - lax.axis_index("core")},
            )

        @pl.when(tick == 0)
        def _():
            greet({**mate_friend(), **beside.friends()})
            beside.begin(link_refs)

        @pl.when(turn == 0)
        def _():
            @pl.when(at_group == 0)
            def _():
                weight_copies(routed, shared, held, sems, step, slot, steps, width, True)

            sum_g[...] = nn(kept_g[0], xc[0])
            sum_u[...] = nn(kept_u[0], xc[0])
            sum_d[...] = nn(kept_h[0], cc[0])
            weight_copies(routed, shared, held, sems, step, slot, steps, width, False)

            @pl.when(at_group < groups - 1)
            def _():
                weight_copies(routed, shared, held, sems, step + 1, 1 - slot, steps, width, True)

        def work(final):
            x = x_ref[0]
            gate = gate_rows(g_ref[0, 0], width)
            parts_ = [slice(i * unit, (i + 1) * unit) for i in range(2)]
            pre = [
                (nt(held[slot, part], x), nt(held[slot, width + part.start : width + part.stop], x))
                for part in parts_
            ]
            terms = []
            for part, (gate_pre, up_pre) in zip(parts_, pre):
                hidden, d_gate, d_up, _ = expert_unit(
                    gate_pre, up_pre, b_ref[0, 0, part].astype(F32), gate[part]
                )
                terms.append(((d_gate, xc), (d_up, xc), (hidden, cc)))
                if not final:
                    for total, (term, columns) in zip(sums, terms[-1]):
                        total[part] += nn(term, columns[0])
            if not final:
                return
            far, near = columns_of(1 - core), columns_of(core)
            for i, part in enumerate(parts_):
                for j, (total, (term, columns)) in enumerate(zip(sums, terms[i])):
                    outbox[j, part] = (total[part, far] + nn(term, columns[0, :, far])).astype(BF)
                swap(i).start()
            for part, made in zip(parts_, terms):
                for total, (term, columns) in zip(sums, made):
                    total[part, near] += nn(term, columns[0, :, near])

        @pl.when((turn > 0) & (turn < chips - 1))
        def _():
            work(False)

        @pl.when(turn == chips - 1)
        def _():
            work(True)
            for i in range(2):
                swap(i).wait()
                part = slice(i * unit, (i + 1) * unit)
                for j, total in enumerate(sums):
                    value = (total[part, columns_of(core)] + inbox[slot, j, part].astype(F32)).astype(BF)
                    if not ends:
                        outs[j][part] = value
                        continue

                    if routes:
                        @pl.when(step < steps - 1)
                        def _():
                            outs[j][part] = value

                    @pl.when(step == steps - 1)
                    def _():
                        shared_outs[j][part] = value

        beside.middle(link_refs, tick, last)

        @pl.when(tick == last)
        def _():
            beside.end(link_refs)

    def chip_at(turn):
        return lax.rem(lax.axis_index("dpo") + turn, chips)

    def at_chip(shape):
        return pl.BlockSpec((1,) + shape, lambda p, k: (chip_at(k), 0, 0))

    def one(shape):
        return pl.BlockSpec((1,) + shape, lambda p, k: (p + first, 0, 0))

    columns = pl.BlockSpec((1, count, 2 * half), lambda p, k: (chip_at(k), 0, lax.axis_index("dpo")))

    anywhere = pl.BlockSpec(memory_space=pl.ANY)
    block = pl.BlockSpec((width, half), lambda p, k: (jnp.minimum(p + first, steps - 2), 0))
    shared_block = pl.BlockSpec((width, half), lambda p, k: (0, 0))
    return pl.pallas_call(
        kernel,
        name="group_gradients",
        grid_spec=pltpu.PrefetchScalarGridSpec(
            num_scalar_prefetch=0,
            grid=(groups, chips),
            in_specs=[at_chip((count, model))]
            + [columns] * 2
            + [pl.BlockSpec((1, 1, width, count), lambda p, k: (p + first, jnp.maximum(k - 1, 0), 0, 0))]
            + [pl.BlockSpec((1, 1, parts, count), lambda p, k: (p + first, chip_at(k), 0, 0))]
            + [one((width, count))] * 3
            + [anywhere] * (4 + n_held)
            + beside.in_specs,
            out_specs=([block] * 3 if routes else []) + ([shared_block] * 3 if ends else []) + beside.out_specs,
            scratch_shapes=[
                pltpu.VMEM((2, 2 * width, model), BF),
                pltpu.SemaphoreType.DMA((2, 2)),
            ]
            + [pltpu.VMEM((width, 2 * half), F32)] * 3
            + [
                pltpu.VMEM((3, width, half), BF),
                pltpu.VMEM((2, 3, width, half), BF),
                pltpu.SemaphoreType.DMA((2, 2)),
                pltpu.SemaphoreType.DMA((2, 2)),
            ]
            + beside.scratch,
        ),
        out_shape=([jax.ShapeDtypeStruct(((steps - 1) * width, half), BF)] * 3 if routes else [])
        + ([jax.ShapeDtypeStruct((width, half), BF)] * 3 if ends else [])
        + beside.outs,
        input_output_aliases={12 + i: i for i in range(n_held)},
        cost_estimate=pl.CostEstimate(
            flops=groups * 2 * width * count * (2 * (chips - 1) * model + 6 * chips * half),
            bytes_accessed=groups * (6 * width * model + 4 * chips * count * model),
            transcendentals=0,
        ),
        compiler_params=pltpu.CompilerParams(
            vmem_limit_bytes=VMEM_LIMIT,
            dimension_semantics=("arbitrary", "arbitrary"),
            collective_id=collective,
            has_side_effects=True,
        ),
    )(
        rows, rows, upstream, products_back, gates, *kept, *weights, *held_back, *beside.ins,
    )


def turn_pairs(values, even, odd):
    lane = lax.broadcasted_iota(jnp.int32, values.shape, 1)
    other = jnp.where(lane < RD // 2, pltpu.roll(values, 128 - RD // 2, 1), pltpu.roll(values, RD // 2, 1))
    return values * even + other * odd


def attention_forward(tokens, gain, query_weight, latent_rows, latent_gain, latent_up, even, odd, key_ids, query_ids, collective):
    count, model = tokens.shape
    heads = latent_up.shape[1] // 256
    chips = lax.axis_size("dpo")
    ranks = lax.axis_size("tensor")
    quarter = count // ranks
    scale = (ND + RD) ** (-0.5) * LOG2E

    def kernel(x_ref, gain_ref, qw_ref, ld_ref, lg_ref, up_ref, even_ref, odd_ref, kid_ref, qid_ref,
               att_ref, lse_ref, all_ref, in_ref, raw_ref, q_ref, factor_ref, lat_ref, rope_ref, keys, top, low, mix,
               send_right, take_left, send_mate, take_mate, send_rank, take_rank):
        chip, core = lax.axis_index("dpo"), lax.axis_index("core")
        rank, peers = ring_of("tensor")
        place = chip * 2 + core
        right = lax.rem(chip + 1, chips)
        own_rows = pl.ds(pl.multiple_of(rank * quarter, quarter), quarter)
        greet({**mate_friend(), **line_friends(), **rank_friends()})

        def to_right(i):
            return remote(
                all_ref.at[2 * i + core, own_rows], all_ref.at[2 * i + core, own_rows],
                send_right.at[i], take_left.at[i], {"dpo": right},
            )

        def to_mate(i):
            return remote(
                all_ref.at[2 * i + core], all_ref.at[2 * i + core],
                send_mate.at[i], take_mate.at[i], {"core": 1 - core},
            )

        def to_ranks(i):
            return [
                remote(
                    all_ref.at[2 * i + core, own_rows], all_ref.at[2 * i + core, own_rows],
                    send_rank.at[i, d], take_rank.at[i, d], {"tensor": peer},
                )
                for d, peer in enumerate(peers)
                if d
            ]

        x = x_ref[...].astype(F32)
        normed, factor = norm_rows(x, gain_ref[...])
        factor_ref[...] = jnp.broadcast_to(factor, (count, 128))
        in_ref[...] = normed.astype(BF)
        raw = nt(in_ref[...], ld_ref[:KVL])
        raw_ref[...] = raw
        rope_ref[...] = jnp.zeros_like(rope_ref)
        rope_ref[:, :RD] = nt(in_ref[...], ld_ref[KVL:])
        latent, _ = norm_rows(raw, lg_ref[...])
        lat_ref[:, :KVL] = latent.astype(BF)
        lat_ref[:, KVL:] = turn_pairs(rope_ref[...], even_ref[...], odd_ref[...]).astype(BF)
        all_ref[place] = lat_ref[...]

        @pl.when(chip < chips - 1)
        def _():
            to_right(chip).start()

        to_mate(chip).start()
        raw_q = nn(in_ref[...], qw_ref[...])
        lane = lax.broadcasted_iota(jnp.int32, (count, 128), 1)
        for h in range(0, heads, 2):
            at = h * (ND + RD)
            former, between, latter = (raw_q[:, at + i : at + i + 128] for i in (0, 128, 256))
            rolled = pltpu.roll(latter, 64, 1)
            nope = jnp.where(lane < 64, pltpu.roll(between, 64, 1), rolled)
            for i, (plain, rope) in enumerate(((former, between), (nope, rolled))):
                to = (h + i) * 256
                q_ref[:, to : to + ND] = plain.astype(BF)
                q_ref[:, to + ND : to + 256] = turn_pairs(rope, even_ref[...], odd_ref[...]).astype(BF)
        top[...] = jnp.full_like(top, -1e30)
        low[...] = jnp.zeros_like(low)
        mix[...] = jnp.zeros_like(mix)

        def chunk(source, masked):
            lat = source[:, :KVL]
            rope = source[:, KVL:]
            for h in range(heads):
                keys[h, :, ND:] = rope
                both = nn(lat, up_ref[:, h * 256 : (h + 1) * 256]).astype(BF)
                keys[h, :, :ND] = both[:, :ND]
                values = both[:, ND:].T
                scores = nt(keys[h], q_ref[:, h * 256 : (h + 1) * 256]) * scale
                if masked:
                    scores = jnp.where(kid_ref[...] <= qid_ref[...], scores, -1e30)
                before = top[h]
                highest = jnp.maximum(before, jnp.max(scores, axis=0, keepdims=True))
                weights = jnp.exp2(scores - highest)
                decay = jnp.exp2(before - highest)
                top[h] = highest
                low[h] = low[h] * decay + jnp.sum(weights, axis=0, keepdims=True)
                mix[h] = mix[h] * decay + nn(values, weights.astype(BF))

        def intake(i):
            to_right(i).wait_recv()

            @pl.when(chip < chips - 1)
            def _():
                to_right(i).start()

            for copy in to_ranks(i):
                copy.start()

        chunk(lat_ref, True)

        @pl.when(chip > 0)
        def _():
            intake(chip - 1)

        to_mate(chip).wait()

        @pl.when(core == 1)
        def _():
            chunk(all_ref.at[place - 1], False)

        def earlier(i, carry):
            at = chip - 1 - i

            @pl.when(at > 0)
            def _():
                intake(at - 1)

            for copy in to_ranks(at):
                copy.wait_recv()
            to_mate(at).start()
            chunk(all_ref.at[2 * at + core], False)
            to_mate(at).wait_recv()
            chunk(all_ref.at[2 * at + 1 - core], False)
            return carry

        lax.fori_loop(0, chip, earlier, 0)
        for h in range(heads):
            att_ref[:, h * VD : (h + 1) * VD] = (mix[h] / low[h]).T.astype(BF)
            lse_ref[h] = top[h] + jnp.log2(low[h])

        def sent(i, carry):
            to_mate(i).wait_send()
            for copy in to_ranks(i):
                copy.wait_send()
            return carry

        lax.fori_loop(0, chip, sent, 0)

        @pl.when(chip < chips - 1)
        def _():
            def sent_right(i, carry):
                to_right(i).wait_send()
                return carry

            lax.fori_loop(0, chip + 1, sent_right, 0)

    vmem = pl.BlockSpec(memory_space=pltpu.VMEM)
    sems = pltpu.SemaphoreType.DMA((chips,))
    rank_sems = pltpu.SemaphoreType.DMA((chips, ranks))
    return pl.pallas_call(
        kernel,
        name="attention_forward",
        in_specs=[vmem] * 10,
        out_specs=[vmem] * 7,
        out_shape=[
            jax.ShapeDtypeStruct((count, heads * VD), BF),
            jax.ShapeDtypeStruct((heads, 1, count), F32),
            jax.ShapeDtypeStruct((2 * chips, count, LAT), BF),
            jax.ShapeDtypeStruct((count, model), BF),
            jax.ShapeDtypeStruct((count, KVL), F32),
            jax.ShapeDtypeStruct((count, heads * 256), BF),
            jax.ShapeDtypeStruct((count, 128), F32),
        ],
        scratch_shapes=[
            pltpu.VMEM((count, LAT), BF),
            pltpu.VMEM((count, 128), F32),
            pltpu.VMEM((heads, count, 256), BF),
            pltpu.VMEM((heads, 1, count), F32),
            pltpu.VMEM((heads, 1, count), F32),
            pltpu.VMEM((heads, VD, count), F32),
            sems,
            sems,
            sems,
            sems,
            rank_sems,
            rank_sems,
        ],
        cost_estimate=SHORT,
        compiler_params=pltpu.CompilerParams(
            vmem_limit_bytes=VMEM_LIMIT, collective_id=collective, has_side_effects=True
        ),
    )(tokens, gain, query_weight, latent_rows, latent_gain, latent_up, even, odd, key_ids, query_ids)


def attention_backward(queries, latents, latent_up, key_ids, query_ids, attended, output_grad, output_weight, lse, even, odd, rows, query_weight, beside, collective):
    count, model = rows.shape
    heads = queries.shape[1] // 256
    blocks = latents.shape[0]
    factor = (ND + RD) ** (-0.5)
    scale = factor * LOG2E

    def kernel(q_ref, lat_ref, up_ref, kid_ref, qid_ref, att_ref, og_ref, ow_ref, lse_ref, even_ref, odd_ref, in_ref, qw_ref,
               sent_ref, dqw_ref, dow_ref, din_ref, dup_ref, dlat_ref, got_ref, dq_ref, do_ref, delta, keys, dq, dup, dlat,
               send, receive):
        link_refs = [sent_ref, got_ref, send, receive]
        greet(beside.friends())
        beside.begin(link_refs)
        place = lax.axis_index("dpo") * 2 + lax.axis_index("core")
        dq[...] = jnp.zeros_like(dq)
        dup[...] = jnp.zeros_like(dup)
        do_ref[...] = nt(og_ref[...], ow_ref[...]).astype(BF)
        for h in range(heads):
            part = slice(h * VD, (h + 1) * VD)
            products = do_ref[:, part].astype(F32) * att_ref[:, part].astype(F32)
            delta[h] = jnp.sum(products.T, axis=0, keepdims=True)

        def chunk(at, masked):
            lat = lat_ref[at, :, :KVL]
            turned = lat.T
            rope = lat_ref[at, :, KVL:]
            dlat[...] = jnp.zeros_like(dlat)
            for h in range(heads):
                up = up_ref[:, h * 256 : (h + 1) * 256]
                query = q_ref[:, h * 256 : (h + 1) * 256]
                upstream = do_ref[:, h * VD : (h + 1) * VD]
                keys[h, :, ND:] = rope
                both = nn(lat, up).astype(BF)
                keys[h, :, :ND] = both[:, :ND]
                scores = nt(keys[h], query) * scale
                chances = jnp.exp2(scores - lse_ref[h])
                if masked:
                    chances = jnp.where(kid_ref[...] <= qid_ref[...], chances, 0.0)
                chance_grad = nt(both[:, ND:], upstream)
                score_grad = (chances * (chance_grad - delta[h])).astype(BF)
                value_grad = nn(chances.astype(BF), upstream)
                key_grad = nn(score_grad, query) * factor
                dq[h] += nn(keys[h].T, score_grad)
                both_grad = jnp.concatenate([key_grad[:, :ND], value_grad], axis=1).astype(BF)
                dlat[:, :KVL] += nt(both_grad, up)
                dlat[:, KVL:] += key_grad[:, ND:]
                dup[:, h * 256 : (h + 1) * 256] += nn(turned, both_grad)
            dlat_ref[at] = dlat[...].astype(BF)

        lax.fori_loop(0, place, lambda at, carry: (chunk(at, False), carry)[1], 0)
        chunk(place, True)

        def clear(at, carry):
            dlat_ref[at] = jnp.zeros((count, LAT), BF)
            return carry

        lax.fori_loop(place + 1, blocks, clear, 0)
        dup_ref[...] = dup[...].astype(BF)
        lane = lax.broadcasted_iota(jnp.int32, (count, 128), 1)
        for h in range(0, heads, 2):
            plain, ropes = [], []
            for i in range(2):
                back = dq[h + i].T * factor
                plain.append(back[:, :ND])
                ropes.append(turn_pairs(back[:, ND:], even_ref[...], -odd_ref[...]))
            moved = pltpu.roll(plain[1], 64, 1)
            at = h * (ND + RD)
            dq_ref[:, at : at + 128] = plain[0].astype(BF)
            dq_ref[:, at + 128 : at + 256] = jnp.where(lane < 64, ropes[0], moved).astype(BF)
            dq_ref[:, at + 256 : at + 384] = jnp.where(
                lane < 64, moved, pltpu.roll(ropes[1], 64, 1)
            ).astype(BF)
        turned_mix = att_ref[...].T
        for at in range(0, model, 512):
            part = slice(at, at + 512)
            dqw_ref[part] = nn(in_ref[:, part].T, dq_ref[...]).astype(BF)
            dow_ref[:, part] = nn(turned_mix, og_ref[:, part]).astype(BF)
            din_ref[:, part] = nt(dq_ref[...], qw_ref[part]).astype(BF)
        beside.end(link_refs)

    vmem = pl.BlockSpec(memory_space=pltpu.VMEM)
    return pl.pallas_call(
        kernel,
        name="attention_backward",
        in_specs=[vmem] * 13 + beside.in_specs,
        out_specs=[vmem] * 5 + beside.out_specs,
        out_shape=[
            jax.ShapeDtypeStruct(query_weight.shape, BF),
            jax.ShapeDtypeStruct(output_weight.shape, BF),
            jax.ShapeDtypeStruct((count, model), BF),
            jax.ShapeDtypeStruct((KVL, heads * 256), BF),
            jax.ShapeDtypeStruct((blocks, count, LAT), BF),
        ]
        + beside.outs,
        scratch_shapes=[
            pltpu.VMEM((count, heads * (ND + RD)), BF),
            pltpu.VMEM((count, heads * VD), BF),
            pltpu.VMEM((heads, 1, count), F32),
            pltpu.VMEM((heads, count, 256), BF),
            pltpu.VMEM((heads, 256, count), F32),
            pltpu.VMEM((KVL, heads * 256), F32),
            pltpu.VMEM((count, LAT), F32),
        ]
        + beside.scratch,
        cost_estimate=SHORT,
        compiler_params=pltpu.CompilerParams(
            vmem_limit_bytes=VMEM_LIMIT, collective_id=collective, has_side_effects=True
        ),
    )(queries, latents, latent_up, key_ids, query_ids, attended, output_grad, output_weight, lse, even, odd, rows, query_weight,
      *beside.ins)


def latents_back(compressed_grad, raw, latent_gain, even, odd, latent_rows, query_part, tokens, first_factor, rows):
    count, model = tokens.shape
    wide = 512
    lanes = KVL + RD

    def kernel(cg_ref, raw_ref, gain_ref, even_ref, odd_ref, ld_ref, qp_ref, x_ref, ff_ref, in_ref,
               out_ref, dld_ref, lgain_ref, fgain_ref, down):
        @pl.when(pl.program_id(0) == 0)
        def _():
            raw = raw_ref[...]
            factor = lax.rsqrt(jnp.mean(raw * raw, axis=-1, keepdims=True) + EPSILON)
            back, gain_grad = norm_back(raw, factor, gain_ref[...], cg_ref[:, :KVL])
            lgain_ref[...] = gain_grad[None]
            down[:, :KVL] = back.astype(BF)
            down[:, KVL:] = turn_pairs(cg_ref[:, KVL:], even_ref[...], -odd_ref[...])[:, :RD].astype(BF)

        grad = qp_ref[...].astype(F32) + nn(down[...], ld_ref[...])
        out_ref[...] = grad.astype(BF)
        fgain_ref[...] = jnp.sum(grad * x_ref[...].astype(F32) * ff_ref[:, :1], axis=0, keepdims=True)
        dld_ref[...] = nn(in_ref[...].T, down[...]).astype(BF)

    def whole(shape):
        return pl.BlockSpec(shape, lambda p: (0,) * len(shape), pipeline_mode=pl.Buffered(1))

    def columns(size):
        return pl.BlockSpec((size, wide), lambda p: (0, p))

    return pl.pallas_call(
        kernel,
        name="latents_back",
        grid=(model // wide,),
        in_specs=[whole(a.shape) for a in (compressed_grad, raw, latent_gain, even, odd)]
        + [columns(lanes), columns(count), columns(count), whole(first_factor.shape), columns(count)],
        out_specs=[
            columns(count),
            pl.BlockSpec((wide, lanes), lambda p: (p, 0)),
            whole((1, KVL)),
            columns(1),
        ],
        out_shape=[
            jax.ShapeDtypeStruct((count, model), BF),
            jax.ShapeDtypeStruct((model, lanes), BF),
            jax.ShapeDtypeStruct((1, KVL), F32),
            jax.ShapeDtypeStruct((1, model), F32),
        ],
        scratch_shapes=[pltpu.VMEM((count, lanes), BF)],
        cost_estimate=SHORT,
        compiler_params=pltpu.CompilerParams(
            vmem_limit_bytes=VMEM_LIMIT, dimension_semantics=("arbitrary",)
        ),
    )(compressed_grad, raw, latent_gain, even, odd, latent_rows, query_part, tokens, first_factor, rows)


def grouped(gates, steps):
    parts = EXPERTS // (steps - 1)
    gates = gates.reshape((steps - 1, parts) + gates.shape[1:])
    return jnp.concatenate([gates, jnp.ones((1,) + gates.shape[1:], F32)], axis=0)


def shards(
    tokens,
    cotangent,
    block_ids,
    routes,
    first_gain,
    query_weight,
    latent_down,
    latent_gain,
    latent_up,
    output_weight,
    second_gain,
    router_weight,
    gate_weight,
    up_weight,
    down_weight,
    shared_gate,
    shared_up,
    shared_down,
):
    count, model = tokens.shape
    key_count = block_ids.shape[0]
    heads = query_weight.shape[1] // (ND + RD)
    unit = gate_weight.shape[2]
    width = shared_down.shape[0]
    steps = EXPERTS * unit // width + 1
    chips = lax.axis_size("dpo")
    ranks = lax.axis_size("tensor")
    devices = chips * 2 * ranks
    chip, core, rank = lax.axis_index("dpo"), lax.axis_index("core"), lax.axis_index("tensor")
    place = chip * 2 + core
    quarter = count // ranks
    half = model // (2 * chips)
    routed_rows = EXPERTS * unit

    def mine(array):
        return lax.dynamic_slice_in_dim(array, rank * quarter, quarter, 0)

    weights = (
        jnp.swapaxes(gate_weight, 1, 2).reshape(routed_rows, model),
        jnp.swapaxes(up_weight, 1, 2).reshape(routed_rows, model),
        down_weight.reshape(routed_rows, model),
        shared_gate.T,
        shared_up.T,
        shared_down,
    )

    row_start = place * count
    cosine, sine_table = rotary_tables((row_start + jnp.arange(count, dtype=jnp.int32)) % key_count)
    own_blocks = lax.dynamic_slice_in_dim(block_ids, row_start, count, 0)
    rest = jnp.zeros((count, 128 - RD), F32)
    even = jnp.concatenate([cosine, cosine, rest], axis=1)
    odd = jnp.concatenate([-sine_table, sine_table, rest], axis=1)
    key_ids, query_ids = own_blocks[:, None], own_blocks[None, :]
    all_upstream = lax.all_gather(cotangent, "dpo", axis=0, tiled=True)
    attended, lse, latents, attention_input, latent_raw, queries, first_factor = attention_forward(
        tokens, first_gain[None], query_weight, latent_down.T, latent_gain[None], latent_up,
        even, odd, key_ids, query_ids, 1,
    )

    named = jnp.any(
        routes[:, :, None] == jnp.arange(128, dtype=jnp.int32)[None, None, :], axis=1
    )
    named = (named | (jnp.arange(128) >= EXPERTS)[None, :]).astype(F32)
    token_quarter = mine(tokens)
    parts = EXPERTS // (steps - 1)

    def second_norm(total, more):
        rows, gain, router_columns, mask = more
        residual = rows.astype(F32) + total
        normed, _ = norm_rows(residual, gain)
        normed = normed.astype(BF)
        logits = nn(normed, router_columns)
        lane = lax.broadcasted_iota(jnp.int32, logits.shape, 1)
        first = lane < EXPERTS
        logits = jnp.where(first | ((lane >= 16) & (lane < 16 + EXPERTS)), logits, -1e30)
        odds = jnp.exp(logits - jnp.max(logits, axis=1, keepdims=True))
        odds = odds / jnp.sum(jnp.where(first, odds, 0.0), axis=1, keepdims=True)
        gates = jnp.where((lane >= EXPERTS) & (lane < EXPERTS + parts), 1.0, mask * odds)
        return residual, jnp.concatenate([normed, gates.astype(BF)], axis=1)

    twice = jnp.pad(router_weight, ((0, 0), (0, 16 - EXPERTS)))
    own_fill = DownProducts(cotangent[None], 1, lambda i: i, weights[2], weights[5])
    wide_input, residual, own_products = settle(
        [attended, output_weight],
        [
            tokens,
            second_gain[None],
            jnp.pad(jnp.concatenate([twice, twice], axis=1), ((0, 0), (0, 96))),
            named,
        ],
        second_norm,
        [jax.ShapeDtypeStruct((quarter, model), F32)],
        model + 128,
        own_fill,
        (0, own_fill.units - 2, own_fill.units),
        2,
    )
    all_input = lax.all_gather(wide_input, "dpo", axis=0, tiled=True)
    all_input = all_input.reshape(chips, count, model + 128)

    expert_part, input_back, kept_h, kept_g, kept_u, logit_grad = own_experts(
        wide_input, own_products, twice.T, weights
    )

    def second_norm_back(total, more):
        rows, gain, upstream_rows = more
        factor = lax.rsqrt(jnp.mean(rows * rows, axis=-1, keepdims=True) + EPSILON)
        back, gain_grad = norm_back(rows, factor, gain, total)
        back = back + upstream_rows.astype(F32)
        return back, gain_grad[None], back.astype(BF)

    input_back, all_upstream = lax.optimization_barrier((input_back, all_upstream))
    all_upstream = all_upstream.reshape(chips, count, model)
    far_fill = DownProducts(
        all_upstream, chips - 1, lambda i: lax.rem(lax.axis_index("dpo") + 1 + i, chips), weights[2], weights[5]
    )
    output_grad, residual_grad, grad_second_gain, far_products = settle(
        [input_back],
        [residual, second_gain[None], cotangent],
        second_norm_back,
        [
            jax.ShapeDtypeStruct((quarter, model), F32),
            jax.ShapeDtypeStruct((1, model), F32),
        ],
        model,
        far_fill,
        (0, far_fill.units * 2 // 7, far_fill.units * 4 // 7),
        3,
    )
    grad_second_gain = grad_second_gain[0]

    all_gates = grouped(
        jnp.transpose(all_input[:, :, model : model + EXPERTS].astype(F32), (2, 0, 1)), steps
    )
    all_gates = jnp.swapaxes(all_gates, 1, 2)

    routed_grads = []

    def piece(first, groups, beside, collective):
        made = group_gradients(
            all_input, all_upstream, far_products, all_gates,
            (kept_h, kept_g, kept_u), weights, first, groups, routed_grads, beside, collective,
        )
        if first == steps - 1:
            return made
        routed_grads[:] = made[:3]
        return made[3:]

    def summed(rows, got):
        return mine(rows).astype(F32) + jnp.sum(got.astype(F32), axis=0)

    grad_query, grad_output, query_part, grad_latent_up, latent_part, got_result = attention_backward(
        queries, latents, latent_up, key_ids, query_ids, attended, output_grad, output_weight, lse, even, odd,
        attention_input, query_weight, Scatter(expert_part), 4,
    )
    query_flow = [(grad_query, 0)]
    other_flow = [(grad_latent_up, 0), (grad_output, 1)]
    compressed_grad, *flows, result = piece(
        0,
        4,
        Beside(
            LineSum(latent_part),
            Beside(
                LineFlow(query_flow + other_flow, True, 2, 3),
                Beside(
                    LineFlow(other_flow, False, 6, 3),
                    Gather((residual + summed(expert_part, got_result)).astype(BF)),
                ),
            ),
        ),
        5,
    )
    attention_grad, grad_latent_down, grad_latent_gain, grad_first_gain = latents_back(
        compressed_grad, latent_raw, latent_gain[None], even, odd, latent_down.T, query_part, tokens,
        first_factor, attention_input,
    )
    grad_latent_down = lax.psum_scatter(grad_latent_down, DP, scatter_dimension=0, tiled=True)

    grad_router = lax.dot_general(
        wide_input[:, :model], logit_grad[:EXPERTS].astype(BF), (((0,), (1,)), ((), ())),
        preferred_element_type=F32,
    )

    def for_ranks(gain):
        return jnp.repeat(gain.reshape(2 * chips, -1), ranks, axis=0)

    small = jnp.concatenate(
        [
            grad_router.reshape(devices, -1),
            for_ranks(grad_second_gain),
            for_ranks(grad_first_gain),
            grad_latent_gain.reshape(devices, -1),
        ],
        axis=1,
    ).astype(BF)
    small = jnp.pad(small, ((0, 0), (0, 2048 - small.shape[1]))).reshape(devices * 16, 128)

    query_flow, small_left, small_right, got = piece(
        4,
        steps - 5,
        Beside(
            Beside(LineFlow(query_flow + [(small, 0)], False, 1, 2), LineFlow([(small, 0)], True, 1, 2)),
            Scatter(attention_grad),
        ),
        6,
    )
    grad_query, grad_latent_up, grad_output = (
        near + far.astype(F32) for near, far in zip([query_flow] + flows[3:], flows[:3])
    )
    token_float = token_quarter.astype(F32)
    _, token_factor = norm_rows(token_float, first_gain)
    token_back, _ = norm_back(token_float, token_factor, first_gain, summed(attention_grad, got))
    small = (small_left + small_right.astype(F32)).astype(BF)
    *shared_grads, token_grad, got_down, got_small = piece(
        steps - 1,
        1,
        Many(
            [
                Gather((token_back + residual_grad).astype(BF)),
                Scatter(grad_latent_down),
                Scatter(small),
            ]
        ),
        7,
    )
    token_grad, result = token_grad.reshape(count, model), result.reshape(count, model)

    def over_ranks(rows, got):
        size = got.shape[1]
        own = lax.dynamic_slice_in_dim(rows, rank * size, size, 0)
        return own.astype(F32) + jnp.sum(got.astype(F32), axis=0)

    grad_latent_down = over_ranks(grad_latent_down, got_down)
    small = over_ranks(small, got_small).reshape(-1)
    router_size = model // devices * EXPERTS
    gain_size = model // (2 * chips)
    latent_size = KVL // devices
    grad_router = small[:router_size].reshape(-1, EXPERTS)
    small = small[router_size:]

    def routed_of(array):
        return array.reshape(EXPERTS, unit, half).astype(F32)

    return (
        result,
        token_grad,
        small[gain_size : 2 * gain_size],
        grad_query,
        grad_latent_down,
        small[2 * gain_size : 2 * gain_size + latent_size],
        grad_latent_up,
        grad_output,
        small[:gain_size],
        grad_router,
        jnp.swapaxes(routed_of(routed_grads[0]), 1, 2),
        jnp.swapaxes(routed_of(routed_grads[1]), 1, 2),
        routed_of(routed_grads[2]),
        shared_grads[0].astype(F32).T,
        shared_grads[1].astype(F32).T,
        shared_grads[2].astype(F32),
    )


def solution(mesh):
    groups, ranks = mesh.devices.shape
    fine = Mesh(mesh.devices.reshape(groups // 2, 2, ranks), ("dpo", "core", "tensor"))
    in_specs = (
        P(DP, None),
        P(DP, None),
        P(),
        P(DP, None),
        P(),
        P(None, "tensor"),
        P(),
        P(),
        P(None, "tensor"),
        P("tensor", None),
        P(),
        P(),
        P(None, None, "tensor"),
        P(None, None, "tensor"),
        P(None, "tensor", None),
        P(None, "tensor"),
        P(None, "tensor"),
        P("tensor", None),
    )
    out_specs = (
        P(DP, None),
        P(DP, None),
        P(DP),
        P(DP, "tensor"),
        P(ALL, None),
        P(ALL),
        P(DP, "tensor"),
        P("tensor", DP),
        P(DP),
        P(ALL, None),
        P(None, DP, "tensor"),
        P(None, DP, "tensor"),
        P(None, "tensor", DP),
        P(DP, "tensor"),
        P(DP, "tensor"),
        P("tensor", DP),
    )
    return jax.shard_map(shards, mesh=fine, in_specs=in_specs, out_specs=out_specs, check_vma=False)
```

```python
import jax
import jax.numpy as jnp
from jax import lax
from jax.experimental import pallas as pl
from jax.experimental.pallas import tpu as pltpu
from jax.sharding import Mesh
from jax.sharding import PartitionSpec as P

ND = 128
RD = 64
VD = 128
KVL = 512
EXPERTS = 12
LAT = 640
EPSILON = 1e-06
LOG2E = 1.4426950408889634
BF = jnp.bfloat16
F32 = jnp.float32
VMEM_LIMIT = 60 * 1024 * 1024
DP = ("dpo", "core")
ALL = ("dpo", "core", "tensor")
MESH = pl.DeviceIdType.MESH
SHORT = pl.CostEstimate(flops=1000, bytes_accessed=100_000, transcendentals=0)


def nn(former, latter):
    return jnp.dot(former, latter, preferred_element_type=F32)


def nt(former, latter):
    return lax.dot_general(former, latter, (((1,), (1,)), ((), ())), preferred_element_type=F32)


def tn(former, latter):
    return lax.dot_general(former, latter, (((0,), (0,)), ((), ())), preferred_element_type=F32)


def rotary_tables(places):
    halfway = RD // 2
    frequency = 10000.0 ** (-jnp.arange(halfway, dtype=F32) * 2.0 / RD)
    angles = places.astype(F32)[:, None] * frequency[None, :]
    return jnp.cos(angles), jnp.sin(angles)


def rotate(values, cosine, sine_table):
    halfway = values.shape[-1] // 2
    leading = values[..., :halfway]
    trailing = values[..., halfway:]
    return jnp.concatenate(
        [leading * cosine - trailing * sine_table, trailing * cosine + leading * sine_table],
        axis=-1,
    )


def norm_rows(values, gain_row):
    factor = lax.rsqrt(jnp.mean(values * values, axis=-1, keepdims=True) + EPSILON)
    return values * factor * gain_row, factor


def norm_back(values, factor, gain_row, upstream):
    weighted = upstream * gain_row
    common = jnp.mean(weighted * values, axis=-1, keepdims=True)
    return (
        factor * weighted - values * factor * factor * factor * common,
        jnp.sum(upstream * values * factor, axis=0),
    )


def expert_unit(gate_pre, up_pre, hidden_grad, gate):
    sigmoid = 0.5 * jnp.tanh(0.5 * gate_pre) + 0.5
    silu = gate_pre * sigmoid
    hidden = silu * up_pre
    scaled = gate * hidden_grad
    d_up = scaled * silu
    d_gate = scaled * up_pre * (sigmoid + silu - silu * sigmoid)
    return (
        (gate * hidden).astype(BF),
        d_gate.astype(BF),
        d_up.astype(BF),
        hidden * hidden_grad,
    )


def weight_copies(routed, shared, held, sems, step, slot, steps, width, begin):
    def each(refs):
        for i, ref in enumerate(refs):
            copy = pltpu.make_async_copy(
                ref, held.at[slot, pl.ds(i * width, width)], sems.at[slot, i]
            )
            if begin:
                copy.start()
            else:
                copy.wait()

    @pl.when(step < steps - 1)
    def _():
        rows = pl.ds(pl.multiple_of(step * width, width), width)
        each([ref.at[rows] for ref in routed])

    @pl.when(step == steps - 1)
    def _():
        each(shared)


def gate_rows(gates, width):
    parts, columns = gates.shape
    return jnp.concatenate(
        [jnp.broadcast_to(gates[i : i + 1], (width // parts, columns)) for i in range(parts)],
        axis=0,
    )


def own_experts(rows, products_back, router_rows, weights):
    steps, _, width, count = products_back.shape
    model = rows.shape[1] - 128
    parts = EXPERTS // (steps - 1)
    unit = width // parts
    wide = 512

    def kernel(x_ref, tail_ref, b_ref, router_ref, gw, uw, dw, sg, su, sd, out_low, back_low, kept_h, kept_g, kept_u, lg_ref,
               held, sems, out, back, gates, router, dots):
        step = pl.program_id(0)
        slot = lax.rem(step, 2)
        routed, shared = (gw, uw, dw), (sg, su, sd)

        @pl.when(step == 0)
        def _():
            weight_copies(routed, shared, held, sems, step, slot, steps, width, True)
            out[...] = jnp.zeros_like(out)
            back[...] = jnp.zeros_like(back)
            tail = tail_ref[...].astype(F32).T
            for p in range(steps):
                gates[p] = tail[p * parts : (p + 1) * parts]
            router[...] = tail[16:32]

        weight_copies(routed, shared, held, sems, step, slot, steps, width, False)

        @pl.when(step < steps - 1)
        def _():
            weight_copies(routed, shared, held, sems, step + 1, 1 - slot, steps, width, True)

        both = nt(held[slot, : 2 * width], x_ref[...])
        hidden, d_gate, d_up, products = expert_unit(
            both[:width], both[width:], b_ref[0, 0].astype(F32), gate_rows(gates[step], width)
        )
        kept_h[0] = hidden
        kept_g[0] = d_gate
        kept_u[0] = d_up
        dots[step] = jnp.concatenate(
            [
                jnp.sum(products[i * unit : (i + 1) * unit], axis=0, keepdims=True)
                for i in range(parts)
            ],
            axis=0,
        )
        turned = hidden.T
        turned_back = jnp.concatenate([d_gate, d_up], axis=0).T
        for at in range(0, model, wide):
            columns = slice(at, at + wide)
            out[:, columns] += nn(turned, held[slot, 2 * width :, columns])
            back[:, columns] += nn(turned_back, held[slot, : 2 * width, columns])

        @pl.when(step == steps - 1)
        def _():
            out_low[...] = out[...].astype(BF)
            spare = jnp.zeros((16 - EXPERTS, count), F32)
            pair_grad = jnp.concatenate([dots[p] for p in range(steps - 1)] + [spare], axis=0)
            named = jnp.concatenate([gates[p] for p in range(steps - 1)] + [spare], axis=0) > 0
            pair_grad = jnp.where(named, pair_grad, 0.0)
            odds = router[...]
            logit_grad = odds * (pair_grad - jnp.sum(odds * pair_grad, axis=0, keepdims=True))
            lg_ref[...] = logit_grad
            turned_logits = logit_grad.T.astype(BF)
            for at in range(0, model, wide):
                columns = slice(at, at + wide)
                back_low[:, columns] = (
                    back[:, columns] + nn(turned_logits, router_ref[:, columns])
                ).astype(BF)

    def whole(shape):
        return pl.BlockSpec(shape, lambda p: (0,) * len(shape), pipeline_mode=pl.Buffered(1))

    def one(shape):
        return pl.BlockSpec((1,) + shape, lambda p: (p, 0, 0))

    kept = jax.ShapeDtypeStruct((steps, width, count), BF)
    total = jax.ShapeDtypeStruct((count, model), BF)
    return pl.pallas_call(
        kernel,
        name="own_experts",
        grid=(steps,),
        in_specs=[
            whole((count, model)),
            pl.BlockSpec((count, 128), lambda p: (0, model // 128), pipeline_mode=pl.Buffered(1)),
            pl.BlockSpec((1, 1, width, count), lambda p: (p, 0, 0, 0)),
            whole((16, model)),
        ]
        + [pl.BlockSpec(memory_space=pl.ANY)] * 6,
        out_specs=[whole((count, model))] * 2 + [one((width, count))] * 3 + [whole((16, count))],
        out_shape=[total, total, kept, kept, kept, jax.ShapeDtypeStruct((16, count), F32)],
        scratch_shapes=[
            pltpu.VMEM((2, 3 * width, model), BF),
            pltpu.SemaphoreType.DMA((2, 3)),
            pltpu.VMEM((count, model), F32),
            pltpu.VMEM((count, model), F32),
            pltpu.VMEM((steps, parts, count), F32),
            pltpu.VMEM((16, count), F32),
            pltpu.VMEM((steps, parts, count), F32),
        ],
        cost_estimate=SHORT,
        compiler_params=pltpu.CompilerParams(
            vmem_limit_bytes=VMEM_LIMIT, dimension_semantics=("arbitrary",)
        ),
    )(rows, rows, products_back, router_rows, *weights)


def ring_of(axis):
    here = lax.axis_index(axis)
    size = lax.axis_size(axis)
    return here, [lax.rem(here + i, size) for i in range(size)]


def greet(friends):
    barrier = pltpu.get_barrier_semaphore()
    total = 0
    for device, present in friends.values():
        if present is None:
            pl.semaphore_signal(barrier, inc=1, device_id=device, device_id_type=MESH)
            total = total + 1
            continue

        @pl.when(present)
        def _():
            pl.semaphore_signal(barrier, inc=1, device_id=device, device_id_type=MESH)

        total = total + jnp.where(present, 1, 0)
    pl.semaphore_wait(barrier, total)


def mate_friend():
    return {"mate": ({"core": 1 - lax.axis_index("core")}, None)}


def rank_friends():
    _, peers = ring_of("tensor")
    return {f"rank{d}": ({"tensor": peer}, None) for d, peer in enumerate(peers) if d}


def line_friends():
    chip, chips = lax.axis_index("dpo"), lax.axis_size("dpo")
    return {
        "left": ({"dpo": lax.rem(chip + chips - 1, chips)}, chip > 0),
        "right": ({"dpo": lax.rem(chip + 1, chips)}, chip < chips - 1),
    }


def remote(source, target, send, receive, device):
    return pltpu.make_async_remote_copy(
        src_ref=source, dst_ref=target, send_sem=send, recv_sem=receive,
        device_id=device, device_id_type=MESH,
    )


class Scatter:
    def __init__(self, rows):
        ranks = lax.axis_size("tensor")
        quarter = rows.shape[0] // ranks
        self.ins = [rows.reshape(ranks, quarter, rows.shape[1])]
        self.in_specs = [pl.BlockSpec(memory_space=pl.ANY)]
        self.outs = [jax.ShapeDtypeStruct((ranks - 1, quarter, rows.shape[1]), rows.dtype)]
        self.out_specs = [pl.BlockSpec(memory_space=pl.ANY)]
        self.scratch = [pltpu.SemaphoreType.DMA((ranks,)), pltpu.SemaphoreType.DMA((ranks,))]

    def copies(self, refs):
        source, target, sends, receives = refs
        _, peers = ring_of("tensor")
        return [
            remote(source.at[peer], target.at[d - 1], sends.at[d], receives.at[d], {"tensor": peer})
            for d, peer in enumerate(peers)
            if d
        ]

    def friends(self):
        return rank_friends()

    def begin(self, refs):
        for copy in self.copies(refs):
            copy.start()

    def middle(self, refs, step, last):
        pass

    def end(self, refs):
        for copy in self.copies(refs):
            copy.wait()


class Gather(Scatter):
    def __init__(self, rows):
        ranks = lax.axis_size("tensor")
        self.ins = [rows]
        self.in_specs = [pl.BlockSpec(memory_space=pl.ANY)]
        self.outs = [jax.ShapeDtypeStruct((ranks,) + rows.shape, rows.dtype)]
        self.out_specs = [pl.BlockSpec(memory_space=pl.ANY)]
        self.scratch = [pltpu.SemaphoreType.DMA((ranks,)), pltpu.SemaphoreType.DMA((ranks,))]

    def copies(self, refs):
        source, target, sends, receives = refs
        rank, peers = ring_of("tensor")
        return [pltpu.make_async_copy(source, target.at[rank], sends.at[0])] + [
            remote(source, target.at[rank], sends.at[d], receives.at[d], {"tensor": peer})
            for d, peer in enumerate(peers)
            if d
        ]


class Many(Scatter):
    def __init__(self, transfers):
        self.transfers = transfers
        self.ins = [x for t in transfers for x in t.ins]
        self.in_specs = [x for t in transfers for x in t.in_specs]
        self.outs = [x for t in transfers for x in t.outs]
        self.out_specs = [x for t in transfers for x in t.out_specs]
        self.scratch = [x for t in transfers for x in t.scratch]

    def copies(self, refs):
        n = len(self.transfers)
        copies = []
        for i, t in enumerate(self.transfers):
            own = [refs[i], refs[n + i], refs[2 * n + 2 * i], refs[2 * n + 2 * i + 1]]
            copies += t.copies(own)
        return copies


class LineSum:
    def __init__(self, blocks):
        chips = lax.axis_size("dpo")
        self.chips = chips
        shape = blocks.shape[1:]
        self.rows = shape[0] // 2
        self.ins = [blocks]
        self.in_specs = [pl.BlockSpec(memory_space=pl.ANY)]
        self.outs = [jax.ShapeDtypeStruct(shape, F32)]
        self.out_specs = [pl.BlockSpec(shape, lambda *_: (0, 0), pipeline_mode=pl.Buffered(1))]
        self.scratch = [
            pltpu.VMEM((chips,) + shape, blocks.dtype),
            pltpu.VMEM((chips,) + shape, blocks.dtype),
            pltpu.VMEM(shape, blocks.dtype),
        ] + [pltpu.SemaphoreType.DMA((chips, 2))] * 4 + [pltpu.SemaphoreType.DMA((2,))]

    def friends(self):
        return line_friends()

    def part(self, s):
        return pl.ds(s * self.rows, self.rows)

    def swap(self, refs, i, s):
        source, _, mate, _, _, sends, receives, _, _, _ = refs
        core = lax.axis_index("core")
        return remote(
            source.at[2 * i + 1 - core, self.part(s)], mate.at[i, self.part(s)],
            sends.at[i, s], receives.at[i, s], {"core": 1 - core},
        )

    def onward(self, refs, i, s):
        _, _, mate, inbox, _, _, _, sends, receives, _ = refs
        left = lax.rem(lax.axis_index("dpo") + self.chips - 1, self.chips)
        return remote(
            mate.at[i, self.part(s)], inbox.at[i, self.part(s)], sends.at[i, s], receives.at[i, s], {"dpo": left}
        )

    def begin(self, refs):
        chip = lax.axis_index("dpo")
        for i in range(self.chips):
            @pl.when(i <= chip)
            def _():
                for s in range(2):
                    self.swap(refs, i, s).start()

    def middle(self, refs, step, last):
        source, out, mate, inbox, mine, _, _, _, _, sems = refs
        chip, core = lax.axis_index("dpo"), lax.axis_index("core")
        for i in range(self.chips):
            for s in range(2):
                self.one(refs, step, last, i, s)

    def one(self, refs, step, last, i, s):
        source, out, mate, inbox, mine, _, _, _, _, sems = refs
        chip, core = lax.axis_index("dpo"), lax.axis_index("core")
        part = self.part(s)
        due = 1 + 2 * (self.chips - 1 - chip) + 2 * i + s
        local = pltpu.make_async_copy(source.at[2 * i + core, part], mine.at[part], sems.at[s])

        @pl.when((i <= chip) & (step == due - 1) & (due <= last))
        def _():
            local.start()

        @pl.when((i <= chip) & (step == jnp.minimum(due, last)))
        def _():
            @pl.when(due > last)
            def _():
                local.start()

            self.swap(refs, i, s).wait()
            local.wait()

            @pl.when(chip == self.chips - 1)
            def _():
                mate[i, part] = (mate[i, part].astype(F32) + mine[part].astype(F32)).astype(mate.dtype)

            @pl.when(chip < self.chips - 1)
            def _():
                self.onward(refs, i, s).wait_recv()
                mate[i, part] = (
                    mate[i, part].astype(F32) + mine[part].astype(F32) + inbox[i, part].astype(F32)
                ).astype(mate.dtype)

            @pl.when(chip > i)
            def _():
                self.onward(refs, i, s).start()

            @pl.when(chip == i)
            def _():
                out[part] = mate[i, part].astype(F32)

    def end(self, refs):
        chip = lax.axis_index("dpo")
        for i in range(self.chips):
            @pl.when(chip > i)
            def _():
                for s in range(2):
                    self.onward(refs, i, s).wait_send()


class LineFlow:
    def __init__(self, arrays, rightward, first, hop):
        chips = lax.axis_size("dpo")
        self.chips, self.rightward, self.first, self.hop = chips, rightward, first, hop
        self.dimensions = [d for _, d in arrays]
        self.shapes = [
            tuple(n // (2 * chips) if i == d else n for i, n in enumerate(a.shape)) for a, d in arrays
        ]
        n = len(arrays)
        self.ins = [a for a, _ in arrays]
        self.in_specs = [pl.BlockSpec(memory_space=pl.ANY)] * n
        self.outs = [jax.ShapeDtypeStruct(shape, BF if rightward else F32) for shape in self.shapes]
        self.out_specs = [
            pl.BlockSpec(shape, lambda *_: (0, 0), pipeline_mode=pl.Buffered(1)) for shape in self.shapes
        ]
        self.scratch = []
        for shape in self.shapes:
            self.scratch += [
                pltpu.VMEM((chips,) + shape, BF),
                pltpu.VMEM((chips,) + shape, BF),
                pltpu.VMEM(shape, BF),
            ]
        self.scratch += [pltpu.SemaphoreType.DMA((n, chips))] * 4 + [pltpu.SemaphoreType.DMA((n,))]

    def friends(self):
        return line_friends()

    def parts(self, refs):
        n = len(self.shapes)
        buffers = refs[2 * n : 5 * n]
        return [(refs[j], refs[n + j]) + tuple(buffers[3 * j : 3 * j + 3]) for j in range(n)], refs[5 * n :]

    def block(self, j, source, place):
        size = self.shapes[j][self.dimensions[j]]
        part = pl.ds(pl.multiple_of(place * size, size), size)
        return source.at[part] if self.dimensions[j] == 0 else source.at[:, part]

    def distance(self, i):
        chip = lax.axis_index("dpo")
        return i - chip if self.rightward else chip - i

    def swap(self, refs, i, j):
        parts, sems = self.parts(refs)
        source, _, mate, _, _ = parts[j]
        core = lax.axis_index("core")
        return remote(
            self.block(j, source, 2 * i + 1 - core), mate.at[i], sems[0].at[j, i], sems[1].at[j, i],
            {"core": 1 - core},
        )

    def onward(self, refs, i, j):
        parts, sems = self.parts(refs)
        _, _, mate, inbox, _ = parts[j]
        step = 1 if self.rightward else self.chips - 1
        to = lax.rem(lax.axis_index("dpo") + step, self.chips)
        return remote(mate.at[i], inbox.at[i], sems[2].at[j, i], sems[3].at[j, i], {"dpo": to})

    def begin(self, refs):
        for i in range(self.chips):
            @pl.when(self.distance(i) >= (1 if self.rightward else 0))
            def _():
                for j in range(len(self.shapes)):
                    self.swap(refs, i, j).start()

    def middle(self, refs, step, last):
        order = range(self.chips - 1, -1, -1) if self.rightward else range(self.chips)
        for i in order:
            for j in range(len(self.shapes)):
                self.one(refs, step, last, i, j)

    def one(self, refs, step, last, i, j):
        chip, core = lax.axis_index("dpo"), lax.axis_index("core")
        parts, sems = self.parts(refs)
        source, out, mate, inbox, mine = parts[j]
        end = self.chips - 1
        away = self.distance(i)
        begins = chip == (0 if self.rightward else end)
        adds = away >= (1 if self.rightward else 0)
        due = self.first + self.hop * (end - away) + min(j, 1)
        ahead = pltpu.make_async_copy(self.block(j, source, 2 * i + core), mine, sems[4].at[j])

        @pl.when(adds & (step == due - 1) & (due <= last))
        def _():
            ahead.start()

        @pl.when(adds & (step == jnp.minimum(due, last)))
        def _():
            @pl.when(due > last)
            def _():
                ahead.start()

            self.swap(refs, i, j).wait()
            ahead.wait()

            @pl.when(begins)
            def _():
                mate[i] = (mate[i].astype(F32) + mine[...].astype(F32)).astype(BF)

        @pl.when((away >= 0) & (step == jnp.minimum(due, last)))
        def _():
            @pl.when(jnp.logical_not(begins))
            def _():
                self.onward(refs, i, j).wait_recv()

            @pl.when(jnp.logical_not(begins) & adds)
            def _():
                mate[i] = (
                    mate[i].astype(F32) + mine[...].astype(F32) + inbox[i].astype(F32)
                ).astype(BF)

            @pl.when(away > 0)
            def _():
                self.onward(refs, i, j).start()

            @pl.when(away == 0)
            def _():
                if not self.rightward:
                    out[...] = mate[i].astype(F32)
                    return

                @pl.when(begins)
                def _():
                    out[...] = jnp.zeros_like(out)

                @pl.when(jnp.logical_not(begins))
                def _():
                    out[...] = inbox[i]

    def end(self, refs):
        for i in range(self.chips):
            @pl.when(self.distance(i) > 0)
            def _():
                for j in range(len(self.shapes)):
                    self.onward(refs, i, j).wait_send()


class Beside:
    def __init__(self, former, latter):
        self.pair = (former, latter)
        self.ins = former.ins + latter.ins
        self.in_specs = former.in_specs + latter.in_specs
        self.outs = former.outs + latter.outs
        self.out_specs = former.out_specs + latter.out_specs
        self.scratch = former.scratch + latter.scratch

    def split(self, refs):
        refs = list(refs)
        lists = ([], [])
        for name in ("ins", "outs", "scratch"):
            for t, held in zip(self.pair, lists):
                n = len(getattr(t, name))
                held += refs[:n]
                del refs[:n]
        return zip(self.pair, lists)

    def friends(self):
        return {**self.pair[0].friends(), **self.pair[1].friends()}

    def begin(self, refs):
        for t, held in self.split(refs):
            t.begin(held)

    def middle(self, refs, step, last):
        for t, held in self.split(refs):
            t.middle(held, step, last)

    def end(self, refs):
        for t, held in self.split(refs):
            t.end(held)


class DownProducts:
    def __init__(self, upstream, count, block_of, down, shared_down):
        _, rows, model = upstream.shape
        self.width = shared_down.shape[0]
        self.steps = down.shape[0] // self.width + 1
        self.count, self.block_of, self.units = count, block_of, self.steps * count
        self.ins = [upstream, down, shared_down]
        self.outs = [jax.ShapeDtypeStruct((self.steps, count, self.width, rows), BF)]
        self.scratch = [
            pltpu.VMEM((2, self.width, model), BF),
            pltpu.VMEM((count, rows, model), BF),
            pltpu.VMEM((2, self.width, rows), BF),
            pltpu.SemaphoreType.DMA((2, 1)),
            pltpu.SemaphoreType.DMA((count,)),
            pltpu.SemaphoreType.DMA((2,)),
        ]

    def load(self, refs, step, begin):
        _, down, shared, _, held, _, _, sems, _, _ = refs
        weight_copies((down,), (shared,), held, sems, step, lax.rem(step, 2), self.steps, self.width, begin)

    def block(self, refs, i):
        source, _, _, _, _, rows, _, _, sems, _ = refs
        return pltpu.make_async_copy(source.at[self.block_of(i)], rows.at[i], sems.at[i])

    def put(self, refs, unit):
        out, stage, sems = refs[3], refs[6], refs[9]
        slot = lax.rem(unit, 2)
        return pltpu.make_async_copy(
            stage.at[slot], out.at[unit // self.count, lax.rem(unit, self.count)], sems.at[slot]
        )

    def begin(self, refs):
        self.load(refs, 0, True)
        for i in range(self.count):
            self.block(refs, i).start()

    def run(self, refs, first, last):
        held, rows, stage = refs[4], refs[5], refs[6]

        def one(unit, carry):
            step, i = unit // self.count, lax.rem(unit, self.count)

            @pl.when(i == 0)
            def _():
                self.load(refs, step, False)

                @pl.when(step < self.steps - 1)
                def _():
                    self.load(refs, step + 1, True)

            @pl.when(step == 0)
            def _():
                self.block(refs, i).wait()

            @pl.when(unit >= 2)
            def _():
                self.put(refs, unit - 2).wait()

            stage[lax.rem(unit, 2)] = nt(held[lax.rem(step, 2)], rows[i]).astype(BF)
            self.put(refs, unit).start()
            return carry

        lax.fori_loop(first, last, one, 0)

    def end(self, refs):
        for unit in (self.units - 2, self.units - 1):
            self.put(refs, unit).wait()


def settle(part, more, finish, extra, wide, fill, splits, collective):
    count, model = part[0].shape[0], part[-1].shape[1]
    ranks = lax.axis_size("tensor")
    quarter = count // ranks
    size = quarter // 2
    n_part, n_more, n_extra = len(part), len(more), len(extra)

    def kernel(*refs):
        refs = list(refs)

        def take(n):
            taken = refs[:n]
            del refs[:n]
            return taken

        part_refs, more_refs = take(n_part), take(n_more)
        fill_refs = take(len(fill.ins))
        (out_ref,), extra_refs = take(1), take(n_extra)
        fill_refs += take(len(fill.outs))
        inbox, block, gathered, send, receive, send_on, receive_on = take(7)
        fill_refs += take(len(fill.scratch))
        part_ref = refs[0] if refs else part_refs[0]
        rank, peers = ring_of("tensor")

        def rows_of(i, s):
            return pl.ds(pl.multiple_of(i * quarter + s * size, size), size)

        fill.begin(fill_refs)
        greet(rank_friends())
        first, then = [[], []], [[], []]
        for s in range(2):
            own = pl.ds(s * size, size)
            for d, peer in enumerate(peers):
                rows = rows_of(peer, s)
                if n_part == 2:
                    part_ref[rows] = nn(part_refs[0][rows], part_refs[1][...]).astype(BF)
                if d:
                    first[s].append(
                        remote(part_ref.at[rows], inbox.at[d, own], send.at[s, d], receive.at[s, d], {"tensor": peer})
                    )
                    first[s][-1].start()
                    then[s].append(
                        remote(block.at[own], gathered.at[d, own], send_on.at[s, d], receive_on.at[s, d], {"tensor": peer})
                    )
        for s in range(2):
            own = pl.ds(s * size, size)
            rows = rows_of(rank, s)
            fill.run(fill_refs, splits[s], splits[s + 1])
            total = part_ref[rows].astype(F32)
            for d, copy in enumerate(first[s]):
                copy.wait()
                total = total + inbox[d + 1, own].astype(F32)
            results = finish(
                total,
                [
                    r[rows] if r.shape[0] == count else r[own] if r.shape[0] == quarter else r[...]
                    for r in more_refs
                ],
            )
            for ref, value in zip(extra_refs, results):
                if ref.shape[0] > 1:
                    ref[own] = value
                elif s:
                    ref[...] += value
                else:
                    ref[...] = value
            block[own] = results[-1]
            for copy in then[s]:
                copy.start()
            out_ref[rows] = block[own]
        fill.run(fill_refs, splits[2], fill.units)
        fill.end(fill_refs)
        for s in range(2):
            for d, copy in enumerate(then[s]):
                copy.wait()
                out_ref[rows_of(lax.rem(rank + ranks - d - 1, ranks), s)] = gathered[d + 1, pl.ds(s * size, size)]

    vmem = pl.BlockSpec(memory_space=pltpu.VMEM)
    anywhere = pl.BlockSpec(memory_space=pl.ANY)
    sems = [pltpu.SemaphoreType.DMA((2, ranks))] * 4
    return pl.pallas_call(
        kernel,
        name="settle",
        in_specs=[vmem] * (n_part + n_more) + [anywhere] * len(fill.ins),
        out_specs=[vmem] * (1 + n_extra) + [anywhere] * len(fill.outs),
        out_shape=[jax.ShapeDtypeStruct((count, wide), BF)] + extra + fill.outs,
        scratch_shapes=[
            pltpu.VMEM((ranks, quarter, model), BF),
            pltpu.VMEM((quarter, wide), BF),
            pltpu.VMEM((ranks, quarter, wide), BF),
        ]
        + sems
        + fill.scratch
        + ([pltpu.VMEM((count, model), BF)] if n_part == 2 else []),
        cost_estimate=SHORT,
        compiler_params=pltpu.CompilerParams(
            vmem_limit_bytes=VMEM_LIMIT, collective_id=collective, has_side_effects=True
        ),
    )(*part, *more, *fill.ins)


def group_gradients(rows, upstream, products_back, gates, kept, weights, first, groups, held_back, beside, collective):
    chips, count, model = upstream.shape
    steps, _, parts, _ = gates.shape
    width = weights[3].shape[0]
    half = model // (2 * chips)
    unit = width // 2
    weights = weights[:2] + weights[3:5]
    n_ins, n_outs = len(beside.ins), len(beside.outs)
    last = groups * chips - 1
    ends, routes = first + groups == steps, first < steps - 1
    held_back = held_back if routes else []
    n_held = len(held_back)

    def kernel(*refs):
        refs = list(refs)

        def take(n):
            taken = refs[:n]
            del refs[:n]
            return taken

        x_ref, xc, cc, b_ref, g_ref, kept_h, kept_g, kept_u = take(8)
        routed, shared = take(2), take(2)
        take(n_held)
        link_refs = take(n_ins)
        outs = take(3) if routes else None
        shared_outs = take(3) if ends else None
        link_refs += take(n_outs)
        held, sems, sum_g, sum_u, sum_d, outbox, inbox, sends, receives = take(9)
        link_refs += refs
        at_group = pl.program_id(0)
        turn = pl.program_id(1)
        step = at_group + first
        slot = lax.rem(at_group, 2)
        tick = at_group * chips + turn
        sums = (sum_g, sum_u, sum_d)
        core = lax.axis_index("core")

        def columns_of(i):
            return pl.ds(pl.multiple_of(i * half, half), half)

        def swap(i):
            part = pl.ds(i * unit, unit)
            return remote(
                outbox.at[:, part], inbox.at[slot, :, part], sends.at[slot, i], receives.at[slot, i],
                {"core": 1 - lax.axis_index("core")},
            )

        @pl.when(tick == 0)
        def _():
            greet({**mate_friend(), **beside.friends()})
            beside.begin(link_refs)

        @pl.when(turn == 0)
        def _():
            @pl.when(at_group == 0)
            def _():
                weight_copies(routed, shared, held, sems, step, slot, steps, width, True)

            sum_g[...] = nn(kept_g[0], xc[0])
            sum_u[...] = nn(kept_u[0], xc[0])
            sum_d[...] = nn(kept_h[0], cc[0])
            weight_copies(routed, shared, held, sems, step, slot, steps, width, False)

            @pl.when(at_group < groups - 1)
            def _():
                weight_copies(routed, shared, held, sems, step + 1, 1 - slot, steps, width, True)

        def work(final):
            x = x_ref[0]
            gate = gate_rows(g_ref[0, 0], width)
            parts_ = [slice(i * unit, (i + 1) * unit) for i in range(2)]
            pre = [
                (nt(held[slot, part], x), nt(held[slot, width + part.start : width + part.stop], x))
                for part in parts_
            ]
            terms = []
            for part, (gate_pre, up_pre) in zip(parts_, pre):
                hidden, d_gate, d_up, _ = expert_unit(
                    gate_pre, up_pre, b_ref[0, 0, part].astype(F32), gate[part]
                )
                terms.append(((d_gate, xc), (d_up, xc), (hidden, cc)))
                if not final:
                    for total, (term, columns) in zip(sums, terms[-1]):
                        total[part] += nn(term, columns[0])
            if not final:
                return
            far, near = columns_of(1 - core), columns_of(core)
            for i, part in enumerate(parts_):
                for j, (total, (term, columns)) in enumerate(zip(sums, terms[i])):
                    outbox[j, part] = (total[part, far] + nn(term, columns[0, :, far])).astype(BF)
                swap(i).start()
            for part, made in zip(parts_, terms):
                for total, (term, columns) in zip(sums, made):
                    total[part, near] += nn(term, columns[0, :, near])

        @pl.when((turn > 0) & (turn < chips - 1))
        def _():
            work(False)

        @pl.when(turn == chips - 1)
        def _():
            work(True)
            for i in range(2):
                swap(i).wait()
                part = slice(i * unit, (i + 1) * unit)
                for j, total in enumerate(sums):
                    value = (total[part, columns_of(core)] + inbox[slot, j, part].astype(F32)).astype(BF)
                    if not ends:
                        outs[j][part] = value
                        continue

                    if routes:
                        @pl.when(step < steps - 1)
                        def _():
                            outs[j][part] = value

                    @pl.when(step == steps - 1)
                    def _():
                        shared_outs[j][part] = value

        beside.middle(link_refs, tick, last)

        @pl.when(tick == last)
        def _():
            beside.end(link_refs)

    def chip_at(turn):
        return lax.rem(lax.axis_index("dpo") + turn, chips)

    def at_chip(shape):
        return pl.BlockSpec((1,) + shape, lambda p, k: (chip_at(k), 0, 0))

    def one(shape):
        return pl.BlockSpec((1,) + shape, lambda p, k: (p + first, 0, 0))

    columns = pl.BlockSpec((1, count, 2 * half), lambda p, k: (chip_at(k), 0, lax.axis_index("dpo")))

    anywhere = pl.BlockSpec(memory_space=pl.ANY)
    block = pl.BlockSpec((width, half), lambda p, k: (jnp.minimum(p + first, steps - 2), 0))
    shared_block = pl.BlockSpec((width, half), lambda p, k: (0, 0))
    return pl.pallas_call(
        kernel,
        name="group_gradients",
        grid_spec=pltpu.PrefetchScalarGridSpec(
            num_scalar_prefetch=0,
            grid=(groups, chips),
            in_specs=[at_chip((count, model))]
            + [columns] * 2
            + [pl.BlockSpec((1, 1, width, count), lambda p, k: (p + first, jnp.maximum(k - 1, 0), 0, 0))]
            + [pl.BlockSpec((1, 1, parts, count), lambda p, k: (p + first, chip_at(k), 0, 0))]
            + [one((width, count))] * 3
            + [anywhere] * (4 + n_held)
            + beside.in_specs,
            out_specs=([block] * 3 if routes else []) + ([shared_block] * 3 if ends else []) + beside.out_specs,
            scratch_shapes=[
                pltpu.VMEM((2, 2 * width, model), BF),
                pltpu.SemaphoreType.DMA((2, 2)),
            ]
            + [pltpu.VMEM((width, 2 * half), F32)] * 3
            + [
                pltpu.VMEM((3, width, half), BF),
                pltpu.VMEM((2, 3, width, half), BF),
                pltpu.SemaphoreType.DMA((2, 2)),
                pltpu.SemaphoreType.DMA((2, 2)),
            ]
            + beside.scratch,
        ),
        out_shape=([jax.ShapeDtypeStruct(((steps - 1) * width, half), BF)] * 3 if routes else [])
        + ([jax.ShapeDtypeStruct((width, half), BF)] * 3 if ends else [])
        + beside.outs,
        input_output_aliases={12 + i: i for i in range(n_held)},
        cost_estimate=pl.CostEstimate(
            flops=groups * 2 * width * count * (2 * (chips - 1) * model + 6 * chips * half),
            bytes_accessed=groups * (6 * width * model + 4 * chips * count * model),
            transcendentals=0,
        ),
        compiler_params=pltpu.CompilerParams(
            vmem_limit_bytes=VMEM_LIMIT,
            dimension_semantics=("arbitrary", "arbitrary"),
            collective_id=collective,
            has_side_effects=True,
        ),
    )(
        rows, rows, upstream, products_back, gates, *kept, *weights, *held_back, *beside.ins,
    )


def turn_pairs(values, even, odd):
    lane = lax.broadcasted_iota(jnp.int32, values.shape, 1)
    other = jnp.where(lane < RD // 2, pltpu.roll(values, 128 - RD // 2, 1), pltpu.roll(values, RD // 2, 1))
    return values * even + other * odd


def attention_forward(tokens, gain, query_weight, latent_rows, latent_gain, latent_up, even, odd, key_ids, query_ids, collective):
    count, model = tokens.shape
    heads = latent_up.shape[1] // 256
    chips = lax.axis_size("dpo")
    ranks = lax.axis_size("tensor")
    quarter = count // ranks
    scale = (ND + RD) ** (-0.5) * LOG2E

    def kernel(x_ref, gain_ref, qw_ref, ld_ref, lg_ref, up_ref, even_ref, odd_ref, kid_ref, qid_ref,
               att_ref, lse_ref, all_ref, in_ref, raw_ref, q_ref, factor_ref, lat_ref, rope_ref, keys, top, low, mix,
               send_right, take_left, send_mate, take_mate, send_rank, take_rank):
        chip, core = lax.axis_index("dpo"), lax.axis_index("core")
        rank, peers = ring_of("tensor")
        place = chip * 2 + core
        right = lax.rem(chip + 1, chips)
        own_rows = pl.ds(pl.multiple_of(rank * quarter, quarter), quarter)
        greet({**mate_friend(), **line_friends(), **rank_friends()})

        def to_right(i):
            return remote(
                all_ref.at[2 * i + core, own_rows], all_ref.at[2 * i + core, own_rows],
                send_right.at[i], take_left.at[i], {"dpo": right},
            )

        def to_mate(i):
            return remote(
                all_ref.at[2 * i + core], all_ref.at[2 * i + core],
                send_mate.at[i], take_mate.at[i], {"core": 1 - core},
            )

        def to_ranks(i):
            return [
                remote(
                    all_ref.at[2 * i + core, own_rows], all_ref.at[2 * i + core, own_rows],
                    send_rank.at[i, d], take_rank.at[i, d], {"tensor": peer},
                )
                for d, peer in enumerate(peers)
                if d
            ]

        x = x_ref[...].astype(F32)
        normed, factor = norm_rows(x, gain_ref[...])
        factor_ref[...] = jnp.broadcast_to(factor, (count, 128))
        in_ref[...] = normed.astype(BF)
        raw = nt(in_ref[...], ld_ref[:KVL])
        raw_ref[...] = raw
        rope_ref[...] = jnp.zeros_like(rope_ref)
        rope_ref[:, :RD] = nt(in_ref[...], ld_ref[KVL:])
        latent, _ = norm_rows(raw, lg_ref[...])
        lat_ref[:, :KVL] = latent.astype(BF)
        lat_ref[:, KVL:] = turn_pairs(rope_ref[...], even_ref[...], odd_ref[...]).astype(BF)
        all_ref[place] = lat_ref[...]

        @pl.when(chip < chips - 1)
        def _():
            to_right(chip).start()

        to_mate(chip).start()
        raw_q = nn(in_ref[...], qw_ref[...])
        lane = lax.broadcasted_iota(jnp.int32, (count, 128), 1)
        for h in range(0, heads, 2):
            at = h * (ND + RD)
            former, between, latter = (raw_q[:, at + i : at + i + 128] for i in (0, 128, 256))
            rolled = pltpu.roll(latter, 64, 1)
            nope = jnp.where(lane < 64, pltpu.roll(between, 64, 1), rolled)
            for i, (plain, rope) in enumerate(((former, between), (nope, rolled))):
                to = (h + i) * 256
                q_ref[:, to : to + ND] = plain.astype(BF)
                q_ref[:, to + ND : to + 256] = turn_pairs(rope, even_ref[...], odd_ref[...]).astype(BF)
        top[...] = jnp.full_like(top, -1e30)
        low[...] = jnp.zeros_like(low)
        mix[...] = jnp.zeros_like(mix)

        def chunk(source, masked):
            lat = source[:, :KVL]
            rope = source[:, KVL:]
            for h in range(heads):
                keys[h, :, ND:] = rope
                both = nn(lat, up_ref[:, h * 256 : (h + 1) * 256]).astype(BF)
                keys[h, :, :ND] = both[:, :ND]
                values = both[:, ND:].T
                scores = nt(keys[h], q_ref[:, h * 256 : (h + 1) * 256]) * scale
                if masked:
                    scores = jnp.where(kid_ref[...] <= qid_ref[...], scores, -1e30)
                before = top[h]
                highest = jnp.maximum(before, jnp.max(scores, axis=0, keepdims=True))
                weights = jnp.exp2(scores - highest)
                decay = jnp.exp2(before - highest)
                top[h] = highest
                low[h] = low[h] * decay + jnp.sum(weights, axis=0, keepdims=True)
                mix[h] = mix[h] * decay + nn(values, weights.astype(BF))

        def intake(i):
            to_right(i).wait_recv()

            @pl.when(chip < chips - 1)
            def _():
                to_right(i).start()

            for copy in to_ranks(i):
                copy.start()

        chunk(lat_ref, True)

        @pl.when(chip > 0)
        def _():
            intake(chip - 1)

        to_mate(chip).wait()

        @pl.when(core == 1)
        def _():
            chunk(all_ref.at[place - 1], False)

        def earlier(i, carry):
            at = chip - 1 - i

            @pl.when(at > 0)
            def _():
                intake(at - 1)

            for copy in to_ranks(at):
                copy.wait_recv()
            to_mate(at).start()
            chunk(all_ref.at[2 * at + core], False)
            to_mate(at).wait_recv()
            chunk(all_ref.at[2 * at + 1 - core], False)
            return carry

        lax.fori_loop(0, chip, earlier, 0)
        for h in range(heads):
            att_ref[:, h * VD : (h + 1) * VD] = (mix[h] / low[h]).T.astype(BF)
            lse_ref[h] = top[h] + jnp.log2(low[h])

        def sent(i, carry):
            to_mate(i).wait_send()
            for copy in to_ranks(i):
                copy.wait_send()
            return carry

        lax.fori_loop(0, chip, sent, 0)

        @pl.when(chip < chips - 1)
        def _():
            def sent_right(i, carry):
                to_right(i).wait_send()
                return carry

            lax.fori_loop(0, chip + 1, sent_right, 0)

    vmem = pl.BlockSpec(memory_space=pltpu.VMEM)
    sems = pltpu.SemaphoreType.DMA((chips,))
    rank_sems = pltpu.SemaphoreType.DMA((chips, ranks))
    return pl.pallas_call(
        kernel,
        name="attention_forward",
        in_specs=[vmem] * 10,
        out_specs=[vmem] * 7,
        out_shape=[
            jax.ShapeDtypeStruct((count, heads * VD), BF),
            jax.ShapeDtypeStruct((heads, 1, count), F32),
            jax.ShapeDtypeStruct((2 * chips, count, LAT), BF),
            jax.ShapeDtypeStruct((count, model), BF),
            jax.ShapeDtypeStruct((count, KVL), F32),
            jax.ShapeDtypeStruct((count, heads * 256), BF),
            jax.ShapeDtypeStruct((count, 128), F32),
        ],
        scratch_shapes=[
            pltpu.VMEM((count, LAT), BF),
            pltpu.VMEM((count, 128), F32),
            pltpu.VMEM((heads, count, 256), BF),
            pltpu.VMEM((heads, 1, count), F32),
            pltpu.VMEM((heads, 1, count), F32),
            pltpu.VMEM((heads, VD, count), F32),
            sems,
            sems,
            sems,
            sems,
            rank_sems,
            rank_sems,
        ],
        cost_estimate=SHORT,
        compiler_params=pltpu.CompilerParams(
            vmem_limit_bytes=VMEM_LIMIT, collective_id=collective, has_side_effects=True
        ),
    )(tokens, gain, query_weight, latent_rows, latent_gain, latent_up, even, odd, key_ids, query_ids)


def attention_backward(queries, latents, latent_up, key_ids, query_ids, attended, output_grad, output_weight, lse, even, odd, rows, query_weight, beside, collective):
    count, model = rows.shape
    heads = queries.shape[1] // 256
    blocks = latents.shape[0]
    factor = (ND + RD) ** (-0.5)
    scale = factor * LOG2E

    def kernel(q_ref, lat_ref, up_ref, kid_ref, qid_ref, att_ref, og_ref, ow_ref, lse_ref, even_ref, odd_ref, in_ref, qw_ref,
               sent_ref, dqw_ref, dow_ref, din_ref, dup_ref, dlat_ref, got_ref, dq_ref, do_ref, delta, keys, dq, dup, dlat,
               send, receive):
        link_refs = [sent_ref, got_ref, send, receive]
        greet(beside.friends())
        beside.begin(link_refs)
        place = lax.axis_index("dpo") * 2 + lax.axis_index("core")
        dq[...] = jnp.zeros_like(dq)
        dup[...] = jnp.zeros_like(dup)
        do_ref[...] = nt(og_ref[...], ow_ref[...]).astype(BF)
        for h in range(heads):
            part = slice(h * VD, (h + 1) * VD)
            products = do_ref[:, part].astype(F32) * att_ref[:, part].astype(F32)
            delta[h] = jnp.sum(products.T, axis=0, keepdims=True)

        def chunk(at, masked):
            lat = lat_ref[at, :, :KVL]
            turned = lat.T
            rope = lat_ref[at, :, KVL:]
            dlat[...] = jnp.zeros_like(dlat)
            for h in range(heads):
                up = up_ref[:, h * 256 : (h + 1) * 256]
                query = q_ref[:, h * 256 : (h + 1) * 256]
                upstream = do_ref[:, h * VD : (h + 1) * VD]
                keys[h, :, ND:] = rope
                both = nn(lat, up).astype(BF)
                keys[h, :, :ND] = both[:, :ND]
                scores = nt(keys[h], query) * scale
                chances = jnp.exp2(scores - lse_ref[h])
                if masked:
                    chances = jnp.where(kid_ref[...] <= qid_ref[...], chances, 0.0)
                chance_grad = nt(both[:, ND:], upstream)
                score_grad = (chances * (chance_grad - delta[h])).astype(BF)
                value_grad = nn(chances.astype(BF), upstream)
                key_grad = nn(score_grad, query) * factor
                dq[h] += nn(keys[h].T, score_grad)
                both_grad = jnp.concatenate([key_grad[:, :ND], value_grad], axis=1).astype(BF)
                dlat[:, :KVL] += nt(both_grad, up)
                dlat[:, KVL:] += key_grad[:, ND:]
                dup[:, h * 256 : (h + 1) * 256] += nn(turned, both_grad)
            dlat_ref[at] = dlat[...].astype(BF)

        lax.fori_loop(0, place, lambda at, carry: (chunk(at, False), carry)[1], 0)
        chunk(place, True)

        def clear(at, carry):
            dlat_ref[at] = jnp.zeros((count, LAT), BF)
            return carry

        lax.fori_loop(place + 1, blocks, clear, 0)
        dup_ref[...] = dup[...].astype(BF)
        lane = lax.broadcasted_iota(jnp.int32, (count, 128), 1)
        for h in range(0, heads, 2):
            plain, ropes = [], []
            for i in range(2):
                back = dq[h + i].T * factor
                plain.append(back[:, :ND])
                ropes.append(turn_pairs(back[:, ND:], even_ref[...], -odd_ref[...]))
            moved = pltpu.roll(plain[1], 64, 1)
            at = h * (ND + RD)
            dq_ref[:, at : at + 128] = plain[0].astype(BF)
            dq_ref[:, at + 128 : at + 256] = jnp.where(lane < 64, ropes[0], moved).astype(BF)
            dq_ref[:, at + 256 : at + 384] = jnp.where(
                lane < 64, moved, pltpu.roll(ropes[1], 64, 1)
            ).astype(BF)
        turned_mix = att_ref[...].T
        for at in range(0, model, 512):
            part = slice(at, at + 512)
            dqw_ref[part] = nn(in_ref[:, part].T, dq_ref[...]).astype(BF)
            dow_ref[:, part] = nn(turned_mix, og_ref[:, part]).astype(BF)
            din_ref[:, part] = nt(dq_ref[...], qw_ref[part]).astype(BF)
        beside.end(link_refs)

    vmem = pl.BlockSpec(memory_space=pltpu.VMEM)
    return pl.pallas_call(
        kernel,
        name="attention_backward",
        in_specs=[vmem] * 13 + beside.in_specs,
        out_specs=[vmem] * 5 + beside.out_specs,
        out_shape=[
            jax.ShapeDtypeStruct(query_weight.shape, BF),
            jax.ShapeDtypeStruct(output_weight.shape, BF),
            jax.ShapeDtypeStruct((count, model), BF),
            jax.ShapeDtypeStruct((KVL, heads * 256), BF),
            jax.ShapeDtypeStruct((blocks, count, LAT), BF),
        ]
        + beside.outs,
        scratch_shapes=[
            pltpu.VMEM((count, heads * (ND + RD)), BF),
            pltpu.VMEM((count, heads * VD), BF),
            pltpu.VMEM((heads, 1, count), F32),
            pltpu.VMEM((heads, count, 256), BF),
            pltpu.VMEM((heads, 256, count), F32),
            pltpu.VMEM((KVL, heads * 256), F32),
            pltpu.VMEM((count, LAT), F32),
        ]
        + beside.scratch,
        cost_estimate=SHORT,
        compiler_params=pltpu.CompilerParams(
            vmem_limit_bytes=VMEM_LIMIT, collective_id=collective, has_side_effects=True
        ),
    )(queries, latents, latent_up, key_ids, query_ids, attended, output_grad, output_weight, lse, even, odd, rows, query_weight,
      *beside.ins)


def latents_back(compressed_grad, raw, latent_gain, even, odd, latent_rows, query_part, tokens, first_factor, rows):
    count, model = tokens.shape
    wide = 512
    lanes = KVL + RD

    def kernel(cg_ref, raw_ref, gain_ref, even_ref, odd_ref, ld_ref, qp_ref, x_ref, ff_ref, in_ref,
               out_ref, dld_ref, lgain_ref, fgain_ref, down):
        @pl.when(pl.program_id(0) == 0)
        def _():
            raw = raw_ref[...]
            factor = lax.rsqrt(jnp.mean(raw * raw, axis=-1, keepdims=True) + EPSILON)
            back, gain_grad = norm_back(raw, factor, gain_ref[...], cg_ref[:, :KVL])
            lgain_ref[...] = gain_grad[None]
            down[:, :KVL] = back.astype(BF)
            down[:, KVL:] = turn_pairs(cg_ref[:, KVL:], even_ref[...], -odd_ref[...])[:, :RD].astype(BF)

        grad = qp_ref[...].astype(F32) + nn(down[...], ld_ref[...])
        out_ref[...] = grad.astype(BF)
        fgain_ref[...] = jnp.sum(grad * x_ref[...].astype(F32) * ff_ref[:, :1], axis=0, keepdims=True)
        dld_ref[...] = nn(in_ref[...].T, down[...]).astype(BF)

    def whole(shape):
        return pl.BlockSpec(shape, lambda p: (0,) * len(shape), pipeline_mode=pl.Buffered(1))

    def columns(size):
        return pl.BlockSpec((size, wide), lambda p: (0, p))

    return pl.pallas_call(
        kernel,
        name="latents_back",
        grid=(model // wide,),
        in_specs=[whole(a.shape) for a in (compressed_grad, raw, latent_gain, even, odd)]
        + [columns(lanes), columns(count), columns(count), whole(first_factor.shape), columns(count)],
        out_specs=[
            columns(count),
            pl.BlockSpec((wide, lanes), lambda p: (p, 0)),
            whole((1, KVL)),
            columns(1),
        ],
        out_shape=[
            jax.ShapeDtypeStruct((count, model), BF),
            jax.ShapeDtypeStruct((model, lanes), BF),
            jax.ShapeDtypeStruct((1, KVL), F32),
            jax.ShapeDtypeStruct((1, model), F32),
        ],
        scratch_shapes=[pltpu.VMEM((count, lanes), BF)],
        cost_estimate=SHORT,
        compiler_params=pltpu.CompilerParams(
            vmem_limit_bytes=VMEM_LIMIT, dimension_semantics=("arbitrary",)
        ),
    )(compressed_grad, raw, latent_gain, even, odd, latent_rows, query_part, tokens, first_factor, rows)


def grouped(gates, steps):
    parts = EXPERTS // (steps - 1)
    gates = gates.reshape((steps - 1, parts) + gates.shape[1:])
    return jnp.concatenate([gates, jnp.ones((1,) + gates.shape[1:], F32)], axis=0)


def shards(
    tokens,
    cotangent,
    block_ids,
    routes,
    first_gain,
    query_weight,
    latent_down,
    latent_gain,
    latent_up,
    output_weight,
    second_gain,
    router_weight,
    gate_weight,
    up_weight,
    down_weight,
    shared_gate,
    shared_up,
    shared_down,
):
    count, model = tokens.shape
    key_count = block_ids.shape[0]
    heads = query_weight.shape[1] // (ND + RD)
    unit = gate_weight.shape[2]
    width = shared_down.shape[0]
    steps = EXPERTS * unit // width + 1
    chips = lax.axis_size("dpo")
    ranks = lax.axis_size("tensor")
    devices = chips * 2 * ranks
    chip, core, rank = lax.axis_index("dpo"), lax.axis_index("core"), lax.axis_index("tensor")
    place = chip * 2 + core
    quarter = count // ranks
    half = model // (2 * chips)
    routed_rows = EXPERTS * unit

    def mine(array):
        return lax.dynamic_slice_in_dim(array, rank * quarter, quarter, 0)

    weights = (
        jnp.swapaxes(gate_weight, 1, 2).reshape(routed_rows, model),
        jnp.swapaxes(up_weight, 1, 2).reshape(routed_rows, model),
        down_weight.reshape(routed_rows, model),
        shared_gate.T,
        shared_up.T,
        shared_down,
    )

    row_start = place * count
    cosine, sine_table = rotary_tables((row_start + jnp.arange(count, dtype=jnp.int32)) % key_count)
    own_blocks = lax.dynamic_slice_in_dim(block_ids, row_start, count, 0)
    rest = jnp.zeros((count, 128 - RD), F32)
    even = jnp.concatenate([cosine, cosine, rest], axis=1)
    odd = jnp.concatenate([-sine_table, sine_table, rest], axis=1)
    key_ids, query_ids = own_blocks[:, None], own_blocks[None, :]
    all_upstream = lax.all_gather(cotangent, "dpo", axis=0, tiled=True)
    attended, lse, latents, attention_input, latent_raw, queries, first_factor = attention_forward(
        tokens, first_gain[None], query_weight, latent_down.T, latent_gain[None], latent_up,
        even, odd, key_ids, query_ids, 1,
    )

    named = jnp.any(
        routes[:, :, None] == jnp.arange(128, dtype=jnp.int32)[None, None, :], axis=1
    )
    named = (named | (jnp.arange(128) >= EXPERTS)[None, :]).astype(F32)
    token_quarter = mine(tokens)
    parts = EXPERTS // (steps - 1)

    def second_norm(total, more):
        rows, gain, router_columns, mask = more
        residual = rows.astype(F32) + total
        normed, _ = norm_rows(residual, gain)
        normed = normed.astype(BF)
        logits = nn(normed, router_columns)
        lane = lax.broadcasted_iota(jnp.int32, logits.shape, 1)
        first = lane < EXPERTS
        logits = jnp.where(first | ((lane >= 16) & (lane < 16 + EXPERTS)), logits, -1e30)
        odds = jnp.exp(logits - jnp.max(logits, axis=1, keepdims=True))
        odds = odds / jnp.sum(jnp.where(first, odds, 0.0), axis=1, keepdims=True)
        gates = jnp.where((lane >= EXPERTS) & (lane < EXPERTS + parts), 1.0, mask * odds)
        return residual, jnp.concatenate([normed, gates.astype(BF)], axis=1)

    twice = jnp.pad(router_weight, ((0, 0), (0, 16 - EXPERTS)))
    own_fill = DownProducts(cotangent[None], 1, lambda i: i, weights[2], weights[5])
    wide_input, residual, own_products = settle(
        [attended, output_weight],
        [
            tokens,
            second_gain[None],
            jnp.pad(jnp.concatenate([twice, twice], axis=1), ((0, 0), (0, 96))),
            named,
        ],
        second_norm,
        [jax.ShapeDtypeStruct((quarter, model), F32)],
        model + 128,
        own_fill,
        (0, own_fill.units - 2, own_fill.units),
        2,
    )
    all_input = lax.all_gather(wide_input, "dpo", axis=0, tiled=True)
    all_input = all_input.reshape(chips, count, model + 128)

    expert_part, input_back, kept_h, kept_g, kept_u, logit_grad = own_experts(
        wide_input, own_products, twice.T, weights
    )

    def second_norm_back(total, more):
        rows, gain, upstream_rows = more
        factor = lax.rsqrt(jnp.mean(rows * rows, axis=-1, keepdims=True) + EPSILON)
        back, gain_grad = norm_back(rows, factor, gain, total)
        back = back + upstream_rows.astype(F32)
        return back, gain_grad[None], back.astype(BF)

    input_back, all_upstream = lax.optimization_barrier((input_back, all_upstream))
    all_upstream = all_upstream.reshape(chips, count, model)
    far_fill = DownProducts(
        all_upstream, chips - 1, lambda i: lax.rem(lax.axis_index("dpo") + 1 + i, chips), weights[2], weights[5]
    )
    output_grad, residual_grad, grad_second_gain, far_products = settle(
        [input_back],
        [residual, second_gain[None], cotangent],
        second_norm_back,
        [
            jax.ShapeDtypeStruct((quarter, model), F32),
            jax.ShapeDtypeStruct((1, model), F32),
        ],
        model,
        far_fill,
        (0, far_fill.units * 2 // 7, far_fill.units * 4 // 7),
        3,
    )
    grad_second_gain = grad_second_gain[0]

    all_gates = grouped(
        jnp.transpose(all_input[:, :, model : model + EXPERTS].astype(F32), (2, 0, 1)), steps
    )
    all_gates = jnp.swapaxes(all_gates, 1, 2)

    routed_grads = []

    def piece(first, groups, beside, collective):
        made = group_gradients(
            all_input, all_upstream, far_products, all_gates,
            (kept_h, kept_g, kept_u), weights, first, groups, routed_grads, beside, collective,
        )
        if first == steps - 1:
            return made
        routed_grads[:] = made[:3]
        return made[3:]

    def summed(rows, got):
        return mine(rows).astype(F32) + jnp.sum(got.astype(F32), axis=0)

    grad_query, grad_output, query_part, grad_latent_up, latent_part, got_result = attention_backward(
        queries, latents, latent_up, key_ids, query_ids, attended, output_grad, output_weight, lse, even, odd,
        attention_input, query_weight, Scatter(expert_part), 4,
    )
    spread = [(grad_query, 0), (grad_latent_up, 0), (grad_output, 1)]
    compressed_grad, *flows, result = piece(
        0,
        steps - 2,
        Beside(
            LineSum(latent_part),
            Beside(
                LineFlow(spread, True, 2, 3),
                Beside(
                    LineFlow(spread, False, 6, 4),
                    Gather((residual + summed(expert_part, got_result)).astype(BF)),
                ),
            ),
        ),
        5,
    )
    grad_query, grad_latent_up, grad_output = (
        near + far.astype(F32) for near, far in zip(flows[3:], flows[:3])
    )
    attention_grad, grad_latent_down, grad_latent_gain, grad_first_gain = latents_back(
        compressed_grad, latent_raw, latent_gain[None], even, odd, latent_down.T, query_part, tokens,
        first_factor, attention_input,
    )
    grad_latent_down = lax.psum_scatter(grad_latent_down, DP, scatter_dimension=0, tiled=True)

    grad_router = lax.dot_general(
        wide_input[:, :model], logit_grad[:EXPERTS].astype(BF), (((0,), (1,)), ((), ())),
        preferred_element_type=F32,
    )

    def for_ranks(gain):
        return jnp.repeat(gain.reshape(2 * chips, -1), ranks, axis=0)

    small = jnp.concatenate(
        [
            grad_router.reshape(devices, -1),
            for_ranks(grad_second_gain),
            for_ranks(grad_first_gain),
            grad_latent_gain.reshape(devices, -1),
        ],
        axis=1,
    ).astype(BF)
    small = jnp.pad(small, ((0, 0), (0, 2048 - small.shape[1]))).reshape(devices * 16, 128)

    small_left, small_right, got = piece(
        steps - 2,
        1,
        Beside(
            Beside(LineFlow([(small, 0)], False, 1, 1), LineFlow([(small, 0)], True, 1, 1)),
            Scatter(attention_grad),
        ),
        6,
    )
    token_float = token_quarter.astype(F32)
    _, token_factor = norm_rows(token_float, first_gain)
    token_back, _ = norm_back(token_float, token_factor, first_gain, summed(attention_grad, got))
    small = (small_left + small_right.astype(F32)).astype(BF)
    *shared_grads, token_grad, got_down, got_small = piece(
        steps - 1,
        1,
        Many(
            [
                Gather((token_back + residual_grad).astype(BF)),
                Scatter(grad_latent_down),
                Scatter(small),
            ]
        ),
        7,
    )
    token_grad, result = token_grad.reshape(count, model), result.reshape(count, model)

    def over_ranks(rows, got):
        size = got.shape[1]
        own = lax.dynamic_slice_in_dim(rows, rank * size, size, 0)
        return own.astype(F32) + jnp.sum(got.astype(F32), axis=0)

    grad_latent_down = over_ranks(grad_latent_down, got_down)
    small = over_ranks(small, got_small).reshape(-1)
    router_size = model // devices * EXPERTS
    gain_size = model // (2 * chips)
    latent_size = KVL // devices
    grad_router = small[:router_size].reshape(-1, EXPERTS)
    small = small[router_size:]

    def routed_of(array):
        return array.reshape(EXPERTS, unit, half).astype(F32)

    return (
        result,
        token_grad,
        small[gain_size : 2 * gain_size],
        grad_query,
        grad_latent_down,
        small[2 * gain_size : 2 * gain_size + latent_size],
        grad_latent_up,
        grad_output,
        small[:gain_size],
        grad_router,
        jnp.swapaxes(routed_of(routed_grads[0]), 1, 2),
        jnp.swapaxes(routed_of(routed_grads[1]), 1, 2),
        routed_of(routed_grads[2]),
        shared_grads[0].astype(F32).T,
        shared_grads[1].astype(F32).T,
        shared_grads[2].astype(F32),
    )


def solution(mesh):
    groups, ranks = mesh.devices.shape
    fine = Mesh(mesh.devices.reshape(groups // 2, 2, ranks), ("dpo", "core", "tensor"))
    in_specs = (
        P(DP, None),
        P(DP, None),
        P(),
        P(DP, None),
        P(),
        P(None, "tensor"),
        P(),
        P(),
        P(None, "tensor"),
        P("tensor", None),
        P(),
        P(),
        P(None, None, "tensor"),
        P(None, None, "tensor"),
        P(None, "tensor", None),
        P(None, "tensor"),
        P(None, "tensor"),
        P("tensor", None),
    )
    out_specs = (
        P(DP, None),
        P(DP, None),
        P(DP),
        P(DP, "tensor"),
        P(ALL, None),
        P(ALL),
        P(DP, "tensor"),
        P("tensor", DP),
        P(DP),
        P(ALL, None),
        P(None, DP, "tensor"),
        P(None, DP, "tensor"),
        P(None, "tensor", DP),
        P(DP, "tensor"),
        P(DP, "tensor"),
        P("tensor", DP),
    )
    return jax.shard_map(shards, mesh=fine, in_specs=in_specs, out_specs=out_specs, check_vma=False)
```
